32 devices in a mesh: row: 4 (over y, x), col: 8 (over z, core).
Axes of the slice: x: 2, y: 2, z: 4, core: 2. Of those that a mesh axis runs over, the one named last changes fastest.
Arguments:
- pair_act: bfloat16 [512, 512, 128], P('row', 'col'), may hold values from -6 to 6
- out_grad: bfloat16 [512, 512, 128], P('row', 'col'), may hold values from -6 to 6
- tri_bias: bfloat16 [4, 512, 512], P(None, 'row', 'col'), may hold values from -6 to 250
- w_query: bfloat16 [128, 128], replicated, may hold values from -0.5 to 0.5
- w_key: bfloat16 [128, 128], replicated, may hold values from -0.5 to 0.5
- w_value: bfloat16 [128, 128], replicated, may hold values from -0.5 to 0.5
- w_gate: bfloat16 [128, 128], replicated, may hold values from -0.5 to 0.5
- w_out: bfloat16 [128, 128], replicated, may hold values from -0.5 to 0.5
- key_blocks: int32 [4, 3], replicated, may hold values from 0 to 3, as said below
- list_len: int32 [4], replicated, may hold values from 1 to 3, as said below
Outputs:
- d_pair: bfloat16 [512, 512, 128], P('row', 'col')
- d_bias: float32 [4, 512, 512], P(None, 'row', 'col')
- d_w_query: float32 [128, 128], replicated
- d_w_key: float32 [128, 128], replicated
- d_w_value: float32 [128, 128], replicated
- d_w_gate: float32 [128, 128], replicated
- d_w_out: float32 [128, 128], replicated
The draws below stay inside these ranges and needn't reach their ends.
Inputs may be any that keep to these rules, and one draw needn't show every extreme that they name: `key_blocks`: entry 0 of query block b's list is b itself; its first list_len[b] entries are distinct; entries past list_len[b] are block numbers that must be ignored. `list_len`: some query block lists 3 key blocks.
All inputs are finite; a program needn't handle non-finite values.
Results may differ from the reference program's by a relative error of at most 0.015.
Values may be sent and summed in bfloat16 or wider, within the bound.
No kernel may reach another device: no remote copies, remote signals or barrier semaphores. Data moves between devices by JAX's collectives and lax.ppermute only.
A program may use at most 192 MiB of HBM per device.

```python
import jax
import jax.numpy as jnp
from jax import lax

CHAN = 128
HEADS = 4
HEAD_DIM = 32
PROJ = 128
BLOCK = 128
QBLOCKS = 4
LISTED = 3
TOKENS = 512


def draw_tri_bias(key, part):
    base_key = jax.random.fold_in(jax.random.fold_in(key, 11), 0)
    full_shape = (HEADS, TOKENS, TOKENS)
    base = jnp.clip(jax.random.normal(base_key, full_shape, jnp.float32), -6.0, 6.0)
    return base.astype(jnp.bfloat16)


def list_tables(key):
    score_key, len_key, pick_key = jax.random.split(jax.random.fold_in(key, 29), 3)
    block_ids = jnp.arange(QBLOCKS, dtype=jnp.int32)
    ranking = jax.random.randint(score_key, (QBLOCKS, QBLOCKS), 0, 1048576) * QBLOCKS + block_ids[None, :]
    ranking = jnp.where(block_ids[:, None] == block_ids[None, :], -1, ranking)
    ordering = jnp.argsort(ranking, axis=1, stable=True)[:, :LISTED].astype(jnp.int32)
    lengths = jax.random.randint(len_key, (QBLOCKS,), 1, LISTED + 1)
    chosen_row = jax.random.randint(pick_key, (), 0, QBLOCKS)
    lengths = jnp.where(block_ids == chosen_row, LISTED, lengths).astype(jnp.int32)
    return (ordering, lengths)


def draw_key_blocks(key, part):
    return list_tables(key)[0]


def draw_list_len(key, part):
    return list_tables(key)[1]


def levels(rng, extent, cuts, low, high):
    def one(position, blocks):
        steps = jax.random.uniform(jax.random.fold_in(jax.random.fold_in(rng, 6), position), (blocks,), jnp.float32, low / len(cuts), high / len(cuts))
        return jnp.repeat(jnp.exp(steps), extent[position] // blocks).reshape((-1,) + (1,) * (len(extent) - position - 1))

    loudness = one(*cuts[0])
    for cut in cuts[1:]:
        loudness = loudness * one(*cut)
    return loudness


def noise(rng, shape, scale, most, cuts=(), kind=jnp.bfloat16):
    result = jax.random.normal(rng, shape, jnp.float32) * scale
    if len(cuts) > 0:
        result = levels(rng, shape, cuts, -0.22, 0.18) * result
    return jnp.clip(result, min=-most, max=most).astype(kind)


def setup_inputs(seed: int = 0) -> dict:
    key_list = jax.random.split(jax.random.key(seed), 11)
    return {
        "pair_act": noise(key_list[0], (TOKENS, TOKENS, CHAN), 1.0, 6.0, ((0, 4), (1, 8))),
        "out_grad": noise(key_list[1], (TOKENS, TOKENS, CHAN), 1.0, 6.0, ((0, 4), (1, 8))),
        "tri_bias": draw_tri_bias(jax.random.fold_in(key_list[10], 71), 0),
        "w_query": noise(key_list[3], (CHAN, PROJ), CHAN ** -0.5, 0.5),
        "w_key": noise(key_list[4], (CHAN, PROJ), CHAN ** -0.5, 0.5),
        "w_value": noise(key_list[5], (CHAN, PROJ), CHAN ** -0.5, 0.5),
        "w_gate": noise(key_list[6], (CHAN, PROJ), CHAN ** -0.5, 0.5),
        "w_out": noise(key_list[7], (PROJ, CHAN), PROJ ** -0.5, 0.5),
        "key_blocks": draw_key_blocks(jax.random.fold_in(key_list[10], 71), 0),
        "list_len": draw_list_len(jax.random.fold_in(key_list[10], 71), 0),
    }


def token_mask(key_blocks, list_len):
    block_count = key_blocks.shape[0]
    live_slots = jnp.arange(key_blocks.shape[1])[None, :] < list_len[:, None]
    block_hits = (key_blocks[:, :, None] == jnp.arange(block_count)[None, None, :]) & live_slots[:, :, None]
    block_allowed = jnp.any(block_hits, axis=1)
    return jnp.repeat(jnp.repeat(block_allowed, BLOCK, axis=0), BLOCK, axis=1)


def rounded(value):
    return lax.optimization_barrier(value.astype(jnp.bfloat16)).astype(jnp.float32)


def reference(pair_act, out_grad, tri_bias, w_query, w_key, w_value, w_gate, w_out, key_blocks, list_len):
    score_scale = HEAD_DIM ** -0.5
    allowed = token_mask(key_blocks, list_len)
    bias_t = jnp.transpose(tri_bias.astype(jnp.float32), (0, 2, 1))
    col_step = 4
    step_count = TOKENS // col_step
    col_acts = jnp.transpose(pair_act.reshape(TOKENS, step_count, col_step, CHAN), (1, 0, 2, 3))
    col_grads = jnp.transpose(out_grad.reshape(TOKENS, step_count, col_step, CHAN), (1, 0, 2, 3))
    head_shape = (TOKENS, col_step, HEADS, HEAD_DIM)

    def one_step(running, inputs):
        bias_acc, wq_acc, wk_acc, wv_acc, wg_acc, wo_acc = running
        act_block, grad_block = inputs
        flat_acts = act_block.reshape(-1, CHAN)
        flat_grads = grad_block.reshape(-1, CHAN)
        queries = (jnp.dot(flat_acts, w_query, preferred_element_type=jnp.float32) * score_scale).astype(jnp.bfloat16)
        key_proj = jnp.dot(flat_acts, w_key, preferred_element_type=jnp.float32).astype(jnp.bfloat16)
        values = jnp.dot(flat_acts, w_value, preferred_element_type=jnp.float32).astype(jnp.bfloat16)
        gate_act = jax.nn.sigmoid(jnp.dot(flat_acts, w_gate, preferred_element_type=jnp.float32))
        query_four = queries.reshape(head_shape).astype(jnp.float32)
        key_four = key_proj.reshape(head_shape).astype(jnp.float32)
        value_four = values.reshape(head_shape).astype(jnp.float32)
        scores = jnp.einsum('ichd,kchd->chik', query_four, key_four) + bias_t[None]
        scores = jnp.where(allowed[None, None], scores, -jnp.inf)
        row_peak = jnp.max(scores, axis=-1, keepdims=True)
        exp_scores = jnp.exp(scores - row_peak)
        att_probs = exp_scores / jnp.sum(exp_scores, axis=-1, keepdims=True)
        probs_low = rounded(att_probs)
        attended = jnp.einsum('chik,kchd->ichd', probs_low, value_four).reshape(-1, PROJ)
        gated = (gate_act * attended).astype(jnp.bfloat16)
        d_gated = lax.dot_general(flat_grads, w_out, (((1,), (1,)), ((), ())), preferred_element_type=jnp.float32)
        d_att = (d_gated * gate_act).astype(jnp.bfloat16)
        d_gpre = (d_gated * attended * gate_act * (1.0 - gate_act)).astype(jnp.bfloat16)
        att_four = d_att.reshape(head_shape).astype(jnp.float32)
        d_probs = jnp.einsum('ichd,kchd->chik', att_four, value_four)
        delta_sum = jnp.einsum('ichd,ichd->chi', att_four, attended.reshape(head_shape))[..., None]
        d_scores = att_probs * (d_probs - delta_sum)
        ds_low = rounded(d_scores)
        d_query = (jnp.einsum('chik,kchd->ichd', ds_low, key_four) * score_scale).reshape(-1, PROJ).astype(jnp.bfloat16)
        d_keys = jnp.einsum('chik,ichd->kchd', ds_low, query_four).reshape(-1, PROJ).astype(jnp.bfloat16)
        d_values = jnp.einsum('chik,ichd->kchd', probs_low, att_four).reshape(-1, PROJ).astype(jnp.bfloat16)
        d_flat = (jnp.dot(d_query, w_query.T, preferred_element_type=jnp.float32)
                  + jnp.dot(d_keys, w_key.T, preferred_element_type=jnp.float32)
                  + jnp.dot(d_values, w_value.T, preferred_element_type=jnp.float32)
                  + jnp.dot(d_gpre, w_gate.T, preferred_element_type=jnp.float32)).astype(jnp.bfloat16)
        acts_t = flat_acts.T
        running = (bias_acc + jnp.sum(d_scores, axis=0),
                   wq_acc + jnp.dot(acts_t, d_query, preferred_element_type=jnp.float32),
                   wk_acc + jnp.dot(acts_t, d_keys, preferred_element_type=jnp.float32),
                   wv_acc + jnp.dot(acts_t, d_values, preferred_element_type=jnp.float32),
                   wg_acc + jnp.dot(acts_t, d_gpre, preferred_element_type=jnp.float32),
                   wo_acc + jnp.dot(gated.T, flat_grads, preferred_element_type=jnp.float32))
        return running, d_flat.reshape(TOKENS, col_step, CHAN)

    start = (jnp.zeros((HEADS, TOKENS, TOKENS), jnp.float32),
             jnp.zeros((CHAN, PROJ), jnp.float32), jnp.zeros((CHAN, PROJ), jnp.float32),
             jnp.zeros((CHAN, PROJ), jnp.float32), jnp.zeros((CHAN, PROJ), jnp.float32),
             jnp.zeros((PROJ, CHAN), jnp.float32))
    final, pieces = lax.scan(one_step, start, (col_acts, col_grads))
    d_pair = jnp.transpose(pieces, (1, 0, 2, 3)).reshape(TOKENS, TOKENS, CHAN)
    d_bias = jnp.transpose(final[0], (0, 2, 1))
    return (d_pair, d_bias, final[1], final[2], final[3], final[4], final[5])
```

```python
import functools

import jax
import jax.numpy as jnp
from jax import lax
from jax.experimental import pallas as pl
from jax.experimental.pallas import tpu as pltpu
from jax.sharding import PartitionSpec as P

F32 = jnp.float32
BF16 = jnp.bfloat16
CHUNKS = 4
VMEM_LIMIT = 56 * 1024 * 1024


def dot(a, b):
    return jnp.dot(a, b, preferred_element_type=F32)


def transposed_bias_kernel(bias_ref, out_ref):
    for kb in range(bias_ref.shape[0]):
        for h in range(bias_ref.shape[2]):
            out_ref[kb, 0, h] = bias_ref[kb, 0, h].astype(F32).T


def transposed_bias(blocks):
    key_blocks, query_blocks, heads, queries, keys = blocks.shape
    return pl.pallas_call(
        transposed_bias_kernel,
        grid=(query_blocks,),
        in_specs=[pl.BlockSpec((key_blocks, 1, heads, queries, keys), lambda b: (0, b, 0, 0, 0))],
        out_specs=pl.BlockSpec((key_blocks, 1, heads, keys, queries), lambda b: (0, b, 0, 0, 0)),
        out_shape=jax.ShapeDtypeStruct((key_blocks, query_blocks, heads, keys, queries), F32),
        compiler_params=pltpu.CompilerParams(vmem_limit_bytes=VMEM_LIMIT),
    )(blocks)


def attention_kernel(
    dims, first, tables_ref, lens_ref, owners_ref, *refs
):
    pieces, heads, head_dim, blocks, size, slots = dims
    refs = list(refs)
    acts_in = [refs.pop(0) for _ in range(pieces)]
    bias_ref, w_all_ref, w_all_t_ref, w_out_t_ref = [refs.pop(0) for _ in range(4)]
    carried = [] if first else [refs.pop(0) for _ in range(3)]
    d_pair_out = [refs.pop(0) for _ in range(pieces)]
    d_bias_ref, d_w_ref, d_wo_ref = [refs.pop(0) for _ in range(3)]
    (act_s, grad_s, kv_s, kv_t_s, joint_s, d_att_s, query_s, d_att_t_s, gate_s, d_gated_s,
     d_kv_s, att_t_s, d_query_t_s, d_pair_s) = refs
    proj = heads * head_dim
    tokens = blocks * size
    scale = head_dim ** (-0.5)
    tile_rows = acts_in[0].shape[2]

    @pl.when(pl.program_id(0) == 0)
    def _():
        joint_s[...] = jnp.zeros_like(joint_s)
        if first:
            for ref in (d_bias_ref, d_w_ref, d_wo_ref):
                ref[...] = jnp.zeros_like(ref)
        else:
            for ref, before in zip((d_bias_ref, d_w_ref, d_wo_ref), carried):
                ref[...] = before[...]

    for s in range(pieces):
        rows = pl.ds(pl.multiple_of(owners_ref[s] * tile_rows, tile_rows), tile_rows)
        act_s[rows, :] = acts_in[s][0, 0]
        grad_s[rows, :] = acts_in[s][1, 0]
    acts = act_s[...]
    grads = grad_s[...]
    projected = dot(acts, w_all_ref[...])
    queries = (projected[:, :proj] * scale).astype(BF16)
    keys = projected[:, proj : 2 * proj].astype(BF16)
    values = projected[:, 2 * proj : 3 * proj].astype(BF16)
    gate = 1.0 / (1.0 + jnp.exp(-projected[:, 3 * proj :]))
    d_gated = dot(grads, w_out_t_ref[...])
    d_att = (d_gated * gate).astype(BF16)
    gate_s[...] = gate
    d_gated_s[...] = d_gated
    lane_head = lax.broadcasted_iota(jnp.int32, (size, proj), 1) // head_dim
    for b in range(blocks):
        part = slice(b * size, (b + 1) * size)
        kv_s[b, :, :proj] = keys[part]
        kv_s[b, :, proj:] = values[part]
        kv_t_s[b, :proj, :] = keys[part].T
        kv_t_s[b, proj:, :] = values[part].T
        query_t = queries[part].T
        d_att_t = d_att[part].T
        d_att_t_s[b] = d_att_t.astype(F32)
        for h in range(heads):
            own = slice(h * head_dim, (h + 1) * head_dim)
            low = slice(proj + h * head_dim, proj + (h + 1) * head_dim)
            joint_s[b, h, own, :size] = query_t[own]
            joint_s[b, h, low, size:] = d_att_t[own]
            here = lane_head == h
            zero = jnp.zeros((size, proj), BF16)
            query_s[b, h * size : (h + 1) * size, :] = jnp.where(here, queries[part], zero)
            d_att_s[b, h * size : (h + 1) * size, :] = jnp.where(here, d_att[part], zero)
    d_kv_s[...] = jnp.zeros_like(d_kv_s)

    def query_block(b, live):
        chosen = [tables_ref[b, e] for e in range(live)]
        kv = jnp.concatenate([kv_s[c] for c in chosen], axis=0)
        kv_t = jnp.concatenate([kv_t_s[c] for c in chosen], axis=1)
        probs_all, ds_all = [], []
        for h in range(heads):
            own = slice(h * head_dim, (h + 1) * head_dim)
            low = slice(proj + h * head_dim, proj + (h + 1) * head_dim)
            joint = dot(kv, joint_s[b, h])
            bias = jnp.concatenate([bias_ref[c, b, h] for c in chosen], axis=0)
            scores = joint[:, :size] + bias
            peak = jnp.max(scores, axis=0, keepdims=True)
            weights = jnp.exp(scores - peak)
            probs = weights * (1.0 / jnp.sum(weights, axis=0, keepdims=True))
            probs_low = probs.astype(BF16)
            att_t = dot(kv_t[low], probs_low)
            delta = jnp.sum(d_att_t_s[b, own, :] * att_t, axis=0, keepdims=True)
            d_scores = probs * (joint[:, size:] - delta)
            for e in range(live):
                d_bias_ref[b, e, h] += d_scores[e * size : (e + 1) * size]
            ds_low = d_scores.astype(BF16)
            att_t_s[b, own, :] = att_t
            d_query_t_s[b, own, :] = dot(kv_t[own], ds_low)
            probs_all.append(probs_low)
            ds_all.append(ds_low)
        d_values = dot(jnp.concatenate(probs_all, axis=1), d_att_s[b])
        d_keys = dot(jnp.concatenate(ds_all, axis=1), query_s[b])
        for e in range(live):
            part = slice(e * size, (e + 1) * size)
            d_kv_s[chosen[e], :, :proj] += d_keys[part]
            d_kv_s[chosen[e], :, proj:] += d_values[part]

    @pl.loop(0, blocks)
    def _(b):
        for live in range(1, slots + 1):

            @pl.when(lens_ref[b] == live)
            def _():
                query_block(b, live)

    d_query, attended = [], []
    for b in range(blocks):
        d_query.append((d_query_t_s[b] * scale).T.astype(BF16))
        attended.append(att_t_s[b].T)
    d_query = jnp.concatenate(d_query, axis=0)
    attended = jnp.concatenate(attended, axis=0)
    gate = gate_s[...]
    gated = (gate * attended).astype(BF16)
    d_gpre = (d_gated_s[...] * attended * gate * (1.0 - gate)).astype(BF16)
    d_kv = d_kv_s[...].reshape(tokens, 2 * proj).astype(BF16)
    d_all = jnp.concatenate([d_query, d_kv, d_gpre], axis=1)
    d_pair_s[...] = dot(d_all, w_all_t_ref[...])
    for s in range(pieces):
        rows = pl.ds(pl.multiple_of(owners_ref[s] * tile_rows, tile_rows), tile_rows)
        d_pair_out[s][0] = d_pair_s[rows, :].astype(BF16)
    d_w_ref[...] += dot(act_s[...].T, d_all)
    d_wo_ref[...] += dot(gated.T, grad_s[...])


def attention(pieces, bias_t, w_all, w_out, key_blocks, list_len, owners, carried):
    count = len(pieces)
    _, columns, tile_rows, chan = pieces[0].shape
    blocks, slots = key_blocks.shape
    heads = bias_t.shape[2]
    proj = w_out.shape[0]
    size = tile_rows * count // blocks
    tokens = blocks * size
    dims = (count, heads, proj // heads, blocks, size, slots)
    first = carried is None
    whole = lambda shape: pl.BlockSpec(shape, lambda j, *_: (0,) * len(shape))
    sums = [
        jax.ShapeDtypeStruct((blocks, slots, heads, size, size), F32),
        jax.ShapeDtypeStruct((chan, 4 * proj), F32),
        jax.ShapeDtypeStruct((proj, chan), F32),
    ]
    fixed = [bias_t, w_all, w_all.T, w_out.T] + ([] if first else list(carried))
    pairs = count * tokens // count * size * slots * heads
    outs = pl.pallas_call(
        functools.partial(attention_kernel, dims, first),
        grid_spec=pltpu.PrefetchScalarGridSpec(
            num_scalar_prefetch=3,
            grid=(columns,),
            in_specs=[pl.BlockSpec((2, 1, tile_rows, chan), lambda j, *_: (0, j, 0, 0))] * count
            + [whole(x.shape) for x in fixed],
            out_specs=[pl.BlockSpec((1, tile_rows, chan), lambda j, *_: (j, 0, 0))] * count
            + [whole(x.shape) for x in sums],
            scratch_shapes=[
                pltpu.VMEM((tokens, chan), BF16),
                pltpu.VMEM((tokens, chan), BF16),
                pltpu.VMEM((blocks, size, 2 * proj), BF16),
                pltpu.VMEM((blocks, 2 * proj, size), BF16),
                pltpu.VMEM((blocks, heads, 2 * proj, 2 * size), BF16),
                pltpu.VMEM((blocks, heads * size, proj), BF16),
                pltpu.VMEM((blocks, heads * size, proj), BF16),
                pltpu.VMEM((blocks, proj, size), F32),
                pltpu.VMEM((tokens, proj), F32),
                pltpu.VMEM((tokens, proj), F32),
                pltpu.VMEM((blocks, size, 2 * proj), F32),
                pltpu.VMEM((blocks, proj, size), F32),
                pltpu.VMEM((blocks, proj, size), F32),
                pltpu.VMEM((tokens, chan), F32),
            ],
        ),
        out_shape=[jax.ShapeDtypeStruct((columns, tile_rows, chan), BF16)] * count + sums,
        compiler_params=pltpu.CompilerParams(vmem_limit_bytes=VMEM_LIMIT),
        cost_estimate=pl.CostEstimate(
            flops=columns * pairs * proj // heads * 12,
            bytes_accessed=columns * tokens * chan * 6 + 10 * 2**20,
            transcendentals=columns * pairs,
        ),
    )(key_blocks, list_len, owners, *pieces, *fixed)
    return outs[:count], outs[count:]


def partner_lists(count):
    paired = count & (count - 1) == 0
    if paired:
        return paired, [[(r, r ^ s) for r in range(count)] for s in range(count)]
    return paired, [[(r, (r + s) % count) for r in range(count)] for s in range(count)]


def on_device(
    pair_act, out_grad, tri_bias, w_query, w_key, w_value, w_gate, w_out, key_blocks, list_len
):
    row_count = lax.axis_size("row")
    col_count = lax.axis_size("col")
    tile_rows, tile_cols, chan = pair_act.shape
    heads = tri_bias.shape[0]
    query_tile = tri_bias.shape[2]
    proj = w_query.shape[1]
    blocks, slots = key_blocks.shape
    tokens = tile_rows * row_count
    size = tokens // blocks
    col_width = tile_cols // row_count
    chunks = CHUNKS if col_width % CHUNKS == 0 else 1
    width = col_width // chunks
    me = lax.axis_index("row")
    paired, partners = partner_lists(row_count)

    bias_all = lax.all_gather(jnp.transpose(tri_bias, (0, 2, 1)), ("row", "col"))
    bias_all = bias_all.reshape(row_count, col_count, heads, query_tile, tile_rows)
    bias_all = jnp.transpose(bias_all, (2, 1, 3, 0, 4)).reshape(heads, blocks, size, blocks, size)
    bias_t = transposed_bias(jnp.transpose(bias_all, (3, 1, 0, 2, 4)))

    both = jnp.stack([pair_act, out_grad]).reshape(
        2, tile_rows, row_count, chunks, width, chan
    )
    both = jnp.transpose(both, (2, 3, 0, 4, 1, 5))
    targets = [me ^ s if paired else (me + s) % row_count for s in range(row_count)]
    sources = [me ^ s if paired else (me - s) % row_count for s in range(row_count)]
    owners = jnp.stack(sources).astype(jnp.int32)
    w_all = jnp.concatenate([w_query, w_key, w_value, w_gate], axis=1)

    arrived = []
    for c in range(chunks):
        pieces = []
        for s in range(row_count):
            piece = lax.dynamic_index_in_dim(both, targets[s], 0, keepdims=False)[c]
            pieces.append(piece if s == 0 else lax.ppermute(piece, "row", partners[s]))
        arrived.append(pieces)
    carried = None
    returned = []
    for c in range(chunks):
        d_pieces, carried = attention(
            arrived[c], bias_t, w_all, w_out, key_blocks, list_len, owners, carried
        )
        back = []
        for s in range(row_count):
            home = [(t, f) for f, t in partners[s]]
            back.append(d_pieces[s] if s == 0 else lax.ppermute(d_pieces[s], "row", home))
        returned.append(jnp.stack(back))
    slot_bias, w_grad, o_grad = carried

    d_pair = jnp.stack(returned, axis=1)
    steps = jnp.arange(row_count)
    order = me ^ steps if paired else (steps - me) % row_count
    d_pair = jnp.take(d_pair, order, axis=0)
    d_pair = jnp.transpose(d_pair, (3, 0, 1, 2, 4)).reshape(tile_rows, tile_cols, chan)

    match = (key_blocks[:, :, None] == jnp.arange(blocks)[None, None, :]) & (
        jnp.arange(slots)[None, :, None] < list_len[:, None, None]
    )
    slot_form = jnp.transpose(slot_bias, (1, 2, 3, 0, 4)).reshape(slots, heads, size, tokens)
    slot_cols = lax.psum_scatter(
        slot_form.astype(BF16), "col", scatter_dimension=3, tiled=True
    ).astype(F32)
    query_ids = lax.axis_index("col") * query_tile + jnp.arange(query_tile, dtype=jnp.int32)
    hit = match[query_ids // size]
    expanded = jnp.sum(
        jnp.where(jnp.transpose(hit, (2, 1, 0))[:, :, None, None, :], slot_cols[None], 0.0), axis=1
    )
    expanded = jnp.transpose(expanded, (1, 0, 2, 3)).reshape(heads, tokens, query_tile)
    d_bias = lax.psum_scatter(
        expanded.astype(BF16), "row", scatter_dimension=1, tiled=True
    ).astype(F32)
    w_sum, o_sum = lax.psum((w_grad, o_grad), ("row", "col"))
    return (
        d_pair,
        d_bias,
        w_sum[:, :proj],
        w_sum[:, proj : 2 * proj],
        w_sum[:, 2 * proj : 3 * proj],
        w_sum[:, 3 * proj :],
        o_sum,
    )


def solution(mesh):
    in_specs = (
        P("row", "col", None),
        P("row", "col", None),
        P(None, "row", "col"),
        P(),
        P(),
        P(),
        P(),
        P(),
        P(),
        P(),
    )
    out_specs = (P("row", "col", None), P(None, "row", "col"), P(), P(), P(), P(), P())
    return jax.shard_map(
        on_device, mesh=mesh, in_specs=in_specs, out_specs=out_specs, check_vma=False
    )
```

```python
import functools
import math

import jax
import jax.numpy as jnp
from jax import lax
from jax.experimental import pallas as pl
from jax.experimental.pallas import tpu as pltpu
from jax.sharding import PartitionSpec as P

F32 = jnp.float32
BF16 = jnp.bfloat16
CHUNKS = 2
TOGETHER = 2
STRIP = 32
LOG2E = math.log2(math.e)
SAFE_SCORE = 30.0
VMEM_LIMIT = 56 * 1024 * 1024


def dot(a, b):
    return jnp.dot(a, b, preferred_element_type=F32)


def bias_kernel(tables_ref, lens_ref, col_pos_ref, row_pos_ref, *refs):
    *parts, out_ref = refs
    b = pl.program_id(0)
    blocks, _, heads, size, _ = out_ref.shape
    slots = tables_ref.shape[1]
    rows, _, _, tile = parts[0].shape[1:]
    per_block = size // tile
    for h in range(heads):
        for r in range(rows):
            piece = jnp.concatenate([p[0, row_pos_ref[r], h] for p in parts], axis=0)
            at = (r % per_block) * tile
            out_ref[r // per_block, 0, h, at : at + tile, :] = piece.astype(F32).T
    for h in range(heads):
        peak = jnp.max(out_ref[tables_ref[b, 0], 0, h], axis=0, keepdims=True)
        for e in range(1, slots):
            other = jnp.max(out_ref[tables_ref[b, e], 0, h], axis=0, keepdims=True)
            peak = jnp.where(e < lens_ref[b], jnp.maximum(peak, other), peak)
        for kb in range(blocks):
            out_ref[kb, 0, h] = (out_ref[kb, 0, h] - peak) * LOG2E


def shifted_bias(gathered, key_blocks, list_len, col_pos, row_pos):
    cols, rows, heads, query_tile, key_tile = gathered.shape
    blocks = key_blocks.shape[0]
    size = cols * query_tile // blocks
    per_block = size // query_tile

    def part(sub):
        return pl.BlockSpec(
            (1, rows, heads, query_tile, key_tile),
            lambda b, tables, lens, col_at, row_at: (col_at[b * per_block + sub], 0, 0, 0, 0),
        )

    return pl.pallas_call(
        bias_kernel,
        grid_spec=pltpu.PrefetchScalarGridSpec(
            num_scalar_prefetch=4,
            grid=(blocks,),
            in_specs=[part(sub) for sub in range(per_block)],
            out_specs=pl.BlockSpec((blocks, 1, heads, size, size), lambda b, *_: (0, b, 0, 0, 0)),
        ),
        out_shape=jax.ShapeDtypeStruct((blocks, blocks, heads, size, size), F32),
        compiler_params=pltpu.CompilerParams(vmem_limit_bytes=VMEM_LIMIT),
    )(key_blocks, list_len, col_pos, row_pos, *([gathered] * per_block))


def attention_kernel(dims, first, last, tables_ref, lens_ref, owners_ref, *refs):
    pieces, heads, head_dim, blocks, size, slots, together = dims
    refs = list(refs)
    take = lambda n: [refs.pop(0) for _ in range(n)]
    inputs = take(pieces)
    bias_ref, w_all_ref, w_all_t_ref, w_out_ref = take(4)
    carried = [] if first else take(4)
    d_pair_out = take(pieces)
    if last:
        d_bias_out, d_w_out = take(2)
    else:
        sums_out = take(4)
    d_bias_s, dw_qg_s, dw_kv_s, dwo_s = sums = take(4) if last else sums_out
    (act_s, grad_s, act_t_s, kv_s, kv_t_s, joint_s, d_att_s, query_s, gate_t_s, d_gated_t_s,
     score_s, probs_s, ds_s, d_kv_s, att_t_s, d_query_t_s, d_pair_s) = refs
    proj = heads * head_dim
    scale = head_dim ** (-0.5)
    tile_rows = inputs[0].shape[2]
    span = [slice(b * size, (b + 1) * size) for b in range(blocks)]
    own = [slice(h * head_dim, (h + 1) * head_dim) for h in range(heads)]
    low = [slice(proj + h * head_dim, proj + (h + 1) * head_dim) for h in range(heads)]

    @pl.when(pl.program_id(0) == 0)
    def _():
        joint_s[...] = jnp.zeros_like(joint_s)
        for n, ref in enumerate(sums):
            ref[...] = jnp.zeros_like(ref) if first else carried[n][...]

    lane_head = lax.broadcasted_iota(jnp.int32, (size, proj), 1) // head_dim
    bound = jnp.float32(0.0)
    for c in range(together):
        for s in range(pieces):
            rows = pl.ds(pl.multiple_of(owners_ref[s] * tile_rows, tile_rows), tile_rows)
            act_s[c, rows, :] = inputs[s][0, c]
            grad_s[c, rows, :] = inputs[s][1, c]
        acts = act_s[c]
        acts_t = acts.T
        act_t_s[c] = acts_t
        natural = dot(acts, w_all_ref[:, : 3 * proj])
        across = dot(w_all_t_ref[...], acts_t)
        queries_t = (across[:proj] * scale).astype(BF16)
        kv_t = across[proj : 3 * proj].astype(BF16)
        gate_t = 1.0 / (1.0 + jnp.exp(-across[3 * proj :]))
        d_gated_t = dot(w_out_ref[...], grad_s[c].T)
        d_att_t = (d_gated_t * gate_t).astype(BF16)
        gate_t_s[c] = gate_t
        d_gated_t_s[c] = d_gated_t
        squares = lambda x: jnp.max(
            jnp.sum(jnp.square(x.astype(F32)).reshape(heads, head_dim, -1), axis=1)
        )
        bound = jnp.maximum(bound, squares(queries_t) * squares(kv_t[:proj]))
        queries = (natural[:, :proj] * scale).astype(BF16)
        kv = natural[:, proj:].astype(BF16)
        zero = jnp.zeros((size, proj), BF16)
        for b in range(blocks):
            kv_s[c, b] = kv[span[b]]
            kv_t_s[c, b] = kv_t[:, span[b]]
            d_att = d_att_t[:, span[b]].T
            for h in range(heads):
                joint_s[c, b, h, own[h], :size] = queries_t[own[h], span[b]]
                joint_s[c, b, h, low[h], size:] = d_att_t[own[h], span[b]]
                here = lane_head == h
                query_s[c, b, h * size : (h + 1) * size, :] = jnp.where(here, queries[span[b]], zero)
                d_att_s[c, b, h * size : (h + 1) * size, :] = jnp.where(here, d_att, zero)
    d_kv_s[...] = jnp.zeros_like(d_kv_s)

    def query_block(b, live, shift):
        chosen = [tables_ref[b, e] for e in range(live)]
        strips = [
            (e, e * size + at, at) for e in range(live) for at in range(0, size, STRIP)
        ]
        rows_of = lambda x: jnp.sum(x.reshape(-1, 8, size), axis=0)
        for c in range(together):
            kv = jnp.concatenate([kv_s[c, k] for k in chosen], axis=0)
            for h in range(heads):
                score_s[c, h, : live * size, :] = dot(kv, joint_s[c, b, h])
        for h in range(heads):
            stats = []
            for c in range(together):
                def scores(e, row, at):
                    return (
                        score_s[c, h, row : row + STRIP, :size] * LOG2E
                        + bias_ref[chosen[e], b, h, at : at + STRIP, :]
                    )

                if shift:
                    peak = jnp.full((8, size), -jnp.inf, F32)
                    for strip in strips:
                        peak = jnp.maximum(
                            peak, jnp.max(scores(*strip).reshape(-1, 8, size), axis=0)
                        )
                    peak = jnp.max(peak, axis=0, keepdims=True)
                total = jnp.zeros((8, size), F32)
                mixed = jnp.zeros((8, size), F32)
                for e, row, at in strips:
                    value = scores(e, row, at)
                    weight = jnp.exp2(value - peak if shift else value)
                    total += rows_of(weight)
                    mixed += rows_of(weight * score_s[c, h, row : row + STRIP, size:])
                    score_s[c, h, row : row + STRIP, :size] = weight
                norm = 1.0 / jnp.sum(total, axis=0, keepdims=True)
                stats.append((norm, jnp.sum(mixed, axis=0, keepdims=True) * norm))
            lanes = slice(h * size, (h + 1) * size)
            for e, row, at in strips:
                part = slice(row, row + STRIP)
                gathered = d_bias_s[b, e, h, at : at + STRIP, :]
                for c, (norm, delta) in enumerate(stats):
                    probs = score_s[c, h, part, :size] * norm
                    d_scores = probs * (score_s[c, h, part, size:] - delta)
                    probs_s[c, part, lanes] = probs.astype(BF16)
                    ds_s[c, part, lanes] = d_scores.astype(BF16)
                    gathered += d_scores
                d_bias_s[b, e, h, at : at + STRIP, :] = gathered
        for c in range(together):
            probs = probs_s[c, : live * size, :]
            ds = ds_s[c, : live * size, :]
            kv_t = jnp.concatenate([kv_t_s[c, k] for k in chosen], axis=1)
            for h in range(heads):
                lanes = slice(h * size, (h + 1) * size)
                att_t_s[c, b, own[h], :] = dot(kv_t[low[h]], probs[:, lanes])
                d_query_t_s[c, b, own[h], :] = dot(kv_t[own[h]], ds[:, lanes])
            d_values = dot(probs, d_att_s[c, b])
            d_keys = dot(ds, query_s[c, b])
            for e in range(live):
                part = slice(e * size, (e + 1) * size)
                d_kv_s[c, chosen[e], :, :proj] += d_keys[part]
                d_kv_s[c, chosen[e], :, proj:] += d_values[part]

    def all_blocks(shift):
        @pl.loop(0, blocks)
        def _(b):
            for live in range(1, slots + 1):

                @pl.when(lens_ref[b] == live)
                def _():
                    query_block(b, live, shift)

    small = bound <= SAFE_SCORE * SAFE_SCORE

    @pl.when(small)
    def _():
        all_blocks(False)

    @pl.when(jnp.logical_not(small))
    def _():
        all_blocks(True)

    for c in range(together):
        att_t = jnp.concatenate([att_t_s[c, b] for b in range(blocks)], axis=1)
        d_query_t = jnp.concatenate([d_query_t_s[c, b] for b in range(blocks)], axis=1)
        gate_t = gate_t_s[c]
        gated_t = (gate_t * att_t).astype(BF16)
        d_gpre_t = (d_gated_t_s[c] * att_t * gate_t * (1.0 - gate_t)).astype(BF16)
        d_qg_t = jnp.concatenate([(d_query_t * scale).astype(BF16), d_gpre_t], axis=0)
        d_kv = d_kv_s[c].reshape(blocks * size, 2 * proj).astype(BF16)
        w_qg = jnp.concatenate([w_all_ref[:, :proj], w_all_ref[:, 3 * proj :]], axis=1)
        d_pair_s[...] = dot(d_kv, w_all_t_ref[proj : 3 * proj, :]) + dot(w_qg, d_qg_t).T
        for s in range(pieces):
            rows = pl.ds(pl.multiple_of(owners_ref[s] * tile_rows, tile_rows), tile_rows)
            d_pair_out[s][c] = d_pair_s[rows, :].astype(BF16)
        dw_qg_s[...] += dot(d_qg_t, act_s[c])
        dw_kv_s[...] += dot(act_t_s[c], d_kv)
        dwo_s[...] += dot(gated_t, grad_s[c])

    if last:

        @pl.when(pl.program_id(0) == pl.num_programs(0) - 1)
        def _():
            tile = d_bias_out.shape[3]
            for b in range(blocks):
                for e in range(slots):
                    for h in range(heads):
                        turned = d_bias_s[b, e, h].T.astype(BF16)
                        for sub in range(size // tile):
                            d_bias_out[b * (size // tile) + sub, e, h] = turned[
                                sub * tile : (sub + 1) * tile
                            ]
            d_w_out[0] = dw_qg_s[:proj, :].T
            d_w_out[1] = dw_kv_s[:, :proj]
            d_w_out[2] = dw_kv_s[:, proj:]
            d_w_out[3] = dw_qg_s[proj:, :].T
            d_w_out[4] = dwo_s[...]


def attention(pieces, bias, w_all, w_out, tables, lens, owners, carried, last, query_tile):
    count = len(pieces)
    _, columns, tile_rows, chan = pieces[0].shape
    blocks, slots = tables.shape
    heads = bias.shape[2]
    proj = w_out.shape[0]
    size = tile_rows * count // blocks
    tokens = blocks * size
    together = math.gcd(TOGETHER, columns)
    dims = (count, heads, proj // heads, blocks, size, slots, together)
    first = carried is None

    def whole(x):
        return pl.BlockSpec(x.shape, lambda j, *_: (0,) * len(x.shape))

    sums = [
        ((blocks, slots, heads, size, size), F32),
        ((2 * proj, chan), F32),
        ((chan, 2 * proj), F32),
        ((proj, chan), F32),
    ]
    if last:
        results = [
            ((tokens // query_tile, slots, heads, query_tile, size), BF16),
            ((5, chan, proj), F32),
        ]
    else:
        results = sums
    results = [jax.ShapeDtypeStruct(*x) for x in results]
    scratch = [
        ((together, tokens, chan), BF16),
        ((together, tokens, chan), BF16),
        ((together, chan, tokens), BF16),
        ((together, blocks, size, 2 * proj), BF16),
        ((together, blocks, 2 * proj, size), BF16),
        ((together, blocks, heads, 2 * proj, 2 * size), BF16),
        ((together, blocks, heads * size, proj), BF16),
        ((together, blocks, heads * size, proj), BF16),
        ((together, proj, tokens), F32),
        ((together, proj, tokens), F32),
        ((together, heads, slots * size, 2 * size), F32),
        ((together, slots * size, heads * size), BF16),
        ((together, slots * size, heads * size), BF16),
        ((together, blocks, size, 2 * proj), F32),
        ((together, blocks, proj, size), F32),
        ((together, blocks, proj, size), F32),
        ((tokens, chan), F32),
    ]
    scratch = [pltpu.VMEM(*x) for x in (sums if last else []) + scratch]
    fixed = [bias, w_all, w_all.T, w_out] + ([] if first else list(carried))
    pairs = tokens * size * slots * heads
    outs = pl.pallas_call(
        functools.partial(attention_kernel, dims, first, last),
        grid_spec=pltpu.PrefetchScalarGridSpec(
            num_scalar_prefetch=3,
            grid=(columns // together,),
            in_specs=[
                pl.BlockSpec((2, together, tile_rows, chan), lambda j, *_: (0, j, 0, 0))
            ] * count
            + [whole(x) for x in fixed],
            out_specs=[pl.BlockSpec((together, tile_rows, chan), lambda j, *_: (j, 0, 0))] * count
            + [whole(x) for x in results],
            scratch_shapes=scratch,
        ),
        out_shape=[jax.ShapeDtypeStruct((columns, tile_rows, chan), BF16)] * count + results,
        compiler_params=pltpu.CompilerParams(vmem_limit_bytes=VMEM_LIMIT),
        cost_estimate=pl.CostEstimate(
            flops=columns * pairs * 1200,
            bytes_accessed=columns * tokens * chan * 6 + 10 * 2**20,
            transcendentals=columns * pairs,
        ),
    )(tables, lens, owners, *pieces, *fixed)
    return outs[:count], outs[count:]


class Peers:
    def __init__(self, axis, stride, count):
        self.axis, self.count = axis, count
        self.paired = count & (count - 1) == 0
        place = lax.axis_index(axis)
        self.digit = place // stride % count
        everyone = range(lax.axis_size(axis))
        self.routes = []
        for s in range(count):
            route = []
            for p in everyone:
                d = p // stride % count
                route.append((p, p + (self.step(d, s) - d) * stride))
            self.routes.append(route)

    def step(self, digit, s):
        return digit ^ s if self.paired else (digit + s) % self.count

    def target(self, s):
        return self.step(self.digit, s)

    def source(self, s):
        return self.target(s) if self.paired else (self.digit - s) % self.count

    def send(self, x, s, home=False):
        route = self.routes[s]
        if home:
            route = [(t, f) for f, t in route]
        return x if s == 0 else lax.ppermute(x, self.axis, route)

    def positions(self):
        digits = jnp.arange(self.count)
        return self.digit ^ digits if self.paired else (self.digit - digits) % self.count

    def gather(self, x):
        return jnp.stack([self.send(x, s) for s in range(self.count)])

    def scatter_sum(self, parts):
        total = None
        for s in range(self.count):
            mine = [lax.dynamic_index_in_dim(p, self.target(s), 0, keepdims=False) for p in parts]
            total = self.add(total, mine, s)
        return total

    def add(self, total, parts, s):
        width = parts[0].shape[-1]
        if s and all(p.shape[-1] == width for p in parts):
            joined = jnp.concatenate([p.reshape(-1, width).astype(BF16) for p in parts])
            joined = self.send(joined, s)
            came, at = [], 0
            for p in parts:
                rows = p.size // width
                came.append(joined[at : at + rows].reshape(p.shape))
                at += rows
        else:
            came = [self.send(p.astype(BF16), s) if s else p for p in parts]
        came = [x.astype(F32) for x in came]
        return came if total is None else [t + x for t, x in zip(total, came)]


def on_device(
    pair_act, out_grad, tri_bias, w_query, w_key, w_value, w_gate, w_out, key_blocks, list_len
):
    row_count = lax.axis_size("row")
    col_count = lax.axis_size("col")
    tile_rows, tile_cols, chan = pair_act.shape
    heads = tri_bias.shape[0]
    query_tile = tri_bias.shape[2]
    proj = w_query.shape[1]
    blocks, slots = key_blocks.shape
    tokens = tile_rows * row_count
    size = tokens // blocks
    col_width = tile_cols // row_count
    chunks = math.gcd(CHUNKS, col_width)
    width = col_width // chunks
    inner = math.gcd(2, col_count)
    rows = Peers("row", 1, row_count)
    near = Peers("col", 1, inner)
    far = Peers("col", inner, col_count // inner)

    gathered = far.gather(rows.gather(jnp.transpose(tri_bias, (0, 2, 1))))
    gathered = near.gather(gathered).reshape((col_count,) + (row_count, heads, query_tile, tile_rows))
    columns = jnp.arange(col_count)
    col_pos = near.positions()[columns % inner] * far.count + far.positions()[columns // inner]
    bias = shifted_bias(
        gathered,
        key_blocks,
        list_len,
        col_pos.astype(jnp.int32),
        rows.positions().astype(jnp.int32),
    )

    both = jnp.stack([pair_act, out_grad]).reshape(2, tile_rows, row_count, chunks, width, chan)
    both = jnp.transpose(both, (2, 3, 0, 4, 1, 5))
    owners = jnp.stack([rows.source(s) for s in range(row_count)]).astype(jnp.int32)
    w_all = jnp.concatenate([w_query, w_key, w_value, w_gate], axis=1)
    outgoing = [
        lax.dynamic_index_in_dim(both, rows.target(s), 0, keepdims=False) for s in range(row_count)
    ]
    carried = None
    returned = []
    for c in range(chunks):
        pieces = [rows.send(outgoing[s][c], s) for s in range(row_count)]
        d_pieces, carried = attention(
            pieces, bias, w_all, w_out, key_blocks, list_len, owners, carried,
            c == chunks - 1, query_tile,
        )
        returned.append(jnp.stack([rows.send(d_pieces[s], s, home=True) for s in range(row_count)]))

    d_pair = jnp.stack(returned, axis=1)
    steps = jnp.arange(row_count)
    order = rows.digit ^ steps if rows.paired else (steps - rows.digit) % row_count
    d_pair = jnp.take(d_pair, order, axis=0)
    d_pair = jnp.transpose(d_pair, (3, 0, 1, 2, 4)).reshape(tile_rows, tile_cols, chan)

    slot_bias, w_part = carried
    weights = w_part.shape[0]
    w_part = w_part.reshape(col_count // inner, inner, -1, proj)
    slot_bias = slot_bias.reshape((col_count // inner, inner) + slot_bias.shape[1:])
    parts = near.scatter_sum([jnp.moveaxis(slot_bias, 1, 0), jnp.moveaxis(w_part, 1, 0)])
    slot_bias, w_part = far.scatter_sum(parts)
    block = lax.axis_index("col") * query_tile // size
    chosen = lax.dynamic_index_in_dim(key_blocks, block, 0, keepdims=False)
    live = jnp.arange(slots) < lax.dynamic_index_in_dim(list_len, block, 0, keepdims=False)
    per_block = size // tile_rows
    slot_bias = slot_bias.reshape(slots, heads, query_tile, per_block, tile_rows)

    total = None
    for s in range(row_count):
        owner = rows.target(s)
        piece = lax.dynamic_index_in_dim(slot_bias, owner % per_block, 3, keepdims=False)
        hit = (chosen == owner // per_block) & live
        piece = jnp.sum(jnp.where(hit[:, None, None, None], piece, 0.0), axis=0)
        total = rows.add(total, [piece, w_part], s)
    d_bias, w_part = total
    w_sum = near.gather(far.gather(w_part.astype(BF16)))
    w_sum = jnp.take(jnp.take(w_sum, near.positions(), axis=0), far.positions(), axis=1)
    w_sum = jnp.moveaxis(w_sum, 0, 1).reshape(weights, chan, proj).astype(F32)
    return (d_pair, jnp.transpose(d_bias, (0, 2, 1))) + tuple(w_sum[n] for n in range(weights))


def solution(mesh):
    in_specs = (
        P("row", "col", None),
        P("row", "col", None),
        P(None, "row", "col"),
        P(),
        P(),
        P(),
        P(),
        P(),
        P(),
        P(),
    )
    out_specs = (P("row", "col", None), P(None, "row", "col"), P(), P(), P(), P(), P())
    return jax.shard_map(
        on_device, mesh=mesh, in_specs=in_specs, out_specs=out_specs, check_vma=False
    )
```

```python
import functools
import math

import jax
import jax.numpy as jnp
from jax import lax
from jax.experimental import pallas as pl
from jax.experimental.pallas import tpu as pltpu
from jax.sharding import PartitionSpec as P

F32 = jnp.float32
BF16 = jnp.bfloat16
CHUNKS = 2
TOGETHER = 2
STRIP = 32
LOG2E = math.log2(math.e)
SAFE_SCORE = 30.0
VMEM_LIMIT = 56 * 1024 * 1024


def dot(a, b):
    return jnp.dot(a, b, preferred_element_type=F32)


def bias_kernel(tables_ref, lens_ref, col_pos_ref, row_pos_ref, *refs):
    *parts, out_ref = refs
    b = pl.program_id(0)
    blocks, _, heads, size, _ = out_ref.shape
    slots = tables_ref.shape[1]
    rows, _, _, tile = parts[0].shape[1:]
    per_block = size // tile
    for h in range(heads):
        for r in range(rows):
            piece = jnp.concatenate([p[0, row_pos_ref[r], h] for p in parts], axis=0)
            at = (r % per_block) * tile
            out_ref[r // per_block, 0, h, at : at + tile, :] = piece.astype(F32).T
    for h in range(heads):
        peak = jnp.max(out_ref[tables_ref[b, 0], 0, h], axis=0, keepdims=True)
        for e in range(1, slots):
            other = jnp.max(out_ref[tables_ref[b, e], 0, h], axis=0, keepdims=True)
            peak = jnp.where(e < lens_ref[b], jnp.maximum(peak, other), peak)
        for kb in range(blocks):
            out_ref[kb, 0, h] = (out_ref[kb, 0, h] - peak) * LOG2E


def shifted_bias(gathered, key_blocks, list_len, col_pos, row_pos):
    cols, rows, heads, query_tile, key_tile = gathered.shape
    blocks = key_blocks.shape[0]
    size = cols * query_tile // blocks
    per_block = size // query_tile

    def part(sub):
        return pl.BlockSpec(
            (1, rows, heads, query_tile, key_tile),
            lambda b, tables, lens, col_at, row_at: (col_at[b * per_block + sub], 0, 0, 0, 0),
        )

    return pl.pallas_call(
        bias_kernel,
        grid_spec=pltpu.PrefetchScalarGridSpec(
            num_scalar_prefetch=4,
            grid=(blocks,),
            in_specs=[part(sub) for sub in range(per_block)],
            out_specs=pl.BlockSpec((blocks, 1, heads, size, size), lambda b, *_: (0, b, 0, 0, 0)),
        ),
        out_shape=jax.ShapeDtypeStruct((blocks, blocks, heads, size, size), F32),
        compiler_params=pltpu.CompilerParams(vmem_limit_bytes=VMEM_LIMIT),
    )(key_blocks, list_len, col_pos, row_pos, *([gathered] * per_block))


def attention_kernel(
    dims, first, last, tables_ref, lens_ref, owners_ref, parity_ref, *refs
):
    pieces, heads, head_dim, blocks, size, slots, together, inner = dims
    refs = list(refs)
    take = lambda n: [refs.pop(0) for _ in range(n)]
    inputs = take(pieces)
    bias_ref, w_all_ref, w_all_t_ref, w_out_ref = take(4)
    carried = [] if first else take(5)
    if last:
        d_pair_out = take(pieces)
        keep_out, message_out, d_w_out = take(3)
        d_pair_s, *sums = take(5)
    else:
        d_pair_s, *sums = take(5)
    d_bias_s, dw_qg_s, dw_kv_s, dwo_s = sums
    (x_s, act_s, grad_s, act_t_s, kv_s, kv_t_s, joint_s, d_att_s, query_s, gate_t_s, d_gated_t_s,
     score_s, probs_s, ds_s, d_kv_s, att_t_s, d_query_t_s) = refs
    proj = heads * head_dim
    scale = head_dim ** (-0.5)
    _, tile_rows, width, chan = inputs[0].shape
    tokens = blocks * size
    all_width = d_pair_s.shape[0] // tokens
    step = pl.program_id(0)
    span = [slice(b * size, (b + 1) * size) for b in range(blocks)]
    own = [slice(h * head_dim, (h + 1) * head_dim) for h in range(heads)]
    low = [slice(proj + h * head_dim, proj + (h + 1) * head_dim) for h in range(heads)]

    def rows_at(s, columns):
        count = tile_rows * columns
        return pl.ds(pl.multiple_of(owners_ref[s] * count, count), count)

    @pl.when(step == 0)
    def _():
        joint_s[...] = jnp.zeros_like(joint_s)
        for n, ref in enumerate(sums):
            ref[...] = jnp.zeros_like(ref) if first else carried[n + 1][...]
        if not first:
            before = all_width - width
            for j in range(before):
                d_pair_s[pl.ds(j, tokens, stride=all_width), :] = carried[0][
                    pl.ds(j, tokens, stride=before), :
                ]
        for s in range(pieces):
            for n in range(2):
                x_s[n, rows_at(s, width), :] = (
                    inputs[s][n].astype(F32).reshape(tile_rows * width, chan)
                )

    lane_head = lax.broadcasted_iota(jnp.int32, (size, proj), 1) // head_dim
    bound = jnp.float32(0.0)
    for c in range(together):
        column = pl.ds(step * together + c, tokens, stride=width)
        acts = x_s[0, column, :].astype(BF16)
        grads = x_s[1, column, :].astype(BF16)
        act_s[c] = acts
        grad_s[c] = grads
        acts_t = acts.T
        act_t_s[c] = acts_t
        natural = dot(acts, w_all_ref[:, : 3 * proj])
        across = dot(w_all_t_ref[...], acts_t)
        queries_t = (across[:proj] * scale).astype(BF16)
        kv_t = across[proj : 3 * proj].astype(BF16)
        gate_t = 1.0 / (1.0 + jnp.exp(-across[3 * proj :]))
        d_gated_t = dot(w_out_ref[...], grads.T)
        d_att_t = (d_gated_t * gate_t).astype(BF16)
        gate_t_s[c] = gate_t
        d_gated_t_s[c] = d_gated_t
        squares = lambda x: jnp.max(
            jnp.sum(jnp.square(x.astype(F32)).reshape(heads, head_dim, -1), axis=1)
        )
        bound = jnp.maximum(bound, squares(queries_t) * squares(kv_t[:proj]))
        queries = (natural[:, :proj] * scale).astype(BF16)
        kv = natural[:, proj:].astype(BF16)
        zero = jnp.zeros((size, proj), BF16)
        for b in range(blocks):
            kv_s[c, b] = kv[span[b]]
            kv_t_s[c, b] = kv_t[:, span[b]]
            d_att = d_att_t[:, span[b]].T
            for h in range(heads):
                joint_s[c, b, h, own[h], :size] = queries_t[own[h], span[b]]
                joint_s[c, b, h, low[h], size:] = d_att_t[own[h], span[b]]
                here = lane_head == h
                query_s[c, b, h * size : (h + 1) * size, :] = jnp.where(here, queries[span[b]], zero)
                d_att_s[c, b, h * size : (h + 1) * size, :] = jnp.where(here, d_att, zero)
    d_kv_s[...] = jnp.zeros_like(d_kv_s)

    def query_block(b, live, shift):
        chosen = [tables_ref[b, e] for e in range(live)]
        strips = [
            (e, e * size + at, at) for e in range(live) for at in range(0, size, STRIP)
        ]
        rows_of = lambda x: jnp.sum(x.reshape(-1, 8, size), axis=0)
        kv = [jnp.concatenate([kv_s[c, k] for k in chosen], axis=0) for c in range(together)]
        kv_t = [jnp.concatenate([kv_t_s[c, k] for k in chosen], axis=1) for c in range(together)]
        for h in range(heads):
            stats = []
            for c in range(together):
                joint = dot(kv[c], joint_s[c, b, h])

                def scores(e, row, at):
                    return (
                        joint[row : row + STRIP, :size] * LOG2E
                        + bias_ref[chosen[e], b, h, at : at + STRIP, :]
                    )

                if shift:
                    peak = jnp.full((8, size), -jnp.inf, F32)
                    for strip in strips:
                        peak = jnp.maximum(
                            peak, jnp.max(scores(*strip).reshape(-1, 8, size), axis=0)
                        )
                    peak = jnp.max(peak, axis=0, keepdims=True)
                total = jnp.zeros((8, size), F32)
                mixed = jnp.zeros((8, size), F32)
                for e, row, at in strips:
                    value = scores(e, row, at)
                    weight = jnp.exp2(value - peak if shift else value)
                    d_probs = joint[row : row + STRIP, size:]
                    total += rows_of(weight)
                    mixed += rows_of(weight * d_probs)
                    score_s[c, h, row : row + STRIP, :size] = weight
                    score_s[c, h, row : row + STRIP, size:] = d_probs
                norm = 1.0 / jnp.sum(total, axis=0, keepdims=True)
                stats.append((norm, jnp.sum(mixed, axis=0, keepdims=True) * norm))
            lanes = slice(h * size, (h + 1) * size)
            for e, row, at in strips:
                part = slice(row, row + STRIP)
                gathered = d_bias_s[b, e, h, at : at + STRIP, :]
                for c, (norm, delta) in enumerate(stats):
                    probs = score_s[c, h, part, :size] * norm
                    d_scores = probs * (score_s[c, h, part, size:] - delta)
                    probs_s[c, part, lanes] = probs.astype(BF16)
                    ds_s[c, part, lanes] = d_scores.astype(BF16)
                    gathered += d_scores
                d_bias_s[b, e, h, at : at + STRIP, :] = gathered
            for c in range(together):
                att_t_s[c, b, own[h], :] = dot(kv_t[c][low[h]], probs_s[c, : live * size, lanes])
                d_query_t_s[c, b, own[h], :] = dot(kv_t[c][own[h]], ds_s[c, : live * size, lanes])
        for c in range(together):
            d_values = dot(probs_s[c, : live * size, :], d_att_s[c, b])
            d_keys = dot(ds_s[c, : live * size, :], query_s[c, b])
            for e in range(live):
                part = slice(e * size, (e + 1) * size)
                d_kv_s[c, chosen[e], :, :proj] += d_keys[part]
                d_kv_s[c, chosen[e], :, proj:] += d_values[part]

    def all_blocks(shift):
        @pl.loop(0, blocks)
        def _(b):
            for live in range(1, slots + 1):

                @pl.when(lens_ref[b] == live)
                def _():
                    query_block(b, live, shift)

    small = bound <= SAFE_SCORE * SAFE_SCORE

    @pl.when(small)
    def _():
        all_blocks(False)

    @pl.when(jnp.logical_not(small))
    def _():
        all_blocks(True)

    w_qg = jnp.concatenate([w_all_ref[:, :proj], w_all_ref[:, 3 * proj :]], axis=1)
    for c in range(together):
        att_t = jnp.concatenate([att_t_s[c, b] for b in range(blocks)], axis=1)
        d_query_t = jnp.concatenate([d_query_t_s[c, b] for b in range(blocks)], axis=1)
        gate_t = gate_t_s[c]
        gated_t = (gate_t * att_t).astype(BF16)
        d_gpre_t = (d_gated_t_s[c] * att_t * gate_t * (1.0 - gate_t)).astype(BF16)
        d_qg_t = jnp.concatenate([(d_query_t * scale).astype(BF16), d_gpre_t], axis=0)
        d_kv = d_kv_s[c].reshape(tokens, 2 * proj).astype(BF16)
        column = pl.ds(all_width - width + step * together + c, tokens, stride=all_width)
        d_pair_s[column, :] = (
            dot(d_kv, w_all_t_ref[proj : 3 * proj, :]) + dot(w_qg, d_qg_t).T
        )
        dw_qg_s[...] += dot(d_qg_t, act_s[c])
        dw_kv_s[...] += dot(act_t_s[c], d_kv)
        dwo_s[...] += dot(gated_t, grad_s[c])

    if not last:
        return

    @pl.when(step == pl.num_programs(0) - 1)
    def _():
        for s in range(pieces):
            piece = d_pair_s[rows_at(s, all_width), :].reshape(tile_rows, all_width, chan)
            d_pair_out[s][...] = piece.astype(BF16)
        weights = [dw_qg_s[:proj, :].T, dw_kv_s[:, :proj], dw_kv_s[:, proj:], dw_qg_s[proj:, :].T]
        weights.append(dwo_s[...])
        far, each = keep_out.shape[0], keep_out.shape[1]
        tile = each // (slots * heads)
        for n, w in enumerate(weights):
            d_w_out[n * chan : (n + 1) * chan, :] = w
            message_out[far * each + n * chan : far * each + (n + 1) * chan, :] = w.astype(BF16)
        for mine in range(inner):

            @pl.when(parity_ref[0] == mine)
            def _():
                for b in range(blocks):
                    for e in range(slots):
                        for h in range(heads):
                            turned = d_bias_s[b, e, h].T.astype(BF16)
                            at = (e * heads + h) * tile
                            for sub in range(size // tile):
                                col = b * (size // tile) + sub
                                piece = turned[sub * tile : (sub + 1) * tile]
                                if col % inner == mine:
                                    keep_out[col // inner, at : at + tile, :] = piece
                                else:
                                    start = (col // inner) * each + at
                                    message_out[start : start + tile, :] = piece


def attention(
    pieces, bias, w_all, w_out, tables, lens, owners, parity, carried, last, query_tile, inner
):
    count = len(pieces)
    _, tile_rows, columns, chan = pieces[0].shape
    blocks, slots = tables.shape
    heads = bias.shape[2]
    proj = w_out.shape[0]
    size = tile_rows * count // blocks
    tokens = blocks * size
    together = math.gcd(TOGETHER, columns)
    dims = (count, heads, proj // heads, blocks, size, slots, together, inner)
    first = carried is None
    all_width = columns + (0 if first else carried[0].shape[0] // tokens)
    far = tokens // query_tile // inner

    def whole(x):
        return pl.BlockSpec(x.shape, lambda j, *_: (0,) * len(x.shape))

    sums = [
        ((tokens * all_width, chan), F32),
        ((blocks, slots, heads, size, size), F32),
        ((2 * proj, chan), F32),
        ((chan, 2 * proj), F32),
        ((proj, chan), F32),
    ]
    if last:
        each = slots * heads * query_tile
        results = [((tile_rows, all_width, chan), BF16)] * count + [
            ((far, each, size), BF16),
            ((far * each + 5 * chan, size), BF16),
            ((5 * chan, proj), F32),
        ]
    else:
        results = sums
    results = [jax.ShapeDtypeStruct(*x) for x in results]
    scratch = [
        ((2, tokens * columns, chan), F32),
        ((together, tokens, chan), BF16),
        ((together, tokens, chan), BF16),
        ((together, chan, tokens), BF16),
        ((together, blocks, size, 2 * proj), BF16),
        ((together, blocks, 2 * proj, size), BF16),
        ((together, blocks, heads, 2 * proj, 2 * size), BF16),
        ((together, blocks, heads * size, proj), BF16),
        ((together, blocks, heads * size, proj), BF16),
        ((together, proj, tokens), F32),
        ((together, proj, tokens), F32),
        ((together, heads, slots * size, 2 * size), F32),
        ((together, slots * size, heads * size), BF16),
        ((together, slots * size, heads * size), BF16),
        ((together, blocks, size, 2 * proj), F32),
        ((together, blocks, proj, size), F32),
        ((together, blocks, proj, size), F32),
    ]
    scratch = [pltpu.VMEM(*x) for x in (sums if last else []) + scratch]
    fixed = [bias, w_all, w_all.T, w_out] + ([] if first else list(carried))
    pairs = tokens * size * slots * heads
    operands = list(pieces) + fixed
    return pl.pallas_call(
        functools.partial(attention_kernel, dims, first, last),
        grid_spec=pltpu.PrefetchScalarGridSpec(
            num_scalar_prefetch=4,
            grid=(columns // together,),
            in_specs=[whole(x) for x in operands],
            out_specs=[whole(x) for x in results],
            scratch_shapes=scratch,
        ),
        out_shape=results,
        compiler_params=pltpu.CompilerParams(vmem_limit_bytes=VMEM_LIMIT),
        cost_estimate=pl.CostEstimate(
            flops=columns * pairs * 1200,
            bytes_accessed=columns * tokens * chan * 6 + 10 * 2**20,
            transcendentals=columns * pairs,
        ),
    )(tables, lens, owners, parity, *operands)


def small_call(body, scalars, arrays, results):
    return pl.pallas_call(
        body,
        grid_spec=pltpu.PrefetchScalarGridSpec(
            num_scalar_prefetch=len(scalars),
            grid=(1,),
            in_specs=[pl.BlockSpec(x.shape, lambda j, *_, n=x.ndim: (0,) * n) for x in arrays],
            out_specs=[
                pl.BlockSpec(x[0], lambda j, *_, n=len(x[0]): (0,) * n) for x in results
            ],
        ),
        out_shape=[jax.ShapeDtypeStruct(*x) for x in results],
        compiler_params=pltpu.CompilerParams(vmem_limit_bytes=VMEM_LIMIT),
    )(*scalars, *arrays)


def aligned(index, count):
    return pl.ds(pl.multiple_of(index * count, count), count)


def split_by_far(targets, keep, came, weights):
    far, each, lanes = keep.shape
    share = weights.shape[0] // far

    def body(targets_ref, keep_ref, came_ref, weights_ref, own_ref, *message_refs):
        for s in range(far):
            t = targets_ref[s]
            out = message_refs[s - 1] if s else own_ref
            bias = keep_ref[t].astype(F32)
            weight = weights_ref[aligned(t, share), :].astype(BF16).astype(F32)
            if came_ref is not None:
                bias += came_ref[aligned(t, each), :].astype(F32)
                rest = came_ref[far * each :, :].astype(F32)
                half = jnp.zeros_like(weight)
                for u in range(far):
                    half = jnp.where(t == u, rest[u * share : (u + 1) * share], half)
                weight += half
            out[:each, :] = bias.astype(out.dtype)
            out[each:, :] = weight.astype(out.dtype)

    results = [((each + share, lanes), F32 if s == 0 else BF16) for s in range(far)]
    return small_call(body, [targets], [keep, came, weights], results)


def split_by_row(owners, chosen, live, own, came, dims):
    rows, slots, per_block, each = dims
    lanes = own.shape[1]
    part = each // slots
    share = own.shape[0] - each

    def body(owners_ref, chosen_ref, live_ref, own_ref, *refs):
        came_refs, outs = refs[: len(came)], refs[len(came) :]
        weight = own_ref[each:, :]
        for ref in came_refs:
            weight += ref[each:, :].astype(F32)
        for s in range(rows):
            outs[s][part:, :] = weight.astype(BF16).astype(outs[s].dtype)
            outs[s][:part, :] = jnp.zeros((part, lanes), outs[s].dtype)
        for e in range(slots):
            at = slice(e * part, (e + 1) * part)
            bias = own_ref[at, :]
            for ref in came_refs:
                bias += ref[at, :].astype(F32)
            for s in range(rows):
                hit = (chosen_ref[e] == owners_ref[s] // per_block) & (e < live_ref[0])

                @pl.when(hit)
                def _():
                    outs[s][:part, :] = bias.astype(outs[s].dtype)

    results = [((part + share, lanes), F32 if s == 0 else BF16) for s in range(rows)]
    return small_call(body, [owners, chosen, live], [own, *came], results)


def add_rows(own, came, part):
    share, lanes = own.shape[0] - part, own.shape[1]

    def body(own_ref, *refs):
        came_refs, (bias_ref, weight_ref) = refs[: len(came)], refs[len(came) :]
        terms = [own_ref[...]] + [ref[...].astype(F32) for ref in came_refs]
        while len(terms) > 1:
            terms = [sum(terms[n : n + 2]) for n in range(0, len(terms), 2)]
        total = terms[0]
        bias_ref[...] = total[:part]
        weight_ref[...] = total[part:].astype(BF16)

    results = [((part, lanes), F32), ((share, lanes), BF16)]
    return small_call(body, [], [own, *came], results)


def place_weights(sources, parts, count):
    share, lanes = parts[0].shape

    def body(sources_ref, *refs):
        part_refs, out_refs, scratch = refs[: len(parts)], refs[len(parts) : -1], refs[-1]
        for s, ref in enumerate(part_refs):
            scratch[aligned(sources_ref[s], share), :] = ref[...].astype(F32)
        for n, ref in enumerate(out_refs):
            ref[...] = scratch[n * lanes : (n + 1) * lanes, :]

    rows = share * len(parts)
    shape = (rows // count, lanes)
    return pl.pallas_call(
        body,
        grid_spec=pltpu.PrefetchScalarGridSpec(
            num_scalar_prefetch=1,
            grid=(1,),
            in_specs=[pl.BlockSpec(x.shape, lambda j, *_: (0, 0)) for x in parts],
            out_specs=[pl.BlockSpec(shape, lambda j, *_: (0, 0))] * count,
            scratch_shapes=[pltpu.VMEM((rows, lanes), F32)],
        ),
        out_shape=[jax.ShapeDtypeStruct(shape, F32)] * count,
    )(sources, *parts)


def place_pair(groups, pieces):
    tile_rows, width, chan = pieces[0].shape

    def body(groups_ref, *refs):
        for s, ref in enumerate(refs[:-1]):
            refs[-1][:, groups_ref[s]] = ref[...]

    out = small_call(body, [groups], pieces, [((tile_rows, len(pieces), width, chan), BF16)])[0]
    return out.reshape(tile_rows, len(pieces) * width, chan)


class Peers:
    def __init__(self, axis, stride, count):
        self.axis, self.count = axis, count
        self.paired = count & (count - 1) == 0
        place = lax.axis_index(axis)
        self.digit = place // stride % count
        everyone = range(lax.axis_size(axis))
        self.routes = []
        for s in range(count):
            route = []
            for p in everyone:
                d = p // stride % count
                route.append((p, p + (self.step(d, s) - d) * stride))
            self.routes.append(route)

    def step(self, digit, s):
        return digit ^ s if self.paired else (digit + s) % self.count

    def target(self, s):
        return self.step(self.digit, s)

    def source(self, s):
        return self.target(s) if self.paired else (self.digit - s) % self.count

    def send(self, x, s, home=False):
        route = self.routes[s]
        if home:
            route = [(t, f) for f, t in route]
        return x if s == 0 else lax.ppermute(x, self.axis, route)

    def positions(self):
        digits = jnp.arange(self.count)
        return self.digit ^ digits if self.paired else (self.digit - digits) % self.count

    def gather(self, x):
        return jnp.stack([self.send(x, s) for s in range(self.count)])

    def targets(self):
        return jnp.stack([self.target(s) for s in range(self.count)]).astype(jnp.int32)

    def sources(self):
        return jnp.stack([self.source(s) for s in range(self.count)]).astype(jnp.int32)

    def swap(self, messages):
        return [self.send(x, s + 1) for s, x in enumerate(messages)]


def on_device(
    pair_act, out_grad, tri_bias, w_query, w_key, w_value, w_gate, w_out, key_blocks, list_len
):
    row_count = lax.axis_size("row")
    col_count = lax.axis_size("col")
    tile_rows, tile_cols, chan = pair_act.shape
    heads = tri_bias.shape[0]
    query_tile = tri_bias.shape[2]
    proj = w_query.shape[1]
    blocks, slots = key_blocks.shape
    tokens = tile_rows * row_count
    size = tokens // blocks
    col_width = tile_cols // row_count
    chunks = math.gcd(CHUNKS, col_width)
    width = col_width // chunks
    inner = math.gcd(2, col_count)
    rows = Peers("row", 1, row_count)
    near = Peers("col", 1, inner)
    far = Peers("col", inner, col_count // inner)

    gathered = far.gather(rows.gather(jnp.transpose(tri_bias, (0, 2, 1))))
    gathered = near.gather(gathered).reshape((col_count,) + (row_count, heads, query_tile, tile_rows))
    columns = jnp.arange(col_count)
    col_pos = near.positions()[columns % inner] * far.count + far.positions()[columns // inner]
    bias = shifted_bias(
        gathered,
        key_blocks,
        list_len,
        col_pos.astype(jnp.int32),
        rows.positions().astype(jnp.int32),
    )

    owners = rows.sources()
    parity = near.targets()[:1]
    w_all = jnp.concatenate([w_query, w_key, w_value, w_gate], axis=1)

    def piece(s, c):
        at = rows.target(s) * col_width + c * width
        cut = lambda x: lax.dynamic_slice_in_dim(x, at, width, 1)
        return rows.send(jnp.stack([cut(pair_act), cut(out_grad)]), s)

    carried = None
    for c in range(chunks):
        pieces = [piece(s, c) for s in range(row_count)]
        carried = attention(
            pieces, bias, w_all, w_out, key_blocks, list_len, owners, parity, carried,
            c == chunks - 1, query_tile, inner,
        )
    *d_pieces, keep, message, w_part = carried
    far_targets, row_targets = far.targets(), rows.targets()

    each = keep.shape[1]
    own, *messages = split_by_far(far_targets, keep, near.send(message, inner - 1), w_part)
    came = far.swap(messages)
    block = lax.axis_index("col") * query_tile // size
    chosen = lax.dynamic_index_in_dim(key_blocks, block, 0, keepdims=False)
    live = lax.dynamic_slice_in_dim(list_len, block, 1)
    per_block = size // tile_rows
    own, *messages = split_by_row(
        row_targets, chosen, live, own, came, (row_count, slots, per_block, each)
    )
    d_bias, w_part = add_rows(own, rows.swap(messages), each // slots)
    weights = place_weights(far.sources(), [far.send(w_part, s) for s in range(far.count)], 5)
    d_bias = d_bias.reshape(heads, query_tile, per_block, tile_rows)
    d_bias = lax.dynamic_index_in_dim(d_bias, rows.digit % per_block, 2, keepdims=False)

    d_pieces = [rows.send(x, s, home=True) for s, x in enumerate(d_pieces)]
    d_pair = place_pair(row_targets, d_pieces)
    return (d_pair, jnp.transpose(d_bias, (0, 2, 1)), *weights)


def solution(mesh):
    in_specs = (
        P("row", "col", None),
        P("row", "col", None),
        P(None, "row", "col"),
        P(),
        P(),
        P(),
        P(),
        P(),
        P(),
        P(),
    )
    out_specs = (P("row", "col", None), P(None, "row", "col"), P(), P(), P(), P(), P())
    return jax.shard_map(
        on_device, mesh=mesh, in_specs=in_specs, out_specs=out_specs, check_vma=False
    )
```

```python
import functools
import math

import jax
import jax.numpy as jnp
from jax import lax
from jax.experimental import pallas as pl
from jax.experimental.pallas import tpu as pltpu
from jax.sharding import PartitionSpec as P

F32 = jnp.float32
BF16 = jnp.bfloat16
CHUNKS = 2
TOGETHER = 4
STRIP = 32
LOG2E = math.log2(math.e)
SAFE_SCORE = 30.0
VMEM_LIMIT = 56 * 1024 * 1024
SMALL_LIMIT = 16 * 1024 * 1024


def dot(a, b):
    return jnp.dot(a, b, preferred_element_type=F32)


def bias_kernel(tables_ref, lens_ref, col_pos_ref, row_pos_ref, *refs):
    *parts, out_ref = refs
    b = pl.program_id(0)
    blocks, _, heads, size, _ = out_ref.shape
    slots = tables_ref.shape[1]
    rows, _, _, tile = parts[0].shape[1:]
    per_block = size // tile
    for h in range(heads):
        for r in range(rows):
            piece = jnp.concatenate([p[0, row_pos_ref[r], h] for p in parts], axis=0)
            at = (r % per_block) * tile
            out_ref[r // per_block, 0, h, at : at + tile, :] = piece.astype(F32).T
    for h in range(heads):
        peak = jnp.max(out_ref[tables_ref[b, 0], 0, h], axis=0, keepdims=True)
        for e in range(1, slots):
            other = jnp.max(out_ref[tables_ref[b, e], 0, h], axis=0, keepdims=True)
            peak = jnp.where(e < lens_ref[b], jnp.maximum(peak, other), peak)
        for kb in range(blocks):
            out_ref[kb, 0, h] = (out_ref[kb, 0, h] - peak) * LOG2E


def shifted_bias(gathered, key_blocks, list_len, col_pos, row_pos):
    cols, rows, heads, query_tile, key_tile = gathered.shape
    blocks = key_blocks.shape[0]
    size = cols * query_tile // blocks
    per_block = size // query_tile

    def part(sub):
        return pl.BlockSpec(
            (1, rows, heads, query_tile, key_tile),
            lambda b, tables, lens, col_at, row_at: (col_at[b * per_block + sub], 0, 0, 0, 0),
        )

    return pl.pallas_call(
        bias_kernel,
        grid_spec=pltpu.PrefetchScalarGridSpec(
            num_scalar_prefetch=4,
            grid=(blocks,),
            in_specs=[part(sub) for sub in range(per_block)],
            out_specs=pl.BlockSpec((blocks, 1, heads, size, size), lambda b, *_: (0, b, 0, 0, 0)),
        ),
        out_shape=jax.ShapeDtypeStruct((blocks, blocks, heads, size, size), F32),
        compiler_params=pltpu.CompilerParams(vmem_limit_bytes=VMEM_LIMIT),
    )(key_blocks, list_len, col_pos, row_pos, *([gathered] * per_block))


def attention_kernel(dims, first, last, tables_ref, lens_ref, parity_ref, *refs):
    heads, head_dim, blocks, size, slots, together, inner = dims
    refs = list(refs)
    take = lambda n: [refs.pop(0) for _ in range(n)]
    x_ref, bias_ref, w_all_ref, w_all_t_ref, w_out_ref = take(5)
    carried = [] if first else take(5)[1:]
    d_pair_ref = refs.pop(0)
    if last:
        keep_out, message_out, d_w_out = take(3)
    d_bias_s, dw_qg_s, dw_kv_s, dwo_s = sums = take(4)
    (act_t_s, kv_s, kv_t_s, w_score_s, w_probs_s, d_att_s, query_s, gate_t_s, d_gated_t_s,
     score_s, d_probs_s, probs_s, ds_s, d_kv_s, att_t_s, d_query_t_s) = refs
    proj = heads * head_dim
    scale = head_dim ** (-0.5)
    pieces, _, _, tile_rows, chan = x_ref.shape
    tokens = blocks * size
    step = pl.program_id(0)
    span = [slice(b * size, (b + 1) * size) for b in range(blocks)]
    own = [slice(h * head_dim, (h + 1) * head_dim) for h in range(heads)]
    low = [slice(proj + h * head_dim, proj + (h + 1) * head_dim) for h in range(heads)]
    head_lanes = [slice(h * size, (h + 1) * size) for h in range(heads)]

    @pl.when(step == 0)
    def _():
        w_score_s[...] = jnp.zeros_like(w_score_s)
        w_probs_s[...] = jnp.zeros_like(w_probs_s)
        for n, ref in enumerate(sums):
            ref[...] = jnp.zeros_like(ref) if first else carried[n][...]

    lane_head = lax.broadcasted_iota(jnp.int32, (size, proj), 1) // head_dim
    bound = jnp.float32(0.0)
    for c in range(together):
        acts = x_ref[:, 0, c].reshape(tokens, chan)
        grads = x_ref[:, 1, c].reshape(tokens, chan)
        acts_t = acts.T
        act_t_s[c] = acts_t
        natural = dot(acts, w_all_ref[:, : 3 * proj])
        across = dot(w_all_t_ref[...], acts_t)
        queries_t = (across[:proj] * scale).astype(BF16)
        kv_t = across[proj : 3 * proj].astype(BF16)
        gate_t = 1.0 / (1.0 + jnp.exp(-across[3 * proj :]))
        d_gated_t = dot(w_out_ref[...], grads.T)
        d_att_t = (d_gated_t * gate_t).astype(BF16)
        gate_t_s[c] = gate_t
        d_gated_t_s[c] = d_gated_t
        squares = lambda x: jnp.max(
            jnp.sum(jnp.square(x.astype(F32)).reshape(heads, head_dim, -1), axis=1)
        )
        bound = jnp.maximum(bound, squares(queries_t) * squares(kv_t[:proj]))
        queries = (natural[:, :proj] * scale).astype(BF16)
        kv = natural[:, proj:].astype(BF16)
        zero = jnp.zeros((size, proj), BF16)
        for b in range(blocks):
            kv_s[c, b] = kv[span[b]]
            kv_t_s[c, b] = kv_t[:, span[b]]
            d_att = d_att_t[:, span[b]].T
            for h in range(heads):
                w_score_s[c, b, own[h], head_lanes[h]] = queries_t[own[h], span[b]]
                w_probs_s[c, b, own[h], head_lanes[h]] = d_att_t[own[h], span[b]]
                here = lane_head == h
                query_s[c, b, h * size : (h + 1) * size, :] = jnp.where(here, queries[span[b]], zero)
                d_att_s[c, b, h * size : (h + 1) * size, :] = jnp.where(here, d_att, zero)
    d_kv_s[...] = jnp.zeros_like(d_kv_s)

    def query_block(b, live, shift):
        chosen = [tables_ref[b, e] for e in range(live)]
        strips = [
            (e, e * size + at, at) for e in range(live) for at in range(0, size, STRIP)
        ]
        rows_of = lambda x: jnp.sum(x.reshape(-1, 8, size), axis=0)
        for c in range(together):
            kv = jnp.concatenate([kv_s[c, k] for k in chosen], axis=0)
            score_s[c, : live * size, :] = dot(kv[:, :proj], w_score_s[c, b])
            d_probs_s[c, : live * size, :] = dot(kv[:, proj:], w_probs_s[c, b])
        for h in range(heads):
            lanes = head_lanes[h]
            stats = []
            for c in range(together):

                def scores(e, row, at):
                    return (
                        score_s[c, row : row + STRIP, lanes] * LOG2E
                        + bias_ref[chosen[e], b, h, at : at + STRIP, :]
                    )

                if shift:
                    peak = jnp.full((8, size), -jnp.inf, F32)
                    for strip in strips:
                        peak = jnp.maximum(
                            peak, jnp.max(scores(*strip).reshape(-1, 8, size), axis=0)
                        )
                    peak = jnp.max(peak, axis=0, keepdims=True)
                total = jnp.zeros((8, size), F32)
                mixed = jnp.zeros((8, size), F32)
                for e, row, at in strips:
                    value = scores(e, row, at)
                    weight = jnp.exp2(value - peak if shift else value)
                    total += rows_of(weight)
                    mixed += rows_of(weight * d_probs_s[c, row : row + STRIP, lanes])
                    score_s[c, row : row + STRIP, lanes] = weight
                norm = 1.0 / jnp.sum(total, axis=0, keepdims=True)
                stats.append((norm, jnp.sum(mixed, axis=0, keepdims=True) * norm))
            for e, row, at in strips:
                part = slice(row, row + STRIP)
                gathered = d_bias_s[b, e, h, at : at + STRIP, :]
                for c, (norm, delta) in enumerate(stats):
                    probs = score_s[c, part, lanes] * norm
                    d_scores = probs * (d_probs_s[c, part, lanes] - delta)
                    probs_s[c, part, lanes] = probs.astype(BF16)
                    ds_s[c, part, lanes] = d_scores.astype(BF16)
                    gathered += d_scores
                d_bias_s[b, e, h, at : at + STRIP, :] = gathered
        for c in range(together):
            kv_t = jnp.concatenate([kv_t_s[c, k] for k in chosen], axis=1)
            for h in range(heads):
                lanes = head_lanes[h]
                att_t_s[c, b, own[h], :] = dot(kv_t[low[h]], probs_s[c, : live * size, lanes])
                d_query_t_s[c, b, own[h], :] = dot(kv_t[own[h]], ds_s[c, : live * size, lanes])
            d_values = dot(probs_s[c, : live * size, :], d_att_s[c, b])
            d_keys = dot(ds_s[c, : live * size, :], query_s[c, b])
            for e in range(live):
                part = slice(e * size, (e + 1) * size)
                d_kv_s[c, chosen[e], :, :proj] += d_keys[part]
                d_kv_s[c, chosen[e], :, proj:] += d_values[part]

    def all_blocks(shift):
        @pl.loop(0, blocks)
        def _(b):
            for live in range(1, slots + 1):

                @pl.when(lens_ref[b] == live)
                def _():
                    query_block(b, live, shift)

    small = bound <= SAFE_SCORE * SAFE_SCORE

    @pl.when(small)
    def _():
        all_blocks(False)

    @pl.when(jnp.logical_not(small))
    def _():
        all_blocks(True)

    w_qg = jnp.concatenate([w_all_ref[:, :proj], w_all_ref[:, 3 * proj :]], axis=1)
    for c in range(together):
        att_t = jnp.concatenate([att_t_s[c, b] for b in range(blocks)], axis=1)
        d_query_t = jnp.concatenate([d_query_t_s[c, b] for b in range(blocks)], axis=1)
        gate_t = gate_t_s[c]
        gated_t = (gate_t * att_t).astype(BF16)
        d_gpre_t = (d_gated_t_s[c] * att_t * gate_t * (1.0 - gate_t)).astype(BF16)
        d_qg_t = jnp.concatenate([(d_query_t * scale).astype(BF16), d_gpre_t], axis=0)
        d_kv = d_kv_s[c].reshape(tokens, 2 * proj).astype(BF16)
        d_pair = dot(d_kv, w_all_t_ref[proj : 3 * proj, :]) + dot(w_qg, d_qg_t).T
        d_pair_ref[:, c] = d_pair.astype(BF16).reshape(pieces, tile_rows, chan)
        dw_qg_s[...] += dot(d_qg_t, x_ref[:, 0, c].reshape(tokens, chan))
        dw_kv_s[...] += dot(act_t_s[c], d_kv)
        dwo_s[...] += dot(gated_t, x_ref[:, 1, c].reshape(tokens, chan))

    if not last:
        return

    @pl.when(step == pl.num_programs(0) - 1)
    def _():
        weights = [dw_qg_s[:proj, :].T, dw_kv_s[:, :proj], dw_kv_s[:, proj:], dw_qg_s[proj:, :].T]
        weights.append(dwo_s[...])
        far, each = keep_out.shape[0], keep_out.shape[1]
        tile = each // (slots * heads)
        for n, w in enumerate(weights):
            d_w_out[n * chan : (n + 1) * chan, :] = w
            message_out[far * each + n * chan : far * each + (n + 1) * chan, :] = w.astype(BF16)
        for mine in range(inner):

            @pl.when(parity_ref[0] == mine)
            def _():
                for b in range(blocks):
                    for e in range(slots):
                        for h in range(heads):
                            turned = d_bias_s[b, e, h].T.astype(BF16)
                            at = (e * heads + h) * tile
                            for sub in range(size // tile):
                                col = b * (size // tile) + sub
                                piece = turned[sub * tile : (sub + 1) * tile]
                                if col % inner == mine:
                                    keep_out[col // inner, at : at + tile, :] = piece
                                else:
                                    start = (col // inner) * each + at
                                    message_out[start : start + tile, :] = piece


def attention(
    arrived, all_columns, bias, w_all, w_out, tables, lens, parity, carried, done, query_tile, inner
):
    count, _, columns, tile_rows, chan = arrived.shape
    blocks, slots = tables.shape
    heads = bias.shape[2]
    proj = w_out.shape[0]
    tokens = tile_rows * count
    size = tokens // blocks
    together = math.gcd(TOGETHER, columns)
    dims = (heads, proj // heads, blocks, size, slots, together, inner)
    first, last = done == 0, done + columns == all_columns
    far = tokens // query_tile // inner

    def whole(x):
        return pl.BlockSpec(
            x.shape, lambda j, *_: (0,) * len(x.shape), pipeline_mode=pl.Buffered(1)
        )

    sums = [
        ((blocks, slots, heads, size, size), F32),
        ((2 * proj, chan), F32),
        ((chan, 2 * proj), F32),
        ((proj, chan), F32),
    ]
    if last:
        each = slots * heads * query_tile
        results = [
            ((far, each, size), BF16),
            ((far * each + 5 * chan, size), BF16),
            ((5 * chan, proj), F32),
        ]
    else:
        results = sums
    results = [((count, all_columns, tile_rows, chan), BF16)] + results
    results = [jax.ShapeDtypeStruct(*x) for x in results]
    scratch = [
        ((together, chan, tokens), BF16),
        ((together, blocks, size, 2 * proj), BF16),
        ((together, blocks, 2 * proj, size), BF16),
        ((together, blocks, proj, heads * size), BF16),
        ((together, blocks, proj, heads * size), BF16),
        ((together, blocks, heads * size, proj), BF16),
        ((together, blocks, heads * size, proj), BF16),
        ((together, proj, tokens), F32),
        ((together, proj, tokens), F32),
        ((together, slots * size, heads * size), F32),
        ((together, slots * size, heads * size), F32),
        ((together, slots * size, heads * size), BF16),
        ((together, slots * size, heads * size), BF16),
        ((together, blocks, size, 2 * proj), F32),
        ((together, blocks, proj, size), F32),
        ((together, blocks, proj, size), F32),
    ]
    scratch = [pltpu.VMEM(*x) for x in (sums if last else []) + scratch]
    fixed = [bias, w_all, w_all.T, w_out]
    before = [] if first else list(carried)
    specs = [whole(x) for x in fixed]
    if before:
        specs += [pl.BlockSpec(memory_space=pl.ANY)] + [whole(x) for x in before[1:]]
    scalars = [tables, lens, parity]
    pairs = tokens * size * slots * heads
    return pl.pallas_call(
        functools.partial(attention_kernel, dims, first, last),
        grid_spec=pltpu.PrefetchScalarGridSpec(
            num_scalar_prefetch=len(scalars),
            grid=(columns // together,),
            in_specs=[
                pl.BlockSpec((count, 2, together, tile_rows, chan), lambda j, *_: (0, 0, j, 0, 0))
            ]
            + specs,
            out_specs=[
                pl.BlockSpec(
                    (count, together, tile_rows, chan),
                    lambda j, *_: (0, j + done // together, 0, 0),
                )
            ]
            + [whole(x) for x in results[1:]],
            scratch_shapes=scratch,
        ),
        out_shape=results,
        input_output_aliases={} if first else {len(scalars) + 1 + len(fixed): 0},
        compiler_params=pltpu.CompilerParams(vmem_limit_bytes=VMEM_LIMIT),
        cost_estimate=pl.CostEstimate(
            flops=columns * pairs * 1200,
            bytes_accessed=columns * tokens * chan * 6 + 10 * 2**20,
            transcendentals=columns * pairs,
        ),
    )(*scalars, arrived, *fixed, *before)


def small_call(body, scalars, arrays, results, scratch=()):
    return pl.pallas_call(
        body,
        in_specs=[pl.BlockSpec(memory_space=pltpu.SMEM)] * len(scalars)
        + [pl.BlockSpec(memory_space=pltpu.VMEM)] * len(arrays),
        out_specs=[pl.BlockSpec(memory_space=pltpu.VMEM)] * len(results),
        out_shape=[jax.ShapeDtypeStruct(*x) for x in results],
        scratch_shapes=list(scratch),
        compiler_params=pltpu.CompilerParams(vmem_limit_bytes=SMALL_LIMIT),
    )(*scalars, *arrays)


def aligned(index, count):
    return pl.ds(pl.multiple_of(index * count, count), count)


def split_by_far(targets, keep, came, weights):
    far, each, lanes = keep.shape
    share = weights.shape[0] // far

    def body(targets_ref, keep_ref, came_ref, weights_ref, own_ref, *message_refs):
        for s in range(far):
            t = targets_ref[s]
            out = message_refs[s - 1] if s else own_ref
            bias = keep_ref[t].astype(F32)
            weight = weights_ref[aligned(t, share), :].astype(BF16).astype(F32)
            if came_ref is not None:
                bias += came_ref[aligned(t, each), :].astype(F32)
                rest = came_ref[far * each :, :].astype(F32)
                half = jnp.zeros_like(weight)
                for u in range(far):
                    half = jnp.where(t == u, rest[u * share : (u + 1) * share], half)
                weight += half
            out[:each, :] = bias.astype(out.dtype)
            out[each:, :] = weight.astype(out.dtype)

    results = [((each + share, lanes), F32 if s == 0 else BF16) for s in range(far)]
    return small_call(body, [targets], [keep, came, weights], results)


def split_by_row(owners, chosen, live, own, came, dims):
    rows, slots, per_block, each = dims
    lanes = own.shape[1]
    part = each // slots
    share = own.shape[0] - each

    def body(owners_ref, chosen_ref, live_ref, own_ref, *refs):
        came_refs, outs = refs[: len(came)], refs[len(came) :]
        weight = own_ref[each:, :]
        for ref in came_refs:
            weight += ref[each:, :].astype(F32)
        for s in range(rows):
            outs[s][part:, :] = weight.astype(BF16).astype(outs[s].dtype)
            outs[s][:part, :] = jnp.zeros((part, lanes), outs[s].dtype)
        for e in range(slots):
            at = slice(e * part, (e + 1) * part)
            bias = own_ref[at, :]
            for ref in came_refs:
                bias += ref[at, :].astype(F32)
            for s in range(rows):
                hit = (chosen_ref[e] == owners_ref[s] // per_block) & (e < live_ref[0])

                @pl.when(hit)
                def _():
                    outs[s][:part, :] = bias.astype(outs[s].dtype)

    results = [((part + share, lanes), F32 if s == 0 else BF16) for s in range(rows)]
    return small_call(body, [owners, chosen, live], [own, *came], results)


def add_rows(own, came, part):
    share, lanes = own.shape[0] - part, own.shape[1]

    def body(own_ref, *refs):
        came_refs, (bias_ref, weight_ref) = refs[: len(came)], refs[len(came) :]
        terms = [own_ref[...]] + [ref[...].astype(F32) for ref in came_refs]
        while len(terms) > 1:
            terms = [sum(terms[n : n + 2]) for n in range(0, len(terms), 2)]
        total = terms[0]
        bias_ref[...] = total[:part]
        weight_ref[...] = total[part:].astype(BF16)

    results = [((part, lanes), F32), ((share, lanes), BF16)]
    return small_call(body, [], [own, *came], results)


def place_weights(sources, parts, count):
    share, lanes = parts[0].shape

    def body(sources_ref, *refs):
        part_refs, out_refs, scratch = refs[: len(parts)], refs[len(parts) : -1], refs[-1]
        for s, ref in enumerate(part_refs):
            scratch[aligned(sources_ref[s], share), :] = ref[...].astype(F32)
        for n, ref in enumerate(out_refs):
            ref[...] = scratch[n * lanes : (n + 1) * lanes, :]

    rows = share * len(parts)
    results = [((rows // count, lanes), F32)] * count
    return small_call(body, [sources], parts, results, [pltpu.VMEM((rows, lanes), F32)])


class Peers:
    def __init__(self, axis, stride, count):
        self.axis, self.count = axis, count
        self.paired = count & (count - 1) == 0
        place = lax.axis_index(axis)
        self.digit = place // stride % count
        everyone = range(lax.axis_size(axis))
        self.routes = []
        for s in range(count):
            route = []
            for p in everyone:
                d = p // stride % count
                route.append((p, p + (self.step(d, s) - d) * stride))
            self.routes.append(route)

    def step(self, digit, s):
        return digit ^ s if self.paired else (digit + s) % self.count

    def target(self, s):
        return self.step(self.digit, s)

    def source(self, s):
        return self.target(s) if self.paired else (self.digit - s) % self.count

    def send(self, x, s):
        return x if s == 0 else lax.ppermute(x, self.axis, self.routes[s])

    def positions(self):
        digits = jnp.arange(self.count)
        return self.digit ^ digits if self.paired else (self.digit - digits) % self.count

    def gather(self, x):
        return jnp.stack([self.send(x, s) for s in range(self.count)])

    def targets(self):
        return jnp.stack([self.target(s) for s in range(self.count)]).astype(jnp.int32)

    def sources(self):
        return jnp.stack([self.source(s) for s in range(self.count)]).astype(jnp.int32)

    def swap(self, messages):
        return [self.send(x, s + 1) for s, x in enumerate(messages)]


def on_device(
    pair_act, out_grad, tri_bias, w_query, w_key, w_value, w_gate, w_out, key_blocks, list_len
):
    row_count = lax.axis_size("row")
    col_count = lax.axis_size("col")
    tile_rows, tile_cols, chan = pair_act.shape
    heads = tri_bias.shape[0]
    query_tile = tri_bias.shape[2]
    proj = w_query.shape[1]
    blocks, slots = key_blocks.shape
    tokens = tile_rows * row_count
    size = tokens // blocks
    col_width = tile_cols // row_count
    chunks = math.gcd(CHUNKS, col_width)
    width = col_width // chunks
    inner = math.gcd(2, col_count)
    rows = Peers("row", 1, row_count)
    near = Peers("col", 1, inner)
    far = Peers("col", inner, col_count // inner)

    gathered = far.gather(rows.gather(jnp.transpose(tri_bias, (0, 2, 1))))
    gathered = near.gather(gathered).reshape((col_count,) + (row_count, heads, query_tile, tile_rows))
    columns = jnp.arange(col_count)
    col_pos = near.positions()[columns % inner] * far.count + far.positions()[columns // inner]
    bias = shifted_bias(
        gathered,
        key_blocks,
        list_len,
        col_pos.astype(jnp.int32),
        rows.positions().astype(jnp.int32),
    )

    parity = near.targets()[:1]
    w_all = jnp.concatenate([w_query, w_key, w_value, w_gate], axis=1)

    by_owner = lambda x: jnp.transpose(x, (1, 0, 2)).reshape(
        row_count, chunks, width, tile_rows, chan
    )
    acts, grads = by_owner(pair_act), by_owner(out_grad)
    carried = None
    for c in range(chunks):
        arrived = lax.all_to_all(
            jnp.stack([acts[:, c], grads[:, c]], axis=1), "row", 0, 0, tiled=True
        )
        carried = attention(
            arrived, col_width, bias, w_all, w_out, key_blocks, list_len, parity, carried,
            c * width, query_tile, inner,
        )
    d_pair, keep, message, w_part = carried
    d_pair = lax.all_to_all(d_pair, "row", 0, 0, tiled=True)
    d_pair = jnp.transpose(d_pair, (2, 0, 1, 3)).reshape(tile_rows, tile_cols, chan)
    far_targets, row_targets = far.targets(), rows.targets()

    each = keep.shape[1]
    own, *messages = split_by_far(far_targets, keep, near.send(message, inner - 1), w_part)
    came = far.swap(messages)
    block = lax.axis_index("col") * query_tile // size
    chosen = lax.dynamic_index_in_dim(key_blocks, block, 0, keepdims=False)
    live = lax.dynamic_slice_in_dim(list_len, block, 1)
    per_block = size // tile_rows
    own, *messages = split_by_row(
        row_targets, chosen, live, own, came, (row_count, slots, per_block, each)
    )
    d_bias, w_part = add_rows(own, rows.swap(messages), each // slots)
    weights = place_weights(far.sources(), [far.send(w_part, s) for s in range(far.count)], 5)
    d_bias = d_bias.reshape(heads, query_tile, per_block, tile_rows)
    d_bias = lax.dynamic_index_in_dim(d_bias, rows.digit % per_block, 2, keepdims=False)

    return (d_pair, jnp.transpose(d_bias, (0, 2, 1)), *weights)


def solution(mesh):
    in_specs = (
        P("row", "col", None),
        P("row", "col", None),
        P(None, "row", "col"),
        P(),
        P(),
        P(),
        P(),
        P(),
        P(),
        P(),
    )
    out_specs = (P("row", "col", None), P(None, "row", "col"), P(), P(), P(), P(), P())
    return jax.shard_map(
        on_device, mesh=mesh, in_specs=in_specs, out_specs=out_specs, check_vma=False
    )
```

```python
import functools
import math

import jax
import jax.numpy as jnp
from jax import lax
from jax.experimental import pallas as pl
from jax.experimental.pallas import tpu as pltpu
from jax.sharding import PartitionSpec as P

F32 = jnp.float32
BF16 = jnp.bfloat16
CHUNKS = 2
TOGETHER = 4
STRIP = 32
LOG2E = math.log2(math.e)
SAFE_SCORE = 30.0
VMEM_LIMIT = 56 * 1024 * 1024
SMALL_LIMIT = 16 * 1024 * 1024


def dot(a, b):
    return jnp.dot(a, b, preferred_element_type=F32)


def bias_kernel(tables_ref, lens_ref, col_pos_ref, row_pos_ref, *refs):
    *parts, out_ref = refs
    b = pl.program_id(0)
    blocks, _, heads, size, _ = out_ref.shape
    slots = tables_ref.shape[1]
    rows, _, _, tile = parts[0].shape[1:]
    per_block = size // tile
    for h in range(heads):
        for r in range(rows):
            piece = jnp.concatenate([p[0, row_pos_ref[r], h] for p in parts], axis=0)
            at = (r % per_block) * tile
            out_ref[r // per_block, 0, h, at : at + tile, :] = piece.astype(F32).T
    for h in range(heads):
        peak = jnp.max(out_ref[tables_ref[b, 0], 0, h], axis=0, keepdims=True)
        for e in range(1, slots):
            other = jnp.max(out_ref[tables_ref[b, e], 0, h], axis=0, keepdims=True)
            peak = jnp.where(e < lens_ref[b], jnp.maximum(peak, other), peak)
        for kb in range(blocks):
            out_ref[kb, 0, h] = (out_ref[kb, 0, h] - peak) * LOG2E


def shifted_bias(gathered, key_blocks, list_len, col_pos, row_pos):
    cols, rows, heads, query_tile, key_tile = gathered.shape
    blocks = key_blocks.shape[0]
    size = cols * query_tile // blocks
    per_block = size // query_tile

    def part(sub):
        return pl.BlockSpec(
            (1, rows, heads, query_tile, key_tile),
            lambda b, tables, lens, col_at, row_at: (col_at[b * per_block + sub], 0, 0, 0, 0),
        )

    return pl.pallas_call(
        bias_kernel,
        grid_spec=pltpu.PrefetchScalarGridSpec(
            num_scalar_prefetch=4,
            grid=(blocks,),
            in_specs=[part(sub) for sub in range(per_block)],
            out_specs=pl.BlockSpec((blocks, 1, heads, size, size), lambda b, *_: (0, b, 0, 0, 0)),
        ),
        out_shape=jax.ShapeDtypeStruct((blocks, blocks, heads, size, size), F32),
        compiler_params=pltpu.CompilerParams(vmem_limit_bytes=VMEM_LIMIT),
    )(key_blocks, list_len, col_pos, row_pos, *([gathered] * per_block))


def attention_kernel(dims, first, last, tables_ref, lens_ref, parity_ref, owners_ref, *refs):
    pieces, heads, head_dim, blocks, size, slots, together, inner = dims
    refs = list(refs)
    take = lambda n: [refs.pop(0) for _ in range(n)]
    inputs = take(pieces)
    bias_ref, w_all_ref, w_all_t_ref, w_out_ref = take(4)
    carried = [] if first else take(4)
    d_pair_out = take(pieces)
    if last:
        keep_out, message_out, d_w_out = take(3)
    d_bias_s, dw_qg_s, dw_kv_s, dwo_s = sums = take(4)
    (act_s, grad_s, d_pair_s, act_t_s, kv_s, kv_t_s, w_score_s, w_probs_s, d_att_s, query_s, gate_t_s, d_gated_t_s,
     score_s, d_probs_s, probs_s, ds_s, d_kv_s, att_t_s, d_query_t_s) = refs
    proj = heads * head_dim
    scale = head_dim ** (-0.5)
    tile_rows, chan = inputs[0].shape[2:]
    tokens = blocks * size
    step = pl.program_id(0)
    span = [slice(b * size, (b + 1) * size) for b in range(blocks)]
    own = [slice(h * head_dim, (h + 1) * head_dim) for h in range(heads)]
    pair = math.gcd(2, heads)
    head_lanes = [slice(h * size, (h + 1) * size) for h in range(heads)]

    @pl.when(step == 0)
    def _():
        w_score_s[...] = jnp.zeros_like(w_score_s)
        w_probs_s[...] = jnp.zeros_like(w_probs_s)
        for n, ref in enumerate(sums):
            ref[...] = jnp.zeros_like(ref) if first else carried[n][...]

    lane_head = lax.broadcasted_iota(jnp.int32, (size, proj), 1) // head_dim
    bound = jnp.float32(0.0)
    for c in range(together):
        for s in range(pieces):
            rows = aligned(owners_ref[s], tile_rows)
            act_s[c, rows, :] = inputs[s][0, c]
            grad_s[c, rows, :] = inputs[s][1, c]
        acts = act_s[c]
        grads = grad_s[c]
        acts_t = acts.T
        act_t_s[c] = acts_t
        natural = dot(acts, w_all_ref[:, : 3 * proj])
        across = dot(w_all_t_ref[...], acts_t)
        queries_t = (across[:proj] * scale).astype(BF16)
        kv_t = across[proj : 3 * proj].astype(BF16)
        gate_t = 1.0 / (1.0 + jnp.exp(-across[3 * proj :]))
        d_gated_t = dot(w_out_ref[...], grads.T)
        d_att_t = (d_gated_t * gate_t).astype(BF16)
        gate_t_s[c] = gate_t
        d_gated_t_s[c] = d_gated_t
        squares = lambda x: jnp.max(
            jnp.sum(jnp.square(x.astype(F32)).reshape(heads, head_dim, -1), axis=1)
        )
        bound = jnp.maximum(bound, squares(queries_t) * squares(kv_t[:proj]))
        queries = (natural[:, :proj] * scale).astype(BF16)
        kv = natural[:, proj:].astype(BF16)
        zero = jnp.zeros((size, proj), BF16)
        for b in range(blocks):
            kv_s[c, b] = kv[span[b]]
            kv_t_s[c, b] = kv_t[:, span[b]]
            d_att = d_att_t[:, span[b]].T
            for h in range(heads):
                w_score_s[c, b, own[h], head_lanes[h]] = queries_t[own[h], span[b]]
                w_probs_s[c, b, own[h], head_lanes[h]] = d_att_t[own[h], span[b]]
                here = lane_head == h
                query_s[c, b, h * size : (h + 1) * size, :] = jnp.where(here, queries[span[b]], zero)
                d_att_s[c, b, h * size : (h + 1) * size, :] = jnp.where(here, d_att, zero)
    d_kv_s[...] = jnp.zeros_like(d_kv_s)

    def query_block(b, live, shift):
        chosen = [tables_ref[b, e] for e in range(live)]
        strips = [
            (e, e * size + at, at) for e in range(live) for at in range(0, size, STRIP)
        ]
        rows_of = lambda x: jnp.sum(x.reshape(-1, 8, size), axis=0)
        for c in range(together):
            kv = jnp.concatenate([kv_s[c, k] for k in chosen], axis=0)
            score_s[c, : live * size, :] = dot(kv[:, :proj], w_score_s[c, b])
            d_probs_s[c, : live * size, :] = dot(kv[:, proj:], w_probs_s[c, b])
        for h in range(heads):
            lanes = head_lanes[h]
            stats = []
            for c in range(together):

                def scores(e, row, at):
                    return (
                        score_s[c, row : row + STRIP, lanes] * LOG2E
                        + bias_ref[chosen[e], b, h, at : at + STRIP, :]
                    )

                if shift:
                    peak = jnp.full((8, size), -jnp.inf, F32)
                    for strip in strips:
                        peak = jnp.maximum(
                            peak, jnp.max(scores(*strip).reshape(-1, 8, size), axis=0)
                        )
                    peak = jnp.max(peak, axis=0, keepdims=True)
                total = jnp.zeros((8, size), F32)
                mixed = jnp.zeros((8, size), F32)
                for e, row, at in strips:
                    value = scores(e, row, at)
                    weight = jnp.exp2(value - peak if shift else value)
                    total += rows_of(weight)
                    mixed += rows_of(weight * d_probs_s[c, row : row + STRIP, lanes])
                    score_s[c, row : row + STRIP, lanes] = weight
                norm = 1.0 / jnp.sum(total, axis=0, keepdims=True)
                stats.append((norm, jnp.sum(mixed, axis=0, keepdims=True) * norm))
            for e, row, at in strips:
                part = slice(row, row + STRIP)
                gathered = d_bias_s[b, e, h, at : at + STRIP, :]
                for c, (norm, delta) in enumerate(stats):
                    probs = score_s[c, part, lanes] * norm
                    d_scores = probs * (d_probs_s[c, part, lanes] - delta)
                    probs_s[c, part, lanes] = probs.astype(BF16)
                    ds_s[c, part, lanes] = d_scores.astype(BF16)
                    gathered += d_scores
                d_bias_s[b, e, h, at : at + STRIP, :] = gathered
        for c in range(together):
            kv_t = jnp.concatenate([kv_t_s[c, k] for k in chosen], axis=1)
            for h in range(0, heads, pair):
                lanes = slice(h * size, (h + pair) * size)
                both = slice(h * head_dim, (h + pair) * head_dim)
                low = slice(proj + both.start, proj + both.stop)
                att_t = dot(kv_t[low], probs_s[c, : live * size, lanes])
                d_query_t = dot(kv_t[both], ds_s[c, : live * size, lanes])
                for n in range(pair):
                    att_t_s[c, b, own[h + n], :] = att_t[own[n], head_lanes[n]]
                    d_query_t_s[c, b, own[h + n], :] = d_query_t[own[n], head_lanes[n]]
            d_values = dot(probs_s[c, : live * size, :], d_att_s[c, b])
            d_keys = dot(ds_s[c, : live * size, :], query_s[c, b])
            for e in range(live):
                part = slice(e * size, (e + 1) * size)
                d_kv_s[c, chosen[e], :, :proj] += d_keys[part]
                d_kv_s[c, chosen[e], :, proj:] += d_values[part]

    def all_blocks(shift):
        @pl.loop(0, blocks)
        def _(b):
            for live in range(1, slots + 1):

                @pl.when(lens_ref[b] == live)
                def _():
                    query_block(b, live, shift)

    small = bound <= SAFE_SCORE * SAFE_SCORE

    @pl.when(small)
    def _():
        all_blocks(False)

    @pl.when(jnp.logical_not(small))
    def _():
        all_blocks(True)

    w_qg = jnp.concatenate([w_all_ref[:, :proj], w_all_ref[:, 3 * proj :]], axis=1)
    for c in range(together):
        att_t = jnp.concatenate([att_t_s[c, b] for b in range(blocks)], axis=1)
        d_query_t = jnp.concatenate([d_query_t_s[c, b] for b in range(blocks)], axis=1)
        gate_t = gate_t_s[c]
        gated_t = (gate_t * att_t).astype(BF16)
        d_gpre_t = (d_gated_t_s[c] * att_t * gate_t * (1.0 - gate_t)).astype(BF16)
        d_qg_t = jnp.concatenate([(d_query_t * scale).astype(BF16), d_gpre_t], axis=0)
        d_kv = d_kv_s[c].reshape(tokens, 2 * proj).astype(BF16)
        d_pair = dot(d_kv, w_all_t_ref[proj : 3 * proj, :]) + dot(w_qg, d_qg_t).T
        d_pair_s[c] = d_pair
        for s in range(pieces):
            d_pair_out[s][c] = d_pair_s[c, aligned(owners_ref[s], tile_rows), :].astype(BF16)
        dw_qg_s[...] += dot(d_qg_t, act_s[c])
        dw_kv_s[...] += dot(act_t_s[c], d_kv)
        dwo_s[...] += dot(gated_t, grad_s[c])

    if not last:
        return

    @pl.when(step == pl.num_programs(0) - 1)
    def _():
        weights = [dw_qg_s[:proj, :].T, dw_kv_s[:, :proj], dw_kv_s[:, proj:], dw_qg_s[proj:, :].T]
        weights.append(dwo_s[...])
        far, each = keep_out.shape[0], keep_out.shape[1]
        tile = each // (slots * heads)
        for n, w in enumerate(weights):
            d_w_out[n * chan : (n + 1) * chan, :] = w
            message_out[far * each + n * chan : far * each + (n + 1) * chan, :] = w.astype(BF16)
        for mine in range(inner):

            @pl.when(parity_ref[0] == mine)
            def _():
                for b in range(blocks):
                    for e in range(slots):
                        for h in range(heads):
                            turned = d_bias_s[b, e, h].T.astype(BF16)
                            at = (e * heads + h) * tile
                            for sub in range(size // tile):
                                col = b * (size // tile) + sub
                                piece = turned[sub * tile : (sub + 1) * tile]
                                if col % inner == mine:
                                    keep_out[col // inner, at : at + tile, :] = piece
                                else:
                                    start = (col // inner) * each + at
                                    message_out[start : start + tile, :] = piece


def attention(
    pieces, bias, w_all, w_out, tables, lens, parity, owners, carried, last, query_tile, inner
):
    count = len(pieces)
    _, columns, tile_rows, chan = pieces[0].shape
    blocks, slots = tables.shape
    heads = bias.shape[2]
    proj = w_out.shape[0]
    tokens = tile_rows * count
    size = tokens // blocks
    together = math.gcd(TOGETHER, columns)
    dims = (count, heads, proj // heads, blocks, size, slots, together, inner)
    first = carried is None
    far = tokens // query_tile // inner

    def whole(x):
        return pl.BlockSpec(
            x.shape, lambda j, *_: (0,) * len(x.shape), pipeline_mode=pl.Buffered(1)
        )

    sums = [
        ((blocks, slots, heads, size, size), F32),
        ((2 * proj, chan), F32),
        ((chan, 2 * proj), F32),
        ((proj, chan), F32),
    ]
    if last:
        each = slots * heads * query_tile
        results = [
            ((far, each, size), BF16),
            ((far * each + 5 * chan, size), BF16),
            ((5 * chan, proj), F32),
        ]
    else:
        results = sums
    results = [((columns, tile_rows, chan), BF16)] * count + results
    results = [jax.ShapeDtypeStruct(*x) for x in results]
    scratch = [
        ((together, tokens, chan), BF16),
        ((together, tokens, chan), BF16),
        ((together, tokens, chan), F32),
        ((together, chan, tokens), BF16),
        ((together, blocks, size, 2 * proj), BF16),
        ((together, blocks, 2 * proj, size), BF16),
        ((together, blocks, proj, heads * size), BF16),
        ((together, blocks, proj, heads * size), BF16),
        ((together, blocks, heads * size, proj), BF16),
        ((together, blocks, heads * size, proj), BF16),
        ((together, proj, tokens), F32),
        ((together, proj, tokens), F32),
        ((together, slots * size, heads * size), F32),
        ((together, slots * size, heads * size), F32),
        ((together, slots * size, heads * size), BF16),
        ((together, slots * size, heads * size), BF16),
        ((together, blocks, size, 2 * proj), F32),
        ((together, blocks, proj, size), F32),
        ((together, blocks, proj, size), F32),
    ]
    scratch = [pltpu.VMEM(*x) for x in (sums if last else []) + scratch]
    fixed = [bias, w_all, w_all.T, w_out] + ([] if first else list(carried))
    scalars = [tables, lens, parity, owners]
    pairs = tokens * size * slots * heads
    outs = pl.pallas_call(
        functools.partial(attention_kernel, dims, first, last),
        grid_spec=pltpu.PrefetchScalarGridSpec(
            num_scalar_prefetch=len(scalars),
            grid=(columns // together,),
            in_specs=[
                pl.BlockSpec((2, together, tile_rows, chan), lambda j, *_: (0, j, 0, 0))
            ] * count
            + [whole(x) for x in fixed],
            out_specs=[pl.BlockSpec((together, tile_rows, chan), lambda j, *_: (j, 0, 0))] * count
            + [whole(x) for x in results[count:]],
            scratch_shapes=scratch,
        ),
        out_shape=results,
        compiler_params=pltpu.CompilerParams(vmem_limit_bytes=VMEM_LIMIT),
        cost_estimate=pl.CostEstimate(
            flops=columns * pairs * 7000,
            bytes_accessed=columns * tokens * chan * 6 + 10 * 2**20,
            transcendentals=columns * pairs,
        ),
    )(*scalars, *pieces, *fixed)
    return outs[:count], outs[count:]


def small_call(body, scalars, arrays, results, scratch=()):
    return pl.pallas_call(
        body,
        in_specs=[pl.BlockSpec(memory_space=pltpu.SMEM)] * len(scalars)
        + [pl.BlockSpec(memory_space=pltpu.VMEM)] * len(arrays),
        out_specs=[pl.BlockSpec(memory_space=pltpu.VMEM)] * len(results),
        out_shape=[jax.ShapeDtypeStruct(*x) for x in results],
        scratch_shapes=list(scratch),
        compiler_params=pltpu.CompilerParams(vmem_limit_bytes=SMALL_LIMIT),
    )(*scalars, *arrays)


def aligned(index, count):
    return pl.ds(pl.multiple_of(index * count, count), count)


def split_by_far(targets, keep, came, weights):
    far, each, lanes = keep.shape
    share = weights.shape[0] // far

    def body(targets_ref, keep_ref, came_ref, weights_ref, own_ref, *message_refs):
        for s in range(far):
            t = targets_ref[s]
            out = message_refs[s - 1] if s else own_ref
            bias = keep_ref[t].astype(F32)
            weight = weights_ref[aligned(t, share), :].astype(BF16).astype(F32)
            if came_ref is not None:
                bias += came_ref[aligned(t, each), :].astype(F32)
                rest = came_ref[far * each :, :].astype(F32)
                half = jnp.zeros_like(weight)
                for u in range(far):
                    half = jnp.where(t == u, rest[u * share : (u + 1) * share], half)
                weight += half
            out[:each, :] = bias.astype(out.dtype)
            out[each:, :] = weight.astype(out.dtype)

    results = [((each + share, lanes), F32 if s == 0 else BF16) for s in range(far)]
    return small_call(body, [targets], [keep, came, weights], results)


def split_by_row(owners, chosen, live, own, came, dims):
    rows, slots, per_block, each = dims
    lanes = own.shape[1]
    part = each // slots
    share = own.shape[0] - each

    def body(owners_ref, chosen_ref, live_ref, own_ref, *refs):
        came_refs, outs = refs[: len(came)], refs[len(came) :]
        weight = own_ref[each:, :]
        for ref in came_refs:
            weight += ref[each:, :].astype(F32)
        for s in range(rows):
            outs[s][part:, :] = weight.astype(BF16).astype(outs[s].dtype)
            outs[s][:part, :] = jnp.zeros((part, lanes), outs[s].dtype)
        for e in range(slots):
            at = slice(e * part, (e + 1) * part)
            bias = own_ref[at, :]
            for ref in came_refs:
                bias += ref[at, :].astype(F32)
            for s in range(rows):
                hit = (chosen_ref[e] == owners_ref[s] // per_block) & (e < live_ref[0])

                @pl.when(hit)
                def _():
                    outs[s][:part, :] = bias.astype(outs[s].dtype)

    results = [((part + share, lanes), F32 if s == 0 else BF16) for s in range(rows)]
    return small_call(body, [owners, chosen, live], [own, *came], results)


def add_rows(own, came, part):
    share, lanes = own.shape[0] - part, own.shape[1]

    def body(own_ref, *refs):
        came_refs, (bias_ref, weight_ref) = refs[: len(came)], refs[len(came) :]
        terms = [own_ref[...]] + [ref[...].astype(F32) for ref in came_refs]
        while len(terms) > 1:
            terms = [sum(terms[n : n + 2]) for n in range(0, len(terms), 2)]
        total = terms[0]
        bias_ref[...] = total[:part]
        weight_ref[...] = total[part:].astype(BF16)

    results = [((part, lanes), F32), ((share, lanes), BF16)]
    return small_call(body, [], [own, *came], results)


def place_weights(sources, parts, count):
    share, lanes = parts[0].shape

    def body(sources_ref, *refs):
        part_refs, out_refs, scratch = refs[: len(parts)], refs[len(parts) : -1], refs[-1]
        for s, ref in enumerate(part_refs):
            scratch[aligned(sources_ref[s], share), :] = ref[...].astype(F32)
        for n, ref in enumerate(out_refs):
            ref[...] = scratch[n * lanes : (n + 1) * lanes, :]

    rows = share * len(parts)
    results = [((rows // count, lanes), F32)] * count
    return small_call(body, [sources], parts, results, [pltpu.VMEM((rows, lanes), F32)])


class Peers:
    def __init__(self, axis, stride, count):
        self.axis, self.count = axis, count
        self.paired = count & (count - 1) == 0
        place = lax.axis_index(axis)
        self.digit = place // stride % count
        everyone = range(lax.axis_size(axis))
        self.routes = []
        for s in range(count):
            route = []
            for p in everyone:
                d = p // stride % count
                route.append((p, p + (self.step(d, s) - d) * stride))
            self.routes.append(route)

    def step(self, digit, s):
        return digit ^ s if self.paired else (digit + s) % self.count

    def target(self, s):
        return self.step(self.digit, s)

    def source(self, s):
        return self.target(s) if self.paired else (self.digit - s) % self.count

    def send(self, x, s, home=False):
        route = self.routes[s]
        if home:
            route = [(t, f) for f, t in route]
        return x if s == 0 else lax.ppermute(x, self.axis, route)

    def steps(self):
        digits = jnp.arange(self.count)
        return self.digit ^ digits if self.paired else (digits - self.digit) % self.count

    def positions(self):
        digits = jnp.arange(self.count)
        return self.digit ^ digits if self.paired else (self.digit - digits) % self.count

    def gather(self, x):
        return jnp.stack([self.send(x, s) for s in range(self.count)])

    def targets(self):
        return jnp.stack([self.target(s) for s in range(self.count)]).astype(jnp.int32)

    def sources(self):
        return jnp.stack([self.source(s) for s in range(self.count)]).astype(jnp.int32)

    def swap(self, messages):
        return [self.send(x, s + 1) for s, x in enumerate(messages)]


def on_device(
    pair_act, out_grad, tri_bias, w_query, w_key, w_value, w_gate, w_out, key_blocks, list_len
):
    row_count = lax.axis_size("row")
    col_count = lax.axis_size("col")
    tile_rows, tile_cols, chan = pair_act.shape
    heads = tri_bias.shape[0]
    query_tile = tri_bias.shape[2]
    proj = w_query.shape[1]
    blocks, slots = key_blocks.shape
    tokens = tile_rows * row_count
    size = tokens // blocks
    col_width = tile_cols // row_count
    chunks = math.gcd(CHUNKS, col_width)
    width = col_width // chunks
    inner = math.gcd(2, col_count)
    rows = Peers("row", 1, row_count)
    near = Peers("col", 1, inner)
    far = Peers("col", inner, col_count // inner)

    gathered = rows.gather(jnp.transpose(tri_bias, (0, 2, 1)))
    gathered, pair_act, out_grad = lax.optimization_barrier((gathered, pair_act, out_grad))
    both = jnp.stack([pair_act, out_grad]).reshape(2, tile_rows, row_count, chunks, width, chan)
    both = jnp.transpose(both, (2, 3, 0, 4, 1, 5))
    owners = rows.sources()
    outgoing = [
        [
            lax.dynamic_index_in_dim(both[:, c], rows.target(s), 0, keepdims=False)
            for s in range(row_count)
        ]
        for c in range(chunks)
    ]
    gathered, outgoing = lax.optimization_barrier((far.gather(gathered), outgoing))
    gathered = near.gather(gathered)
    gathered = gathered.reshape((col_count, row_count, heads, query_tile, tile_rows))
    columns = jnp.arange(col_count)
    col_pos = near.positions()[columns % inner] * far.count + far.positions()[columns // inner]
    bias = shifted_bias(
        gathered,
        key_blocks,
        list_len,
        col_pos.astype(jnp.int32),
        rows.positions().astype(jnp.int32),
    )

    parity = near.targets()[:1]
    w_all = jnp.concatenate([w_query, w_key, w_value, w_gate], axis=1)
    arrived = [[rows.send(x, s) for s, x in enumerate(part)] for part in outgoing]
    carried = None
    returned = []
    for c in range(chunks):
        d_pieces, carried = attention(
            arrived[c], bias, w_all, w_out, key_blocks, list_len, parity, owners, carried,
            c == chunks - 1, query_tile, inner,
        )
        if c < chunks - 1:
            d_pieces = [rows.send(x, s, home=True) for s, x in enumerate(d_pieces)]
        returned.append(d_pieces)
    keep, message, w_part = carried
    message, returned[:-1] = lax.optimization_barrier((message, returned[:-1]))
    far_targets, row_targets = far.targets(), rows.targets()

    each = keep.shape[1]
    own, *messages = split_by_far(far_targets, keep, near.send(message, inner - 1), w_part)
    messages, returned[-1] = lax.optimization_barrier((messages, returned[-1]))
    came = far.swap(messages)
    returned[-1] = [rows.send(x, s, home=True) for s, x in enumerate(returned[-1])]
    block = lax.axis_index("col") * query_tile // size
    chosen = lax.dynamic_index_in_dim(key_blocks, block, 0, keepdims=False)
    live = lax.dynamic_slice_in_dim(list_len, block, 1)
    per_block = size // tile_rows
    own, *messages = split_by_row(
        row_targets, chosen, live, own, came, (row_count, slots, per_block, each)
    )
    d_bias, w_part = add_rows(own, rows.swap(messages), each // slots)
    weights = place_weights(far.sources(), [far.send(w_part, s) for s in range(far.count)], 5)
    d_bias = d_bias.reshape(heads, query_tile, per_block, tile_rows)
    d_bias = lax.dynamic_index_in_dim(d_bias, rows.digit % per_block, 2, keepdims=False)


    by_step = [jnp.stack([part[s] for part in returned]) for s in range(row_count)]
    d_pair = jnp.stack(by_step)
    d_pair = jnp.take(d_pair, rows.steps(), axis=0)
    d_pair = jnp.transpose(d_pair, (3, 0, 1, 2, 4)).reshape(tile_rows, tile_cols, chan)
    return (d_pair, jnp.transpose(d_bias, (0, 2, 1)), *weights)


def solution(mesh):
    in_specs = (
        P("row", "col", None),
        P("row", "col", None),
        P(None, "row", "col"),
        P(),
        P(),
        P(),
        P(),
        P(),
        P(),
        P(),
    )
    out_specs = (P("row", "col", None), P(None, "row", "col"), P(), P(), P(), P(), P())
    return jax.shard_map(
        on_device, mesh=mesh, in_specs=in_specs, out_specs=out_specs, check_vma=False
    )
```

```python
import functools
import math

import jax
import jax.numpy as jnp
from jax import lax
from jax.experimental import pallas as pl
from jax.experimental.pallas import tpu as pltpu
from jax.sharding import PartitionSpec as P

F32 = jnp.float32
BF16 = jnp.bfloat16
CHUNKS = 2
TOGETHER = 2
STRIP = 32
LOG2E = math.log2(math.e)
SAFE_SCORE = 30.0
VMEM_LIMIT = 56 * 1024 * 1024
SMALL_LIMIT = 16 * 1024 * 1024


def dot(a, b):
    return jnp.dot(a, b, preferred_element_type=F32)


def bias_kernel(tables_ref, lens_ref, col_pos_ref, row_pos_ref, *refs):
    *parts, out_ref = refs
    b = pl.program_id(0)
    blocks, _, heads, size, _ = out_ref.shape
    slots = tables_ref.shape[1]
    rows, _, _, tile = parts[0].shape[1:]
    per_block = size // tile
    for h in range(heads):
        for r in range(rows):
            piece = jnp.concatenate([p[0, row_pos_ref[r], h] for p in parts], axis=0)
            at = (r % per_block) * tile
            out_ref[r // per_block, 0, h, at : at + tile, :] = piece.astype(F32).T
    for h in range(heads):
        peak = jnp.max(out_ref[tables_ref[b, 0], 0, h], axis=0, keepdims=True)
        for e in range(1, slots):
            other = jnp.max(out_ref[tables_ref[b, e], 0, h], axis=0, keepdims=True)
            peak = jnp.where(e < lens_ref[b], jnp.maximum(peak, other), peak)
        for kb in range(blocks):
            out_ref[kb, 0, h] = (out_ref[kb, 0, h] - peak) * LOG2E


def shifted_bias(gathered, key_blocks, list_len, col_pos, row_pos):
    cols, rows, heads, query_tile, key_tile = gathered.shape
    blocks = key_blocks.shape[0]
    size = cols * query_tile // blocks
    per_block = size // query_tile

    def part(sub):
        return pl.BlockSpec(
            (1, rows, heads, query_tile, key_tile),
            lambda b, tables, lens, col_at, row_at: (col_at[b * per_block + sub], 0, 0, 0, 0),
        )

    return pl.pallas_call(
        bias_kernel,
        grid_spec=pltpu.PrefetchScalarGridSpec(
            num_scalar_prefetch=4,
            grid=(blocks,),
            in_specs=[part(sub) for sub in range(per_block)],
            out_specs=pl.BlockSpec((blocks, 1, heads, size, size), lambda b, *_: (0, b, 0, 0, 0)),
        ),
        out_shape=jax.ShapeDtypeStruct((blocks, blocks, heads, size, size), F32),
        compiler_params=pltpu.CompilerParams(vmem_limit_bytes=VMEM_LIMIT),
    )(key_blocks, list_len, col_pos, row_pos, *([gathered] * per_block))


def attention_kernel(dims, first, last, tables_ref, lens_ref, parity_ref, owners_ref, *refs):
    pieces, heads, head_dim, blocks, size, slots, together, inner = dims
    refs = list(refs)
    take = lambda n: [refs.pop(0) for _ in range(n)]
    inputs = take(pieces)
    bias_ref, w_all_ref, w_all_t_ref, w_out_ref = take(4)
    carried = [] if first else take(4)
    d_pair_out = take(pieces)
    if last:
        keep_out, message_out, d_w_out = take(3)
    d_bias_s, dw_qg_s, dw_kv_s, dwo_s = sums = take(4)
    (act_s, grad_s, d_pair_s, act_t_s, kv_s, kv_t_s, w_score_s, w_probs_s, d_att_s, query_s, gate_t_s, d_gated_t_s,
     score_s, d_probs_s, probs_s, ds_s, d_kv_s, att_t_s, d_query_t_s) = refs
    proj = heads * head_dim
    scale = head_dim ** (-0.5)
    tile_rows, chan = inputs[0].shape[2:]
    tokens = blocks * size
    step = pl.program_id(0)
    span = [slice(b * size, (b + 1) * size) for b in range(blocks)]
    own = [slice(h * head_dim, (h + 1) * head_dim) for h in range(heads)]
    pair = math.gcd(2, heads)
    head_lanes = [slice(h * size, (h + 1) * size) for h in range(heads)]

    @pl.when(step == 0)
    def _():
        w_score_s[...] = jnp.zeros_like(w_score_s)
        w_probs_s[...] = jnp.zeros_like(w_probs_s)
        for n, ref in enumerate(sums):
            ref[...] = jnp.zeros_like(ref) if first else carried[n][...]

    lane_head = lax.broadcasted_iota(jnp.int32, (size, proj), 1) // head_dim
    bound = jnp.float32(0.0)
    for c in range(together):
        for s in range(pieces):
            rows = aligned(owners_ref[s], tile_rows)
            act_s[c, rows, :] = inputs[s][0, c]
            grad_s[c, rows, :] = inputs[s][1, c]
        acts = act_s[c]
        grads = grad_s[c]
        acts_t = acts.T
        act_t_s[c] = acts_t
        natural = dot(acts, w_all_ref[:, : 3 * proj])
        across = dot(w_all_t_ref[...], acts_t)
        queries_t = (across[:proj] * scale).astype(BF16)
        kv_t = across[proj : 3 * proj].astype(BF16)
        gate_t = 1.0 / (1.0 + jnp.exp(-across[3 * proj :]))
        d_gated_t = dot(w_out_ref[...], grads.T)
        d_att_t = (d_gated_t * gate_t).astype(BF16)
        gate_t_s[c] = gate_t
        d_gated_t_s[c] = d_gated_t
        squares = lambda x: jnp.max(
            jnp.sum(jnp.square(x.astype(F32)).reshape(heads, head_dim, -1), axis=1)
        )
        bound = jnp.maximum(bound, squares(queries_t) * squares(kv_t[:proj]))
        queries = (natural[:, :proj] * scale).astype(BF16)
        kv = natural[:, proj:].astype(BF16)
        zero = jnp.zeros((size, proj), BF16)
        for b in range(blocks):
            kv_s[c, b] = kv[span[b]]
            kv_t_s[c, b] = kv_t[:, span[b]]
            d_att = d_att_t[:, span[b]].T
            for h in range(heads):
                w_score_s[c, b, own[h], head_lanes[h]] = queries_t[own[h], span[b]]
                w_probs_s[c, b, own[h], head_lanes[h]] = d_att_t[own[h], span[b]]
                here = lane_head == h
                query_s[c, b, h * size : (h + 1) * size, :] = jnp.where(here, queries[span[b]], zero)
                d_att_s[c, b, h * size : (h + 1) * size, :] = jnp.where(here, d_att, zero)
    d_kv_s[...] = jnp.zeros_like(d_kv_s)

    def query_block(b, live, shift):
        chosen = [tables_ref[b, e] for e in range(live)]
        strips = [
            (e, e * size + at, at) for e in range(live) for at in range(0, size, STRIP)
        ]
        rows_of = lambda x: jnp.sum(x.reshape(-1, 8, size), axis=0)
        for c in range(together):
            kv = jnp.concatenate([kv_s[c, k] for k in chosen], axis=0)
            score_s[c, : live * size, :] = dot(kv[:, :proj], w_score_s[c, b])
            d_probs_s[c, : live * size, :] = dot(kv[:, proj:], w_probs_s[c, b])
        for h in range(heads):
            lanes = head_lanes[h]
            stats = []
            for c in range(together):

                def scores(e, row, at):
                    return (
                        score_s[c, row : row + STRIP, lanes] * LOG2E
                        + bias_ref[chosen[e], b, h, at : at + STRIP, :]
                    )

                if shift:
                    peak = jnp.full((8, size), -jnp.inf, F32)
                    for strip in strips:
                        peak = jnp.maximum(
                            peak, jnp.max(scores(*strip).reshape(-1, 8, size), axis=0)
                        )
                    peak = jnp.max(peak, axis=0, keepdims=True)
                total = jnp.zeros((8, size), F32)
                mixed = jnp.zeros((8, size), F32)
                for e, row, at in strips:
                    value = scores(e, row, at)
                    weight = jnp.exp2(value - peak if shift else value)
                    total += rows_of(weight)
                    mixed += rows_of(weight * d_probs_s[c, row : row + STRIP, lanes])
                    score_s[c, row : row + STRIP, lanes] = weight
                norm = 1.0 / jnp.sum(total, axis=0, keepdims=True)
                stats.append((norm, jnp.sum(mixed, axis=0, keepdims=True) * norm))
            for e, row, at in strips:
                part = slice(row, row + STRIP)
                gathered = d_bias_s[b, e, h, at : at + STRIP, :]
                for c, (norm, delta) in enumerate(stats):
                    probs = score_s[c, part, lanes] * norm
                    d_scores = probs * (d_probs_s[c, part, lanes] - delta)
                    probs_s[c, part, lanes] = probs.astype(BF16)
                    ds_s[c, part, lanes] = d_scores.astype(BF16)
                    gathered += d_scores
                d_bias_s[b, e, h, at : at + STRIP, :] = gathered
        for c in range(together):
            kv_t = jnp.concatenate([kv_t_s[c, k] for k in chosen], axis=1)
            for h in range(0, heads, pair):
                lanes = slice(h * size, (h + pair) * size)
                both = slice(h * head_dim, (h + pair) * head_dim)
                low = slice(proj + both.start, proj + both.stop)
                att_t = dot(kv_t[low], probs_s[c, : live * size, lanes])
                d_query_t = dot(kv_t[both], ds_s[c, : live * size, lanes])
                for n in range(pair):
                    att_t_s[c, b, own[h + n], :] = att_t[own[n], head_lanes[n]]
                    d_query_t_s[c, b, own[h + n], :] = d_query_t[own[n], head_lanes[n]]
            d_values = dot(probs_s[c, : live * size, :], d_att_s[c, b])
            d_keys = dot(ds_s[c, : live * size, :], query_s[c, b])
            for e in range(live):
                part = slice(e * size, (e + 1) * size)
                d_kv_s[c, chosen[e], :, :proj] += d_keys[part]
                d_kv_s[c, chosen[e], :, proj:] += d_values[part]

    def all_blocks(shift):
        @pl.loop(0, blocks)
        def _(b):
            for live in range(1, slots + 1):

                @pl.when(lens_ref[b] == live)
                def _():
                    query_block(b, live, shift)

    small = bound <= SAFE_SCORE * SAFE_SCORE

    @pl.when(small)
    def _():
        all_blocks(False)

    @pl.when(jnp.logical_not(small))
    def _():
        all_blocks(True)

    w_qg = jnp.concatenate([w_all_ref[:, :proj], w_all_ref[:, 3 * proj :]], axis=1)
    for c in range(together):
        att_t = jnp.concatenate([att_t_s[c, b] for b in range(blocks)], axis=1)
        d_query_t = jnp.concatenate([d_query_t_s[c, b] for b in range(blocks)], axis=1)
        gate_t = gate_t_s[c]
        gated_t = (gate_t * att_t).astype(BF16)
        d_gpre_t = (d_gated_t_s[c] * att_t * gate_t * (1.0 - gate_t)).astype(BF16)
        d_qg_t = jnp.concatenate([(d_query_t * scale).astype(BF16), d_gpre_t], axis=0)
        d_kv = d_kv_s[c].reshape(tokens, 2 * proj).astype(BF16)
        d_pair = dot(d_kv, w_all_t_ref[proj : 3 * proj, :]) + dot(w_qg, d_qg_t).T
        d_pair_s[c] = d_pair
        for s in range(pieces):
            d_pair_out[s][c] = d_pair_s[c, aligned(owners_ref[s], tile_rows), :].astype(BF16)
        dw_qg_s[...] += dot(d_qg_t, act_s[c])
        dw_kv_s[...] += dot(act_t_s[c], d_kv)
        dwo_s[...] += dot(gated_t, grad_s[c])

    if not last:
        return

    @pl.when(step == pl.num_programs(0) - 1)
    def _():
        weights = [dw_qg_s[:proj, :].T, dw_kv_s[:, :proj], dw_kv_s[:, proj:], dw_qg_s[proj:, :].T]
        weights.append(dwo_s[...])
        far, each = keep_out.shape[0], keep_out.shape[1]
        tile = each // (slots * heads)
        for n, w in enumerate(weights):
            d_w_out[n * chan : (n + 1) * chan, :] = w
            message_out[far * each + n * chan : far * each + (n + 1) * chan, :] = w.astype(BF16)
        for mine in range(inner):

            @pl.when(parity_ref[0] == mine)
            def _():
                for b in range(blocks):
                    for e in range(slots):
                        for h in range(heads):
                            turned = d_bias_s[b, e, h].T.astype(BF16)
                            at = (e * heads + h) * tile
                            for sub in range(size // tile):
                                col = b * (size // tile) + sub
                                piece = turned[sub * tile : (sub + 1) * tile]
                                if col % inner == mine:
                                    keep_out[col // inner, at : at + tile, :] = piece
                                else:
                                    start = (col // inner) * each + at
                                    message_out[start : start + tile, :] = piece


def attention(
    pieces, bias, w_all, w_out, tables, lens, parity, owners, carried, last, query_tile, inner
):
    count = len(pieces)
    _, columns, tile_rows, chan = pieces[0].shape
    blocks, slots = tables.shape
    heads = bias.shape[2]
    proj = w_out.shape[0]
    tokens = tile_rows * count
    size = tokens // blocks
    together = math.gcd(TOGETHER, columns)
    dims = (count, heads, proj // heads, blocks, size, slots, together, inner)
    first = carried is None
    far = tokens // query_tile // inner

    def whole(x):
        return pl.BlockSpec(
            x.shape, lambda j, *_: (0,) * len(x.shape), pipeline_mode=pl.Buffered(1)
        )

    sums = [
        ((blocks, slots, heads, size, size), F32),
        ((2 * proj, chan), F32),
        ((chan, 2 * proj), F32),
        ((proj, chan), F32),
    ]
    if last:
        each = slots * heads * query_tile
        results = [
            ((far, each, size), BF16),
            ((far * each + 5 * chan, size), BF16),
            ((5 * chan, proj), F32),
        ]
    else:
        results = sums
    results = [((columns, tile_rows, chan), BF16)] * count + results
    results = [jax.ShapeDtypeStruct(*x) for x in results]
    scratch = [
        ((together, tokens, chan), BF16),
        ((together, tokens, chan), BF16),
        ((together, tokens, chan), F32),
        ((together, chan, tokens), BF16),
        ((together, blocks, size, 2 * proj), BF16),
        ((together, blocks, 2 * proj, size), BF16),
        ((together, blocks, proj, heads * size), BF16),
        ((together, blocks, proj, heads * size), BF16),
        ((together, blocks, heads * size, proj), BF16),
        ((together, blocks, heads * size, proj), BF16),
        ((together, proj, tokens), F32),
        ((together, proj, tokens), F32),
        ((together, slots * size, heads * size), F32),
        ((together, slots * size, heads * size), F32),
        ((together, slots * size, heads * size), BF16),
        ((together, slots * size, heads * size), BF16),
        ((together, blocks, size, 2 * proj), F32),
        ((together, blocks, proj, size), F32),
        ((together, blocks, proj, size), F32),
    ]
    scratch = [pltpu.VMEM(*x) for x in (sums if last else []) + scratch]
    fixed = [bias, w_all, w_all.T, w_out] + ([] if first else list(carried))
    scalars = [tables, lens, parity, owners]
    pairs = tokens * size * slots * heads
    outs = pl.pallas_call(
        functools.partial(attention_kernel, dims, first, last),
        grid_spec=pltpu.PrefetchScalarGridSpec(
            num_scalar_prefetch=len(scalars),
            grid=(columns // together,),
            in_specs=[
                pl.BlockSpec((2, together, tile_rows, chan), lambda j, *_: (0, j, 0, 0))
            ] * count
            + [whole(x) for x in fixed],
            out_specs=[pl.BlockSpec((together, tile_rows, chan), lambda j, *_: (j, 0, 0))] * count
            + [whole(x) for x in results[count:]],
            scratch_shapes=scratch,
        ),
        out_shape=results,
        compiler_params=pltpu.CompilerParams(vmem_limit_bytes=VMEM_LIMIT),
        cost_estimate=pl.CostEstimate(
            flops=columns * pairs * 7000,
            bytes_accessed=columns * tokens * chan * 6 + 10 * 2**20,
            transcendentals=columns * pairs,
        ),
    )(*scalars, *pieces, *fixed)
    return outs[:count], outs[count:]


def small_call(body, scalars, arrays, results, scratch=()):
    return pl.pallas_call(
        body,
        in_specs=[pl.BlockSpec(memory_space=pltpu.SMEM)] * len(scalars)
        + [pl.BlockSpec(memory_space=pltpu.VMEM)] * len(arrays),
        out_specs=[pl.BlockSpec(memory_space=pltpu.VMEM)] * len(results),
        out_shape=[jax.ShapeDtypeStruct(*x) for x in results],
        scratch_shapes=list(scratch),
        compiler_params=pltpu.CompilerParams(vmem_limit_bytes=SMALL_LIMIT),
    )(*scalars, *arrays)


def aligned(index, count):
    return pl.ds(pl.multiple_of(index * count, count), count)


def split_by_far(targets, keep, came, weights):
    far, each, lanes = keep.shape
    share = weights.shape[0] // far

    def body(targets_ref, keep_ref, came_ref, weights_ref, own_ref, *message_refs):
        for s in range(far):
            t = targets_ref[s]
            out = message_refs[s - 1] if s else own_ref
            bias = keep_ref[t].astype(F32)
            weight = weights_ref[aligned(t, share), :].astype(BF16).astype(F32)
            if came_ref is not None:
                bias += came_ref[aligned(t, each), :].astype(F32)
                rest = came_ref[far * each :, :].astype(F32)
                half = jnp.zeros_like(weight)
                for u in range(far):
                    half = jnp.where(t == u, rest[u * share : (u + 1) * share], half)
                weight += half
            out[:each, :] = bias.astype(out.dtype)
            out[each:, :] = weight.astype(out.dtype)

    results = [((each + share, lanes), F32 if s == 0 else BF16) for s in range(far)]
    return small_call(body, [targets], [keep, came, weights], results)


def split_by_row(owners, chosen, live, own, came, dims):
    rows, slots, per_block, each = dims
    lanes = own.shape[1]
    part = each // slots
    share = own.shape[0] - each

    def body(owners_ref, chosen_ref, live_ref, own_ref, *refs):
        came_refs, outs = refs[: len(came)], refs[len(came) :]
        weight = own_ref[each:, :]
        for ref in came_refs:
            weight += ref[each:, :].astype(F32)
        for s in range(rows):
            outs[s][part:, :] = weight.astype(BF16).astype(outs[s].dtype)
            outs[s][:part, :] = jnp.zeros((part, lanes), outs[s].dtype)
        for e in range(slots):
            at = slice(e * part, (e + 1) * part)
            bias = own_ref[at, :]
            for ref in came_refs:
                bias += ref[at, :].astype(F32)
            for s in range(rows):
                hit = (chosen_ref[e] == owners_ref[s] // per_block) & (e < live_ref[0])

                @pl.when(hit)
                def _():
                    outs[s][:part, :] = bias.astype(outs[s].dtype)

    results = [((part + share, lanes), F32 if s == 0 else BF16) for s in range(rows)]
    return small_call(body, [owners, chosen, live], [own, *came], results)


def add_rows(own, came, part):
    share, lanes = own.shape[0] - part, own.shape[1]

    def body(own_ref, *refs):
        came_refs, (bias_ref, weight_ref) = refs[: len(came)], refs[len(came) :]
        terms = [own_ref[...]] + [ref[...].astype(F32) for ref in came_refs]
        while len(terms) > 1:
            terms = [sum(terms[n : n + 2]) for n in range(0, len(terms), 2)]
        total = terms[0]
        bias_ref[...] = total[:part]
        weight_ref[...] = total[part:].astype(BF16)

    results = [((part, lanes), F32), ((share, lanes), BF16)]
    return small_call(body, [], [own, *came], results)


def place_weights(sources, parts, count):
    share, lanes = parts[0].shape

    def body(sources_ref, *refs):
        part_refs, out_refs, scratch = refs[: len(parts)], refs[len(parts) : -1], refs[-1]
        for s, ref in enumerate(part_refs):
            scratch[aligned(sources_ref[s], share), :] = ref[...].astype(F32)
        for n, ref in enumerate(out_refs):
            ref[...] = scratch[n * lanes : (n + 1) * lanes, :]

    rows = share * len(parts)
    results = [((rows // count, lanes), F32)] * count
    return small_call(body, [sources], parts, results, [pltpu.VMEM((rows, lanes), F32)])


class Peers:
    def __init__(self, axis, stride, count):
        self.axis, self.count = axis, count
        self.paired = count & (count - 1) == 0
        place = lax.axis_index(axis)
        self.digit = place // stride % count
        everyone = range(lax.axis_size(axis))
        self.routes = []
        for s in range(count):
            route = []
            for p in everyone:
                d = p // stride % count
                route.append((p, p + (self.step(d, s) - d) * stride))
            self.routes.append(route)

    def step(self, digit, s):
        return digit ^ s if self.paired else (digit + s) % self.count

    def target(self, s):
        return self.step(self.digit, s)

    def source(self, s):
        return self.target(s) if self.paired else (self.digit - s) % self.count

    def send(self, x, s, home=False):
        route = self.routes[s]
        if home:
            route = [(t, f) for f, t in route]
        return x if s == 0 else lax.ppermute(x, self.axis, route)

    def positions(self):
        digits = jnp.arange(self.count)
        return self.digit ^ digits if self.paired else (self.digit - digits) % self.count

    def gather(self, x):
        return jnp.stack([self.send(x, s) for s in range(self.count)])

    def targets(self):
        return jnp.stack([self.target(s) for s in range(self.count)]).astype(jnp.int32)

    def sources(self):
        return jnp.stack([self.source(s) for s in range(self.count)]).astype(jnp.int32)

    def swap(self, messages):
        return [self.send(x, s + 1) for s, x in enumerate(messages)]


def on_device(
    pair_act, out_grad, tri_bias, w_query, w_key, w_value, w_gate, w_out, key_blocks, list_len
):
    row_count = lax.axis_size("row")
    col_count = lax.axis_size("col")
    tile_rows, tile_cols, chan = pair_act.shape
    heads = tri_bias.shape[0]
    query_tile = tri_bias.shape[2]
    proj = w_query.shape[1]
    blocks, slots = key_blocks.shape
    tokens = tile_rows * row_count
    size = tokens // blocks
    col_width = tile_cols // row_count
    chunks = math.gcd(CHUNKS, col_width)
    width = col_width // chunks
    inner = math.gcd(2, col_count)
    rows = Peers("row", 1, row_count)
    near = Peers("col", 1, inner)
    far = Peers("col", inner, col_count // inner)

    gathered = rows.gather(jnp.transpose(tri_bias, (0, 2, 1)))
    both = jnp.stack([pair_act, out_grad]).reshape(2, tile_rows, row_count, chunks, width, chan)
    both = jnp.transpose(both, (2, 3, 0, 4, 1, 5))
    owners = rows.sources()
    outgoing = [
        [
            lax.dynamic_index_in_dim(both[:, c], rows.target(s), 0, keepdims=False)
            for s in range(row_count)
        ]
        for c in range(chunks)
    ]
    gathered, outgoing = lax.optimization_barrier((gathered, outgoing))
    arrived = [[rows.send(x, s) for s, x in enumerate(outgoing[0])]]
    gathered, arrived[0], outgoing[1:] = lax.optimization_barrier(
        (far.gather(gathered), arrived[0], outgoing[1:])
    )
    gathered = near.gather(gathered)
    gathered = gathered.reshape((col_count, row_count, heads, query_tile, tile_rows))
    columns = jnp.arange(col_count)
    col_pos = near.positions()[columns % inner] * far.count + far.positions()[columns // inner]
    bias = shifted_bias(
        gathered,
        key_blocks,
        list_len,
        col_pos.astype(jnp.int32),
        rows.positions().astype(jnp.int32),
    )

    parity = near.targets()[:1]
    w_all = jnp.concatenate([w_query, w_key, w_value, w_gate], axis=1)
    arrived += [[rows.send(x, s) for s, x in enumerate(part)] for part in outgoing[1:]]
    carried = None
    returned = []
    for c in range(chunks):
        d_pieces, carried = attention(
            arrived[c], bias, w_all, w_out, key_blocks, list_len, parity, owners, carried,
            c == chunks - 1, query_tile, inner,
        )
        if c < chunks - 1:
            d_pieces = [rows.send(x, s, home=True) for s, x in enumerate(d_pieces)]
        returned.append(d_pieces)
    keep, message, w_part = carried
    message, returned[:-1] = lax.optimization_barrier((message, returned[:-1]))
    far_targets, row_targets = far.targets(), rows.targets()

    each = keep.shape[1]
    own, *messages = split_by_far(far_targets, keep, near.send(message, inner - 1), w_part)
    messages, returned[-1] = lax.optimization_barrier((messages, returned[-1]))
    came = far.swap(messages)
    returned[-1] = [rows.send(x, s, home=True) for s, x in enumerate(returned[-1])]
    block = lax.axis_index("col") * query_tile // size
    chosen = lax.dynamic_index_in_dim(key_blocks, block, 0, keepdims=False)
    live = lax.dynamic_slice_in_dim(list_len, block, 1)
    per_block = size // tile_rows
    own, *messages = split_by_row(
        row_targets, chosen, live, own, came, (row_count, slots, per_block, each)
    )
    d_bias, w_part = add_rows(own, rows.swap(messages), each // slots)
    weights = place_weights(far.sources(), [far.send(w_part, s) for s in range(far.count)], 5)
    d_bias = d_bias.reshape(heads, query_tile, per_block, tile_rows)
    d_bias = lax.dynamic_index_in_dim(d_bias, rows.digit % per_block, 2, keepdims=False)


    d_pair = jnp.zeros((tile_rows, tile_cols, chan), BF16)
    for c, part in enumerate(returned):
        for s, x in enumerate(part):
            at = rows.target(s) * col_width + c * width
            d_pair = lax.dynamic_update_slice(d_pair, jnp.transpose(x, (1, 0, 2)), (0, at, 0))
    return (d_pair, jnp.transpose(d_bias, (0, 2, 1)), *weights)


def solution(mesh):
    in_specs = (
        P("row", "col", None),
        P("row", "col", None),
        P(None, "row", "col"),
        P(),
        P(),
        P(),
        P(),
        P(),
        P(),
        P(),
    )
    out_specs = (P("row", "col", None), P(None, "row", "col"), P(), P(), P(), P(), P())
    return jax.shard_map(
        on_device, mesh=mesh, in_specs=in_specs, out_specs=out_specs, check_vma=False
    )
```

```python
import functools
import math

import jax
import jax.numpy as jnp
from jax import lax
from jax.experimental import pallas as pl
from jax.experimental.pallas import tpu as pltpu
from jax.sharding import PartitionSpec as P

F32 = jnp.float32
BF16 = jnp.bfloat16
CHUNKS = 1
TOGETHER = 2
STRIP = 32
LOG2E = math.log2(math.e)
SAFE_SCORE = 30.0
VMEM_LIMIT = 32 * 1024 * 1024
SMALL_LIMIT = 16 * 1024 * 1024


def dot(a, b):
    return jnp.dot(a, b, preferred_element_type=F32)


def bias_kernel(inner, came_at, tables_ref, lens_ref, place_ref, *refs):
    *parts, out_ref = refs
    b = pl.program_id(0)
    blocks, _, heads, size, _ = out_ref.shape
    slots = tables_ref.shape[1]
    _, rows, _, query_tile, tile = parts[0].shape
    per_block = size // tile
    subs = size // query_tile
    for h in range(heads):
        for r in range(rows):
            at = came_at(place_ref[0], r)
            pieces = [p[0, at, h] for p in parts]
            if inner > 1:
                own, other = pieces[:subs], pieces[subs:]
                near = [(b * subs + n) % inner == place_ref[1] for n in range(subs)]
                pieces = [jnp.where(*x) for x in zip(near, own, other)]
            start = (r % per_block) * tile
            out_ref[r // per_block, 0, h, start : start + tile, :] = (
                jnp.concatenate(pieces, axis=0).T.astype(F32)
            )
    for h in range(heads):
        peak = jnp.max(out_ref[tables_ref[b, 0], 0, h], axis=0, keepdims=True)
        for e in range(1, slots):
            other = jnp.max(out_ref[tables_ref[b, e], 0, h], axis=0, keepdims=True)
            peak = jnp.where(e < lens_ref[b], jnp.maximum(peak, other), peak)
        for kb in range(blocks):
            out_ref[kb, 0, h] = (out_ref[kb, 0, h] - peak) * LOG2E


def shifted_bias(halves, key_blocks, list_len, place, rows, far):
    _, row_count, heads, query_tile, key_tile = halves[0].shape
    inner = len(halves)
    blocks = key_blocks.shape[0]
    size = inner * far.count * query_tile // blocks
    subs = size // query_tile

    def part(sub):
        return pl.BlockSpec(
            (1, row_count, heads, query_tile, key_tile),
            lambda b, tables, lens, at: (
                far.came_at(at[2], (b * subs + sub) // inner), 0, 0, 0, 0
            ),
        )

    return pl.pallas_call(
        functools.partial(bias_kernel, inner, rows.came_at),
        grid_spec=pltpu.PrefetchScalarGridSpec(
            num_scalar_prefetch=3,
            grid=(blocks,),
            in_specs=[part(sub) for _ in halves for sub in range(subs)],
            out_specs=pl.BlockSpec((blocks, 1, heads, size, size), lambda b, *_: (0, b, 0, 0, 0)),
        ),
        out_shape=jax.ShapeDtypeStruct((blocks, blocks, heads, size, size), F32),
        compiler_params=pltpu.CompilerParams(vmem_limit_bytes=SMALL_LIMIT),
    )(key_blocks, list_len, place, *[x for x in halves for _ in range(subs)])


def attention_kernel(dims, first, last, owner_of, tables_ref, lens_ref, place_ref, *refs):
    pieces, heads, head_dim, blocks, size, slots, together, inner = dims
    refs = list(refs)
    take = lambda n: [refs.pop(0) for _ in range(n)]
    inputs = take(pieces)
    bias_ref, *w_refs, w_out_ref = take(6)
    carried = [] if first else take(4)
    d_pair_out = take(pieces)
    if last:
        keep_out, message_out, d_w_out = take(3)
    d_bias_s, dw_qg_s, dw_kv_s, dwo_s = sums = take(4)
    (w_all_ref, w_all_t_ref, act_s, grad_s, d_pair_s, act_t_s, kv_s, kv_t_s, w_score_s, w_probs_s, d_att_s, query_s, gate_t_s, d_gated_t_s,
     score_s, d_probs_s, probs_s, ds_s, d_kv_s, att_t_s, d_query_t_s) = refs
    proj = heads * head_dim
    scale = head_dim ** (-0.5)
    tile_rows, chan = inputs[0].shape[2:]
    tokens = blocks * size
    step = pl.program_id(0)
    span = [slice(b * size, (b + 1) * size) for b in range(blocks)]
    own = [slice(h * head_dim, (h + 1) * head_dim) for h in range(heads)]
    pair = math.gcd(2, heads)
    head_lanes = [slice(h * size, (h + 1) * size) for h in range(heads)]

    @pl.when(step == 0)
    def _():
        for n, ref in enumerate(w_refs):
            w_all_ref[:, n * proj : (n + 1) * proj] = ref[...]
            w_all_t_ref[n * proj : (n + 1) * proj, :] = ref[...].T
        w_score_s[...] = jnp.zeros_like(w_score_s)
        w_probs_s[...] = jnp.zeros_like(w_probs_s)
        for n, ref in enumerate(sums):
            ref[...] = jnp.zeros_like(ref) if first else carried[n][...]

    lane_head = lax.broadcasted_iota(jnp.int32, (size, proj), 1) // head_dim
    bound = jnp.float32(0.0)
    for c in range(together):
        for s in range(pieces):
            rows = aligned(owner_of(place_ref[0], s), tile_rows)
            act_s[c, rows, :] = inputs[s][0, c]
            grad_s[c, rows, :] = inputs[s][1, c]
        acts = act_s[c]
        grads = grad_s[c]
        acts_t = acts.T
        act_t_s[c] = acts_t
        natural = dot(acts, w_all_ref[:, : 3 * proj])
        across = dot(w_all_t_ref[...], acts_t)
        queries_t = (across[:proj] * scale).astype(BF16)
        kv_t = across[proj : 3 * proj].astype(BF16)
        gate_t = 1.0 / (1.0 + jnp.exp(-across[3 * proj :]))
        d_gated_t = dot(w_out_ref[...], grads.T)
        d_att_t = (d_gated_t * gate_t).astype(BF16)
        gate_t_s[c] = gate_t
        d_gated_t_s[c] = d_gated_t
        squares = lambda x: jnp.max(
            jnp.sum(jnp.square(x.astype(F32)).reshape(heads, head_dim, -1), axis=1)
        )
        bound = jnp.maximum(bound, squares(queries_t) * squares(kv_t[:proj]))
        queries = (natural[:, :proj] * scale).astype(BF16)
        kv = natural[:, proj:].astype(BF16)
        zero = jnp.zeros((size, proj), BF16)
        for b in range(blocks):
            kv_s[c, b] = kv[span[b]]
            kv_t_s[c, b] = kv_t[:, span[b]]
            d_att = d_att_t[:, span[b]].T
            for h in range(heads):
                w_score_s[c, b, own[h], head_lanes[h]] = queries_t[own[h], span[b]]
                w_probs_s[c, b, own[h], head_lanes[h]] = d_att_t[own[h], span[b]]
                here = lane_head == h
                query_s[c, b, h * size : (h + 1) * size, :] = jnp.where(here, queries[span[b]], zero)
                d_att_s[c, b, h * size : (h + 1) * size, :] = jnp.where(here, d_att, zero)
    d_kv_s[...] = jnp.zeros_like(d_kv_s)

    def query_block(b, live, shift):
        chosen = [tables_ref[b, e] for e in range(live)]
        strips = [
            (e, e * size + at, at) for e in range(live) for at in range(0, size, STRIP)
        ]
        rows_of = lambda x: jnp.sum(x.reshape(-1, 8, size), axis=0)
        for c in range(together):
            kv = jnp.concatenate([kv_s[c, k] for k in chosen], axis=0)
            score_s[c, : live * size, :] = dot(kv[:, :proj], w_score_s[c, b])
            d_probs_s[c, : live * size, :] = dot(kv[:, proj:], w_probs_s[c, b])
        for h in range(heads):
            lanes = head_lanes[h]
            stats = []
            for c in range(together):

                def scores(e, row, at):
                    return (
                        score_s[c, row : row + STRIP, lanes] * LOG2E
                        + bias_ref[chosen[e], b, h, at : at + STRIP, :]
                    )

                if shift:
                    peak = jnp.full((8, size), -jnp.inf, F32)
                    for strip in strips:
                        peak = jnp.maximum(
                            peak, jnp.max(scores(*strip).reshape(-1, 8, size), axis=0)
                        )
                    peak = jnp.max(peak, axis=0, keepdims=True)
                total = jnp.zeros((8, size), F32)
                mixed = jnp.zeros((8, size), F32)
                for e, row, at in strips:
                    value = scores(e, row, at)
                    weight = jnp.exp2(value - peak if shift else value)
                    total += rows_of(weight)
                    mixed += rows_of(weight * d_probs_s[c, row : row + STRIP, lanes])
                    score_s[c, row : row + STRIP, lanes] = weight
                norm = 1.0 / jnp.sum(total, axis=0, keepdims=True)
                stats.append((norm, jnp.sum(mixed, axis=0, keepdims=True) * norm))
            for e, row, at in strips:
                part = slice(row, row + STRIP)
                gathered = d_bias_s[b, e, h, at : at + STRIP, :]
                for c, (norm, delta) in enumerate(stats):
                    probs = score_s[c, part, lanes] * norm
                    d_scores = probs * (d_probs_s[c, part, lanes] - delta)
                    probs_s[c, part, lanes] = probs.astype(BF16)
                    ds_s[c, part, lanes] = d_scores.astype(BF16)
                    gathered += d_scores
                d_bias_s[b, e, h, at : at + STRIP, :] = gathered
        for c in range(together):
            kv_t = jnp.concatenate([kv_t_s[c, k] for k in chosen], axis=1)
            for h in range(0, heads, pair):
                lanes = slice(h * size, (h + pair) * size)
                both = slice(h * head_dim, (h + pair) * head_dim)
                low = slice(proj + both.start, proj + both.stop)
                att_t = dot(kv_t[low], probs_s[c, : live * size, lanes])
                d_query_t = dot(kv_t[both], ds_s[c, : live * size, lanes])
                for n in range(pair):
                    att_t_s[c, b, own[h + n], :] = att_t[own[n], head_lanes[n]]
                    d_query_t_s[c, b, own[h + n], :] = d_query_t[own[n], head_lanes[n]]
            d_values = dot(probs_s[c, : live * size, :], d_att_s[c, b])
            d_keys = dot(ds_s[c, : live * size, :], query_s[c, b])
            for e in range(live):
                part = slice(e * size, (e + 1) * size)
                d_kv_s[c, chosen[e], :, :proj] += d_keys[part]
                d_kv_s[c, chosen[e], :, proj:] += d_values[part]

    def all_blocks(shift):
        @pl.loop(0, blocks)
        def _(b):
            for live in range(1, slots + 1):

                @pl.when(lens_ref[b] == live)
                def _():
                    query_block(b, live, shift)

    small = bound <= SAFE_SCORE * SAFE_SCORE

    @pl.when(small)
    def _():
        all_blocks(False)

    @pl.when(jnp.logical_not(small))
    def _():
        all_blocks(True)

    w_qg = jnp.concatenate([w_all_ref[:, :proj], w_all_ref[:, 3 * proj :]], axis=1)
    for c in range(together):
        att_t = jnp.concatenate([att_t_s[c, b] for b in range(blocks)], axis=1)
        d_query_t = jnp.concatenate([d_query_t_s[c, b] for b in range(blocks)], axis=1)
        gate_t = gate_t_s[c]
        gated_t = (gate_t * att_t).astype(BF16)
        d_gpre_t = (d_gated_t_s[c] * att_t * gate_t * (1.0 - gate_t)).astype(BF16)
        d_qg_t = jnp.concatenate([(d_query_t * scale).astype(BF16), d_gpre_t], axis=0)
        d_kv = d_kv_s[c].reshape(tokens, 2 * proj).astype(BF16)
        d_pair = dot(d_kv, w_all_t_ref[proj : 3 * proj, :]) + dot(w_qg, d_qg_t).T
        d_pair_s[c] = d_pair
        for s in range(pieces):
            d_pair_out[s][c] = d_pair_s[c, aligned(owner_of(place_ref[0], s), tile_rows), :].astype(BF16)
        dw_qg_s[...] += dot(d_qg_t, act_s[c])
        dw_kv_s[...] += dot(act_t_s[c], d_kv)
        dwo_s[...] += dot(gated_t, grad_s[c])

    if not last:
        return

    @pl.when(step == pl.num_programs(0) - 1)
    def _():
        weights = [dw_qg_s[:proj, :].T, dw_kv_s[:, :proj], dw_kv_s[:, proj:], dw_qg_s[proj:, :].T]
        weights.append(dwo_s[...])
        far, each = keep_out.shape[0], keep_out.shape[1]
        tile = each // (slots * heads)
        for n, w in enumerate(weights):
            d_w_out[n * chan : (n + 1) * chan, :] = w
            message_out[far * each + n * chan : far * each + (n + 1) * chan, :] = w.astype(BF16)
        for mine in range(inner):

            @pl.when(place_ref[1] == mine)
            def _():
                for b in range(blocks):
                    for e in range(slots):
                        for h in range(heads):
                            turned = d_bias_s[b, e, h].astype(BF16).T
                            at = (e * heads + h) * tile
                            for sub in range(size // tile):
                                col = b * (size // tile) + sub
                                piece = turned[sub * tile : (sub + 1) * tile]
                                if col % inner == mine:
                                    keep_out[col // inner, at : at + tile, :] = piece
                                else:
                                    start = (col // inner) * each + at
                                    message_out[start : start + tile, :] = piece


def attention(
    pieces, bias, weights, tables, lens, place, rows, carried, last, query_tile, inner
):
    count = len(pieces)
    _, columns, tile_rows, chan = pieces[0].shape
    blocks, slots = tables.shape
    heads = bias.shape[2]
    proj = weights[-1].shape[0]
    tokens = tile_rows * count
    size = tokens // blocks
    together = math.gcd(TOGETHER, columns)
    dims = (count, heads, proj // heads, blocks, size, slots, together, inner)
    first = carried is None
    far = tokens // query_tile // inner

    def whole(x):
        return pl.BlockSpec(
            x.shape, lambda j, *_: (0,) * len(x.shape), pipeline_mode=pl.Buffered(1)
        )

    sums = [
        ((blocks, slots, heads, size, size), F32),
        ((2 * proj, chan), F32),
        ((chan, 2 * proj), F32),
        ((proj, chan), F32),
    ]
    if last:
        each = slots * heads * query_tile
        results = [
            ((far, each, size), BF16),
            ((far * each + 5 * chan, size), BF16),
            ((5 * chan, proj), F32),
        ]
    else:
        results = sums
    results = [((columns, tile_rows, chan), BF16)] * count + results
    results = [jax.ShapeDtypeStruct(*x) for x in results]
    scratch = [
        ((chan, 4 * proj), BF16),
        ((4 * proj, chan), BF16),
        ((together, tokens, chan), BF16),
        ((together, tokens, chan), BF16),
        ((together, tokens, chan), F32),
        ((together, chan, tokens), BF16),
        ((together, blocks, size, 2 * proj), BF16),
        ((together, blocks, 2 * proj, size), BF16),
        ((together, blocks, proj, heads * size), BF16),
        ((together, blocks, proj, heads * size), BF16),
        ((together, blocks, heads * size, proj), BF16),
        ((together, blocks, heads * size, proj), BF16),
        ((together, proj, tokens), F32),
        ((together, proj, tokens), F32),
        ((together, slots * size, heads * size), F32),
        ((together, slots * size, heads * size), F32),
        ((together, slots * size, heads * size), BF16),
        ((together, slots * size, heads * size), BF16),
        ((together, blocks, size, 2 * proj), F32),
        ((together, blocks, proj, size), F32),
        ((together, blocks, proj, size), F32),
    ]
    scratch = [pltpu.VMEM(*x) for x in (sums if last else []) + scratch]
    fixed = [bias, *weights] + ([] if first else list(carried))
    scalars = [tables, lens, place]
    pairs = tokens * size * slots * heads
    outs = pl.pallas_call(
        functools.partial(attention_kernel, dims, first, last, rows.source_of),
        grid_spec=pltpu.PrefetchScalarGridSpec(
            num_scalar_prefetch=len(scalars),
            grid=(columns // together,),
            in_specs=[
                pl.BlockSpec((2, together, tile_rows, chan), lambda j, *_: (0, j, 0, 0))
            ] * count
            + [whole(x) for x in fixed],
            out_specs=[pl.BlockSpec((together, tile_rows, chan), lambda j, *_: (j, 0, 0))] * count
            + [whole(x) for x in results[count:]],
            scratch_shapes=scratch,
        ),
        out_shape=results,
        compiler_params=pltpu.CompilerParams(vmem_limit_bytes=VMEM_LIMIT),
        cost_estimate=pl.CostEstimate(
            flops=columns * pairs * 7000,
            bytes_accessed=columns * tokens * chan * 6 + 10 * 2**20,
            transcendentals=columns * pairs,
        ),
    )(*scalars, *pieces, *fixed)
    return outs[:count], outs[count:]


def small_call(body, scalars, arrays, results, scratch=()):
    return pl.pallas_call(
        body,
        in_specs=[pl.BlockSpec(memory_space=pltpu.SMEM)] * len(scalars)
        + [pl.BlockSpec(memory_space=pltpu.VMEM)] * len(arrays),
        out_specs=[pl.BlockSpec(memory_space=pltpu.VMEM)] * len(results),
        out_shape=[jax.ShapeDtypeStruct(*x) for x in results],
        scratch_shapes=list(scratch),
        compiler_params=pltpu.CompilerParams(vmem_limit_bytes=SMALL_LIMIT),
    )(*scalars, *arrays)


def aligned(index, count):
    return pl.ds(pl.multiple_of(index * count, count), count)


def split_by_far(place, peers, keep, came, weights):
    far, each, lanes = keep.shape
    share = weights.shape[0] // far

    def body(place_ref, keep_ref, came_ref, weights_ref, own_ref, *message_refs):
        for s in range(far):
            t = peers.step(place_ref[2], s)
            out = message_refs[s - 1] if s else own_ref
            bias = keep_ref[t].astype(F32)
            weight = weights_ref[aligned(t, share), :].astype(BF16).astype(F32)
            if came_ref is not None:
                bias += came_ref[aligned(t, each), :].astype(F32)
                rest = came_ref[far * each :, :].astype(F32)
                half = jnp.zeros_like(weight)
                for u in range(far):
                    half = jnp.where(t == u, rest[u * share : (u + 1) * share], half)
                weight += half
            out[:each, :] = bias.astype(out.dtype)
            out[each:, :] = weight.astype(out.dtype)

    results = [((each + share, lanes), F32 if s == 0 else BF16) for s in range(far)]
    return small_call(body, [place], [keep, came, weights], results)


def split_by_row(place, tables, lens, peers, own, came, dims):
    slots, per_block, each, block_of = dims
    rows = peers.count
    lanes = own.shape[1]
    part = each // slots
    share = own.shape[0] - each

    def body(place_ref, tables_ref, lens_ref, own_ref, *refs):
        block = block_of(place_ref)
        came_refs, outs = refs[: len(came)], refs[len(came) :]
        weight = own_ref[each:, :]
        for ref in came_refs:
            weight += ref[each:, :].astype(F32)
        for s in range(rows):
            outs[s][part:, :] = weight.astype(BF16).astype(outs[s].dtype)
            outs[s][:part, :] = jnp.zeros((part, lanes), outs[s].dtype)
        for e in range(slots):
            at = slice(e * part, (e + 1) * part)
            bias = own_ref[at, :]
            for ref in came_refs:
                bias += ref[at, :].astype(F32)
            for s in range(rows):
                owner = peers.step(place_ref[0], s)
                hit = (tables_ref[block, e] == owner // per_block) & (e < lens_ref[block])

                @pl.when(hit)
                def _():
                    outs[s][:part, :] = bias.astype(outs[s].dtype)

    results = [((part + share, lanes), F32 if s == 0 else BF16) for s in range(rows)]
    return small_call(body, [place, tables, lens], [own, *came], results)


def add_rows(own, came, part):
    share, lanes = own.shape[0] - part, own.shape[1]

    def body(own_ref, *refs):
        came_refs, (bias_ref, weight_ref) = refs[: len(came)], refs[len(came) :]
        terms = [own_ref[...]] + [ref[...].astype(F32) for ref in came_refs]
        while len(terms) > 1:
            terms = [sum(terms[n : n + 2]) for n in range(0, len(terms), 2)]
        total = terms[0]
        bias_ref[...] = total[:part]
        weight_ref[...] = total[part:].astype(BF16)

    results = [((part, lanes), F32), ((share, lanes), BF16)]
    return small_call(body, [], [own, *came], results)


def place_weights(place, peers, parts, count):
    share, lanes = parts[0].shape

    def body(place_ref, *refs):
        part_refs, out_refs, scratch = refs[: len(parts)], refs[len(parts) : -1], refs[-1]
        for s, ref in enumerate(part_refs):
            scratch[aligned(peers.source_of(place_ref[2], s), share), :] = ref[...].astype(F32)
        for n, ref in enumerate(out_refs):
            ref[...] = scratch[n * lanes : (n + 1) * lanes, :]

    rows = share * len(parts)
    results = [((rows // count, lanes), F32)] * count
    return small_call(body, [place], parts, results, [pltpu.VMEM((rows, lanes), F32)])


class Peers:
    def __init__(self, axis, stride, count):
        self.axis, self.count = axis, count
        self.paired = count & (count - 1) == 0
        place = lax.axis_index(axis)
        self.digit = place // stride % count
        everyone = range(lax.axis_size(axis))
        self.routes = []
        for s in range(count):
            route = []
            for p in everyone:
                d = p // stride % count
                route.append((p, p + (self.step(d, s) - d) * stride))
            self.routes.append(route)

    def step(self, digit, s):
        return digit ^ s if self.paired else (digit + s) % self.count

    def target(self, s):
        return self.step(self.digit, s)

    def source_of(self, digit, s):
        return self.step(digit, s) if self.paired else (digit + self.count - s) % self.count

    def came_at(self, digit, source):
        return digit ^ source if self.paired else (digit + self.count - source) % self.count

    def send(self, x, s, home=False):
        route = self.routes[s]
        if home:
            route = [(t, f) for f, t in route]
        return x if s == 0 else lax.ppermute(x, self.axis, route)

    def gather(self, x):
        return jnp.stack([self.send(x, s) for s in range(self.count)])

    def swap(self, messages):
        return [self.send(x, s + 1) for s, x in enumerate(messages)]


def on_device(
    pair_act, out_grad, tri_bias, w_query, w_key, w_value, w_gate, w_out, key_blocks, list_len
):
    row_count = lax.axis_size("row")
    col_count = lax.axis_size("col")
    tile_rows, tile_cols, chan = pair_act.shape
    heads = tri_bias.shape[0]
    query_tile = tri_bias.shape[2]
    proj = w_query.shape[1]
    blocks, slots = key_blocks.shape
    tokens = tile_rows * row_count
    size = tokens // blocks
    col_width = tile_cols // row_count
    chunks = math.gcd(CHUNKS, col_width)
    width = col_width // chunks
    inner = math.gcd(2, col_count)
    rows = Peers("row", 1, row_count)
    near = Peers("col", 1, inner)
    far = Peers("col", inner, col_count // inner)

    gathered = rows.gather(jnp.transpose(tri_bias, (0, 2, 1)))
    both = jnp.stack([pair_act, out_grad]).reshape(2, tile_rows, row_count, chunks, width, chan)
    both = jnp.transpose(both, (2, 3, 0, 4, 1, 5))
    outgoing = [
        [
            lax.dynamic_index_in_dim(both[:, c], rows.target(s), 0, keepdims=False)
            for s in range(row_count)
        ]
        for c in range(chunks)
    ]
    gathered, outgoing = lax.optimization_barrier((gathered, outgoing))
    arrived = [[rows.send(x, s) for s, x in enumerate(outgoing[0])]]
    gathered, arrived[0], outgoing[1:] = lax.optimization_barrier(
        (far.gather(gathered), arrived[0], outgoing[1:])
    )
    place = jnp.stack([rows.digit, near.digit, far.digit]).astype(jnp.int32)
    halves = [near.send(gathered, s) for s in range(inner)]
    bias = shifted_bias(halves, key_blocks, list_len, place, rows, far)
    projections = [w_query, w_key, w_value, w_gate, w_out]
    arrived += [[rows.send(x, s) for s, x in enumerate(part)] for part in outgoing[1:]]
    carried = None
    returned = []
    for c in range(chunks):
        d_pieces, carried = attention(
            arrived[c], bias, projections, key_blocks, list_len, place, rows, carried,
            c == chunks - 1, query_tile, inner,
        )
        if c < chunks - 1:
            d_pieces = [rows.send(x, s, home=True) for s, x in enumerate(d_pieces)]
        returned.append(d_pieces)
    keep, message, w_part = carried
    message, returned[:-1] = lax.optimization_barrier((message, returned[:-1]))

    each = keep.shape[1]
    own, *messages = split_by_far(place, far, keep, near.send(message, inner - 1), w_part)
    messages, returned[-1] = lax.optimization_barrier((messages, returned[-1]))
    came = far.swap(messages)
    returned[-1] = [rows.send(x, s, home=True) for s, x in enumerate(returned[-1])]
    per_block = size // tile_rows
    block_of = lambda at: (at[2] * inner + at[1]) * query_tile // size
    own, *messages = split_by_row(
        place, key_blocks, list_len, rows, own, came, (slots, per_block, each, block_of)
    )
    d_bias, w_part = add_rows(own, rows.swap(messages), each // slots)
    weights = place_weights(place, far, [far.send(w_part, s) for s in range(far.count)], 5)
    d_bias = d_bias.reshape(heads, query_tile, per_block, tile_rows)
    d_bias = lax.dynamic_index_in_dim(d_bias, rows.digit % per_block, 2, keepdims=False)


    d_pair = jnp.zeros((tile_rows, tile_cols, chan), BF16)
    for c, part in enumerate(returned):
        for s, x in enumerate(part):
            at = rows.target(s) * col_width + c * width
            d_pair = lax.dynamic_update_slice(d_pair, jnp.transpose(x, (1, 0, 2)), (0, at, 0))
    return (d_pair, jnp.transpose(d_bias, (0, 2, 1)), *weights)


def solution(mesh):
    in_specs = (
        P("row", "col", None),
        P("row", "col", None),
        P(None, "row", "col"),
        P(),
        P(),
        P(),
        P(),
        P(),
        P(),
        P(),
    )
    out_specs = (P("row", "col", None), P(None, "row", "col"), P(), P(), P(), P(), P())
    return jax.shard_map(
        on_device, mesh=mesh, in_specs=in_specs, out_specs=out_specs, check_vma=False
    )
```

```python
import functools
import math

import jax
import jax.numpy as jnp
from jax import lax
from jax.experimental import pallas as pl
from jax.experimental.pallas import tpu as pltpu
from jax.sharding import PartitionSpec as P

F32 = jnp.float32
BF16 = jnp.bfloat16
CHUNKS = 2
TOGETHER = 2
STRIP = 32
LOG2E = math.log2(math.e)
SAFE_SCORE = 30.0
VMEM_LIMIT = 32 * 1024 * 1024
SMALL_LIMIT = 16 * 1024 * 1024


def dot(a, b):
    return jnp.dot(a, b, preferred_element_type=F32)


def bias_kernel(inner, came_at, tables_ref, lens_ref, place_ref, *refs):
    *parts, out_ref = refs
    b = pl.program_id(0)
    blocks, _, heads, size, _ = out_ref.shape
    slots = tables_ref.shape[1]
    _, rows, _, query_tile, tile = parts[0].shape
    per_block = size // tile
    subs = size // query_tile
    for h in range(heads):
        for r in range(rows):
            at = came_at(place_ref[0], r)
            pieces = [p[0, at, h] for p in parts]
            if inner > 1:
                own, other = pieces[:subs], pieces[subs:]
                near = [(b * subs + n) % inner == place_ref[1] for n in range(subs)]
                pieces = [jnp.where(*x) for x in zip(near, own, other)]
            start = (r % per_block) * tile
            out_ref[r // per_block, 0, h, start : start + tile, :] = (
                jnp.concatenate(pieces, axis=0).T.astype(F32)
            )
    for h in range(heads):
        peak = jnp.max(out_ref[tables_ref[b, 0], 0, h], axis=0, keepdims=True)
        for e in range(1, slots):
            other = jnp.max(out_ref[tables_ref[b, e], 0, h], axis=0, keepdims=True)
            peak = jnp.where(e < lens_ref[b], jnp.maximum(peak, other), peak)
        for kb in range(blocks):
            out_ref[kb, 0, h] = (out_ref[kb, 0, h] - peak) * LOG2E


def shifted_bias(halves, key_blocks, list_len, place, rows, far):
    _, row_count, heads, query_tile, key_tile = halves[0].shape
    inner = len(halves)
    blocks = key_blocks.shape[0]
    size = inner * far.count * query_tile // blocks
    subs = size // query_tile

    def part(sub):
        return pl.BlockSpec(
            (1, row_count, heads, query_tile, key_tile),
            lambda b, tables, lens, at: (
                far.came_at(at[2], (b * subs + sub) // inner), 0, 0, 0, 0
            ),
        )

    return pl.pallas_call(
        functools.partial(bias_kernel, inner, rows.came_at),
        grid_spec=pltpu.PrefetchScalarGridSpec(
            num_scalar_prefetch=3,
            grid=(blocks,),
            in_specs=[part(sub) for _ in halves for sub in range(subs)],
            out_specs=pl.BlockSpec((blocks, 1, heads, size, size), lambda b, *_: (0, b, 0, 0, 0)),
        ),
        out_shape=jax.ShapeDtypeStruct((blocks, blocks, heads, size, size), F32),
        compiler_params=pltpu.CompilerParams(vmem_limit_bytes=SMALL_LIMIT),
    )(key_blocks, list_len, place, *[x for x in halves for _ in range(subs)])


def attention_kernel(dims, first, last, owner_of, tables_ref, lens_ref, place_ref, *refs):
    pieces, heads, head_dim, blocks, size, slots, together, inner = dims
    refs = list(refs)
    take = lambda n: [refs.pop(0) for _ in range(n)]
    inputs = take(pieces)
    bias_ref, *w_refs, w_out_ref = take(6)
    carried = [] if first else take(4)
    d_pair_out = take(pieces)
    if last:
        keep_out, message_out, d_w_out = take(3)
    d_bias_s, dw_qg_s, dw_kv_s, dwo_s = sums = take(4)
    (w_all_ref, w_all_t_ref, act_s, grad_s, d_pair_s, act_t_s, kv_s, kv_t_s, w_score_s, w_probs_s, d_att_s, query_s, gate_t_s, d_gated_t_s,
     score_s, d_probs_s, probs_s, ds_s, d_kv_s, att_t_s, d_query_t_s) = refs
    proj = heads * head_dim
    scale = head_dim ** (-0.5)
    tile_rows, chan = inputs[0].shape[2:]
    tokens = blocks * size
    step = pl.program_id(0)
    span = [slice(b * size, (b + 1) * size) for b in range(blocks)]
    own = [slice(h * head_dim, (h + 1) * head_dim) for h in range(heads)]
    pair = math.gcd(2, heads)
    head_lanes = [slice(h * size, (h + 1) * size) for h in range(heads)]

    @pl.when(step == 0)
    def _():
        for n, ref in enumerate(w_refs):
            w_all_ref[:, n * proj : (n + 1) * proj] = ref[...]
            w_all_t_ref[n * proj : (n + 1) * proj, :] = ref[...].T
        w_score_s[...] = jnp.zeros_like(w_score_s)
        w_probs_s[...] = jnp.zeros_like(w_probs_s)
        for n, ref in enumerate(sums):
            ref[...] = jnp.zeros_like(ref) if first else carried[n][...]

    lane_head = lax.broadcasted_iota(jnp.int32, (size, proj), 1) // head_dim
    bound = jnp.float32(0.0)
    for c in range(together):
        for s in range(pieces):
            rows = aligned(owner_of(place_ref[0], s), tile_rows)
            act_s[c, rows, :] = inputs[s][0, c]
            grad_s[c, rows, :] = inputs[s][1, c]
        acts = act_s[c]
        grads = grad_s[c]
        acts_t = acts.T
        act_t_s[c] = acts_t
        natural = dot(acts, w_all_ref[:, : 3 * proj])
        across = dot(w_all_t_ref[...], acts_t)
        queries_t = (across[:proj] * scale).astype(BF16)
        kv_t = across[proj : 3 * proj].astype(BF16)
        gate_t = 1.0 / (1.0 + jnp.exp(-across[3 * proj :]))
        d_gated_t = dot(w_out_ref[...], grads.T)
        d_att_t = (d_gated_t * gate_t).astype(BF16)
        gate_t_s[c] = gate_t
        d_gated_t_s[c] = d_gated_t
        squares = lambda x: jnp.max(
            jnp.sum(jnp.square(x.astype(F32)).reshape(heads, head_dim, -1), axis=1)
        )
        bound = jnp.maximum(bound, squares(queries_t) * squares(kv_t[:proj]))
        queries = (natural[:, :proj] * scale).astype(BF16)
        kv = natural[:, proj:].astype(BF16)
        zero = jnp.zeros((size, proj), BF16)
        for b in range(blocks):
            kv_s[c, b] = kv[span[b]]
            kv_t_s[c, b] = kv_t[:, span[b]]
            d_att = d_att_t[:, span[b]].T
            for h in range(heads):
                w_score_s[c, b, own[h], head_lanes[h]] = queries_t[own[h], span[b]]
                w_probs_s[c, b, own[h], head_lanes[h]] = d_att_t[own[h], span[b]]
                here = lane_head == h
                query_s[c, b, h * size : (h + 1) * size, :] = jnp.where(here, queries[span[b]], zero)
                d_att_s[c, b, h * size : (h + 1) * size, :] = jnp.where(here, d_att, zero)
    d_kv_s[...] = jnp.zeros_like(d_kv_s)

    def query_block(b, live, shift):
        chosen = [tables_ref[b, e] for e in range(live)]
        strips = [
            (e, e * size + at, at) for e in range(live) for at in range(0, size, STRIP)
        ]
        rows_of = lambda x: jnp.sum(x.reshape(-1, 8, size), axis=0)
        for c in range(together):
            kv = jnp.concatenate([kv_s[c, k] for k in chosen], axis=0)
            score_s[c, : live * size, :] = dot(kv[:, :proj], w_score_s[c, b])
            d_probs_s[c, : live * size, :] = dot(kv[:, proj:], w_probs_s[c, b])
        for h in range(heads):
            lanes = head_lanes[h]
            stats = []
            for c in range(together):

                def scores(e, row, at):
                    return (
                        score_s[c, row : row + STRIP, lanes] * LOG2E
                        + bias_ref[chosen[e], b, h, at : at + STRIP, :]
                    )

                if shift:
                    peak = jnp.full((8, size), -jnp.inf, F32)
                    for strip in strips:
                        peak = jnp.maximum(
                            peak, jnp.max(scores(*strip).reshape(-1, 8, size), axis=0)
                        )
                    peak = jnp.max(peak, axis=0, keepdims=True)
                total = jnp.zeros((8, size), F32)
                mixed = jnp.zeros((8, size), F32)
                for e, row, at in strips:
                    value = scores(e, row, at)
                    weight = jnp.exp2(value - peak if shift else value)
                    total += rows_of(weight)
                    mixed += rows_of(weight * d_probs_s[c, row : row + STRIP, lanes])
                    score_s[c, row : row + STRIP, lanes] = weight
                norm = 1.0 / jnp.sum(total, axis=0, keepdims=True)
                stats.append((norm, jnp.sum(mixed, axis=0, keepdims=True) * norm))
            for e, row, at in strips:
                part = slice(row, row + STRIP)
                gathered = d_bias_s[b, e, h, at : at + STRIP, :]
                for c, (norm, delta) in enumerate(stats):
                    probs = score_s[c, part, lanes] * norm
                    d_scores = probs * (d_probs_s[c, part, lanes] - delta)
                    probs_s[c, part, lanes] = probs.astype(BF16)
                    ds_s[c, part, lanes] = d_scores.astype(BF16)
                    gathered += d_scores
                d_bias_s[b, e, h, at : at + STRIP, :] = gathered
        for c in range(together):
            kv_t = jnp.concatenate([kv_t_s[c, k] for k in chosen], axis=1)
            for h in range(0, heads, pair):
                lanes = slice(h * size, (h + pair) * size)
                both = slice(h * head_dim, (h + pair) * head_dim)
                low = slice(proj + both.start, proj + both.stop)
                att_t = dot(kv_t[low], probs_s[c, : live * size, lanes])
                d_query_t = dot(kv_t[both], ds_s[c, : live * size, lanes])
                for n in range(pair):
                    att_t_s[c, b, own[h + n], :] = att_t[own[n], head_lanes[n]]
                    d_query_t_s[c, b, own[h + n], :] = d_query_t[own[n], head_lanes[n]]
            d_values = dot(probs_s[c, : live * size, :], d_att_s[c, b])
            d_keys = dot(ds_s[c, : live * size, :], query_s[c, b])
            for e in range(live):
                part = slice(e * size, (e + 1) * size)
                d_kv_s[c, chosen[e], :, :proj] += d_keys[part]
                d_kv_s[c, chosen[e], :, proj:] += d_values[part]

    def all_blocks(shift):
        @pl.loop(0, blocks)
        def _(b):
            for live in range(1, slots + 1):

                @pl.when(lens_ref[b] == live)
                def _():
                    query_block(b, live, shift)

    small = bound <= SAFE_SCORE * SAFE_SCORE

    @pl.when(small)
    def _():
        all_blocks(False)

    @pl.when(jnp.logical_not(small))
    def _():
        all_blocks(True)

    w_qg = jnp.concatenate([w_all_ref[:, :proj], w_all_ref[:, 3 * proj :]], axis=1)
    for c in range(together):
        att_t = jnp.concatenate([att_t_s[c, b] for b in range(blocks)], axis=1)
        d_query_t = jnp.concatenate([d_query_t_s[c, b] for b in range(blocks)], axis=1)
        gate_t = gate_t_s[c]
        gated_t = (gate_t * att_t).astype(BF16)
        d_gpre_t = (d_gated_t_s[c] * att_t * gate_t * (1.0 - gate_t)).astype(BF16)
        d_qg_t = jnp.concatenate([(d_query_t * scale).astype(BF16), d_gpre_t], axis=0)
        d_kv = d_kv_s[c].reshape(tokens, 2 * proj).astype(BF16)
        d_pair = dot(d_kv, w_all_t_ref[proj : 3 * proj, :]) + dot(w_qg, d_qg_t).T
        d_pair_s[c] = d_pair
        for s in range(pieces):
            d_pair_out[s][c] = d_pair_s[c, aligned(owner_of(place_ref[0], s), tile_rows), :].astype(BF16)
        dw_qg_s[...] += dot(d_qg_t, act_s[c])
        dw_kv_s[...] += dot(act_t_s[c], d_kv)
        dwo_s[...] += dot(gated_t, grad_s[c])

    if not last:
        return

    @pl.when(step == pl.num_programs(0) - 1)
    def _():
        weights = [dw_qg_s[:proj, :].T, dw_kv_s[:, :proj], dw_kv_s[:, proj:], dw_qg_s[proj:, :].T]
        weights.append(dwo_s[...])
        far, each = keep_out.shape[0], keep_out.shape[1]
        tile = each // (slots * heads)
        for n, w in enumerate(weights):
            d_w_out[n * chan : (n + 1) * chan, :] = w
            message_out[far * each + n * chan : far * each + (n + 1) * chan, :] = w.astype(BF16)
        for mine in range(inner):

            @pl.when(place_ref[1] == mine)
            def _():
                for b in range(blocks):
                    for e in range(slots):
                        for h in range(heads):
                            turned = d_bias_s[b, e, h].astype(BF16).T
                            at = (e * heads + h) * tile
                            for sub in range(size // tile):
                                col = b * (size // tile) + sub
                                piece = turned[sub * tile : (sub + 1) * tile]
                                if col % inner == mine:
                                    keep_out[col // inner, at : at + tile, :] = piece
                                else:
                                    start = (col // inner) * each + at
                                    message_out[start : start + tile, :] = piece


def attention(
    pieces, bias, weights, tables, lens, place, rows, carried, last, query_tile, inner
):
    count = len(pieces)
    _, columns, tile_rows, chan = pieces[0].shape
    blocks, slots = tables.shape
    heads = bias.shape[2]
    proj = weights[-1].shape[0]
    tokens = tile_rows * count
    size = tokens // blocks
    together = math.gcd(TOGETHER, columns)
    dims = (count, heads, proj // heads, blocks, size, slots, together, inner)
    first = carried is None
    far = tokens // query_tile // inner

    def whole(x):
        return pl.BlockSpec(
            x.shape, lambda j, *_: (0,) * len(x.shape), pipeline_mode=pl.Buffered(1)
        )

    sums = [
        ((blocks, slots, heads, size, size), F32),
        ((2 * proj, chan), F32),
        ((chan, 2 * proj), F32),
        ((proj, chan), F32),
    ]
    if last:
        each = slots * heads * query_tile
        results = [
            ((far, each, size), BF16),
            ((far * each + 5 * chan, size), BF16),
            ((5 * chan, proj), F32),
        ]
    else:
        results = sums
    results = [((columns, tile_rows, chan), BF16)] * count + results
    results = [jax.ShapeDtypeStruct(*x) for x in results]
    scratch = [
        ((chan, 4 * proj), BF16),
        ((4 * proj, chan), BF16),
        ((together, tokens, chan), BF16),
        ((together, tokens, chan), BF16),
        ((together, tokens, chan), F32),
        ((together, chan, tokens), BF16),
        ((together, blocks, size, 2 * proj), BF16),
        ((together, blocks, 2 * proj, size), BF16),
        ((together, blocks, proj, heads * size), BF16),
        ((together, blocks, proj, heads * size), BF16),
        ((together, blocks, heads * size, proj), BF16),
        ((together, blocks, heads * size, proj), BF16),
        ((together, proj, tokens), F32),
        ((together, proj, tokens), F32),
        ((together, slots * size, heads * size), F32),
        ((together, slots * size, heads * size), F32),
        ((together, slots * size, heads * size), BF16),
        ((together, slots * size, heads * size), BF16),
        ((together, blocks, size, 2 * proj), F32),
        ((together, blocks, proj, size), F32),
        ((together, blocks, proj, size), F32),
    ]
    scratch = [pltpu.VMEM(*x) for x in (sums if last else []) + scratch]
    fixed = [bias, *weights] + ([] if first else list(carried))
    scalars = [tables, lens, place]
    pairs = tokens * size * slots * heads
    outs = pl.pallas_call(
        functools.partial(attention_kernel, dims, first, last, rows.source_of),
        grid_spec=pltpu.PrefetchScalarGridSpec(
            num_scalar_prefetch=len(scalars),
            grid=(columns // together,),
            in_specs=[
                pl.BlockSpec((2, together, tile_rows, chan), lambda j, *_: (0, j, 0, 0))
            ] * count
            + [whole(x) for x in fixed],
            out_specs=[pl.BlockSpec((together, tile_rows, chan), lambda j, *_: (j, 0, 0))] * count
            + [whole(x) for x in results[count:]],
            scratch_shapes=scratch,
        ),
        out_shape=results,
        compiler_params=pltpu.CompilerParams(vmem_limit_bytes=VMEM_LIMIT),
        cost_estimate=pl.CostEstimate(
            flops=columns * pairs * 7000,
            bytes_accessed=columns * tokens * chan * 6 + 10 * 2**20,
            transcendentals=columns * pairs,
        ),
    )(*scalars, *pieces, *fixed)
    return outs[:count], outs[count:]


def small_call(body, scalars, arrays, results, scratch=()):
    return pl.pallas_call(
        body,
        in_specs=[pl.BlockSpec(memory_space=pltpu.SMEM)] * len(scalars)
        + [pl.BlockSpec(memory_space=pltpu.VMEM)] * len(arrays),
        out_specs=[pl.BlockSpec(memory_space=pltpu.VMEM)] * len(results),
        out_shape=[jax.ShapeDtypeStruct(*x) for x in results],
        scratch_shapes=list(scratch),
        compiler_params=pltpu.CompilerParams(vmem_limit_bytes=SMALL_LIMIT),
    )(*scalars, *arrays)


def aligned(index, count):
    return pl.ds(pl.multiple_of(index * count, count), count)


def split_by_far(place, peers, keep, came, weights):
    far, each, lanes = keep.shape
    share = weights.shape[0] // far

    def body(place_ref, keep_ref, came_ref, weights_ref, own_ref, *message_refs):
        for s in range(far):
            t = peers.step(place_ref[2], s)
            out = message_refs[s - 1] if s else own_ref
            bias = keep_ref[t].astype(F32)
            weight = weights_ref[aligned(t, share), :].astype(BF16).astype(F32)
            if came_ref is not None:
                bias += came_ref[aligned(t, each), :].astype(F32)
                rest = came_ref[far * each :, :].astype(F32)
                half = jnp.zeros_like(weight)
                for u in range(far):
                    half = jnp.where(t == u, rest[u * share : (u + 1) * share], half)
                weight += half
            out[:each, :] = bias.astype(out.dtype)
            out[each:, :] = weight.astype(out.dtype)

    results = [((each + share, lanes), F32 if s == 0 else BF16) for s in range(far)]
    return small_call(body, [place], [keep, came, weights], results)


def split_by_row(place, tables, lens, peers, own, came, dims):
    slots, per_block, each, block_of = dims
    rows = peers.count
    lanes = own.shape[1]
    part = each // slots
    share = own.shape[0] - each

    def body(place_ref, tables_ref, lens_ref, own_ref, *refs):
        block = block_of(place_ref)
        came_refs, outs = refs[: len(came)], refs[len(came) :]
        weight = own_ref[each:, :]
        for ref in came_refs:
            weight += ref[each:, :].astype(F32)
        for s in range(rows):
            outs[s][part:, :] = weight.astype(BF16).astype(outs[s].dtype)
            outs[s][:part, :] = jnp.zeros((part, lanes), outs[s].dtype)
        for e in range(slots):
            at = slice(e * part, (e + 1) * part)
            bias = own_ref[at, :]
            for ref in came_refs:
                bias += ref[at, :].astype(F32)
            for s in range(rows):
                owner = peers.step(place_ref[0], s)
                hit = (tables_ref[block, e] == owner // per_block) & (e < lens_ref[block])

                @pl.when(hit)
                def _():
                    outs[s][:part, :] = bias.astype(outs[s].dtype)

    results = [((part + share, lanes), F32 if s == 0 else BF16) for s in range(rows)]
    return small_call(body, [place, tables, lens], [own, *came], results)


def add_rows(own, came, part):
    share, lanes = own.shape[0] - part, own.shape[1]

    def body(own_ref, *refs):
        came_refs, (bias_ref, weight_ref) = refs[: len(came)], refs[len(came) :]
        terms = [own_ref[...]] + [ref[...].astype(F32) for ref in came_refs]
        while len(terms) > 1:
            terms = [sum(terms[n : n + 2]) for n in range(0, len(terms), 2)]
        total = terms[0]
        bias_ref[...] = total[:part]
        weight_ref[...] = total[part:].astype(BF16)

    results = [((part, lanes), F32), ((share, lanes), BF16)]
    return small_call(body, [], [own, *came], results)


def place_weights(place, peers, parts, count):
    share, lanes = parts[0].shape

    def body(place_ref, *refs):
        part_refs, out_refs, scratch = refs[: len(parts)], refs[len(parts) : -1], refs[-1]
        for s, ref in enumerate(part_refs):
            scratch[aligned(peers.source_of(place_ref[2], s), share), :] = ref[...].astype(F32)
        for n, ref in enumerate(out_refs):
            ref[...] = scratch[n * lanes : (n + 1) * lanes, :]

    rows = share * len(parts)
    results = [((rows // count, lanes), F32)] * count
    return small_call(body, [place], parts, results, [pltpu.VMEM((rows, lanes), F32)])


class Peers:
    def __init__(self, axis, stride, count):
        self.axis, self.count = axis, count
        self.paired = count & (count - 1) == 0
        place = lax.axis_index(axis)
        self.digit = place // stride % count
        everyone = range(lax.axis_size(axis))
        self.routes = []
        for s in range(count):
            route = []
            for p in everyone:
                d = p // stride % count
                route.append((p, p + (self.step(d, s) - d) * stride))
            self.routes.append(route)

    def step(self, digit, s):
        return digit ^ s if self.paired else (digit + s) % self.count

    def target(self, s):
        return self.step(self.digit, s)

    def source_of(self, digit, s):
        return self.step(digit, s) if self.paired else (digit + self.count - s) % self.count

    def came_at(self, digit, source):
        return digit ^ source if self.paired else (digit + self.count - source) % self.count

    def send(self, x, s, home=False):
        route = self.routes[s]
        if home:
            route = [(t, f) for f, t in route]
        return x if s == 0 else lax.ppermute(x, self.axis, route)

    def gather(self, x):
        return jnp.stack([self.send(x, s) for s in range(self.count)])

    def swap(self, messages):
        return [self.send(x, s + 1) for s, x in enumerate(messages)]


def on_device(
    pair_act, out_grad, tri_bias, w_query, w_key, w_value, w_gate, w_out, key_blocks, list_len
):
    row_count = lax.axis_size("row")
    col_count = lax.axis_size("col")
    tile_rows, tile_cols, chan = pair_act.shape
    heads = tri_bias.shape[0]
    query_tile = tri_bias.shape[2]
    proj = w_query.shape[1]
    blocks, slots = key_blocks.shape
    tokens = tile_rows * row_count
    size = tokens // blocks
    col_width = tile_cols // row_count
    chunks = math.gcd(CHUNKS, col_width)
    width = col_width // chunks
    inner = math.gcd(2, col_count)
    rows = Peers("row", 1, row_count)
    near = Peers("col", 1, inner)
    far = Peers("col", inner, col_count // inner)

    gathered = rows.gather(jnp.transpose(tri_bias, (0, 2, 1)))
    both = jnp.stack([pair_act, out_grad]).reshape(2, tile_rows, row_count, chunks, width, chan)
    both = jnp.transpose(both, (2, 3, 0, 4, 1, 5))
    outgoing = [
        [
            lax.dynamic_index_in_dim(both[:, c], rows.target(s), 0, keepdims=False)
            for s in range(row_count)
        ]
        for c in range(chunks)
    ]
    gathered, outgoing = lax.optimization_barrier((gathered, outgoing))
    arrived = [[rows.send(x, s) for s, x in enumerate(outgoing[0])]]
    gathered, arrived[0], outgoing[1:] = lax.optimization_barrier(
        (far.gather(gathered), arrived[0], outgoing[1:])
    )
    place = jnp.stack([rows.digit, near.digit, far.digit]).astype(jnp.int32)
    halves = [near.send(gathered, s) for s in range(inner)]
    bias = shifted_bias(halves, key_blocks, list_len, place, rows, far)
    projections = [w_query, w_key, w_value, w_gate, w_out]
    arrived += [[rows.send(x, s) for s, x in enumerate(part)] for part in outgoing[1:]]
    carried = None
    returned = []
    for c in range(chunks):
        d_pieces, carried = attention(
            arrived[c], bias, projections, key_blocks, list_len, place, rows, carried,
            c == chunks - 1, query_tile, inner,
        )
        if c < chunks - 1:
            d_pieces = [rows.send(x, s, home=True) for s, x in enumerate(d_pieces)]
        returned.append(d_pieces)
    keep, message, w_part = carried
    message, returned[:-1] = lax.optimization_barrier((message, returned[:-1]))

    each = keep.shape[1]
    own, *messages = split_by_far(place, far, keep, near.send(message, inner - 1), w_part)
    messages, returned[-1] = lax.optimization_barrier((messages, returned[-1]))
    came = far.swap(messages)
    returned[-1] = [rows.send(x, s, home=True) for s, x in enumerate(returned[-1])]
    per_block = size // tile_rows
    block_of = lambda at: (at[2] * inner + at[1]) * query_tile // size
    own, *messages = split_by_row(
        place, key_blocks, list_len, rows, own, came, (slots, per_block, each, block_of)
    )
    d_bias, w_part = add_rows(own, rows.swap(messages), each // slots)
    weights = place_weights(place, far, [far.send(w_part, s) for s in range(far.count)], 5)
    d_bias = d_bias.reshape(heads, query_tile, per_block, tile_rows)
    d_bias = lax.dynamic_index_in_dim(d_bias, rows.digit % per_block, 2, keepdims=False)


    d_pair = jnp.zeros((tile_rows, tile_cols, chan), BF16)
    for c, part in enumerate(returned):
        for s, x in enumerate(part):
            at = rows.target(s) * col_width + c * width
            d_pair = lax.dynamic_update_slice(d_pair, jnp.transpose(x, (1, 0, 2)), (0, at, 0))
    return (d_pair, jnp.transpose(d_bias, (0, 2, 1)), *weights)


def solution(mesh):
    in_specs = (
        P("row", "col", None),
        P("row", "col", None),
        P(None, "row", "col"),
        P(),
        P(),
        P(),
        P(),
        P(),
        P(),
        P(),
    )
    out_specs = (P("row", "col", None), P(None, "row", "col"), P(), P(), P(), P(), P())
    return jax.shard_map(
        on_device, mesh=mesh, in_specs=in_specs, out_specs=out_specs, check_vma=False
    )
```

```python
import functools
import math

import jax
import jax.numpy as jnp
from jax import lax
from jax.experimental import pallas as pl
from jax.experimental.pallas import tpu as pltpu
from jax.sharding import PartitionSpec as P

F32 = jnp.float32
BF16 = jnp.bfloat16
CHUNKS = 2
TOGETHER = 2
STRIP = 32
LOG2E = math.log2(math.e)
SAFE_SCORE = 30.0
VMEM_LIMIT = 32 * 1024 * 1024
SMALL_LIMIT = 16 * 1024 * 1024


def dot(a, b):
    return jnp.dot(a, b, preferred_element_type=F32)


def bias_kernel(inner, came_at, tables_ref, lens_ref, place_ref, *refs):
    *parts, out_ref = refs
    b = pl.program_id(0)
    blocks, _, heads, size, _ = out_ref.shape
    slots = tables_ref.shape[1]
    _, rows, _, query_tile, tile = parts[0].shape
    per_block = size // tile
    subs = size // query_tile
    for h in range(heads):
        for r in range(rows):
            at = came_at(place_ref[0], r)
            pieces = [p[0, at, h] for p in parts]
            if inner > 1:
                own, other = pieces[:subs], pieces[subs:]
                near = [(b * subs + n) % inner == place_ref[1] for n in range(subs)]
                pieces = [jnp.where(*x) for x in zip(near, own, other)]
            start = (r % per_block) * tile
            out_ref[r // per_block, 0, h, start : start + tile, :] = (
                jnp.concatenate(pieces, axis=0).T.astype(F32)
            )
    for h in range(heads):
        peak = jnp.max(out_ref[tables_ref[b, 0], 0, h], axis=0, keepdims=True)
        for e in range(1, slots):
            other = jnp.max(out_ref[tables_ref[b, e], 0, h], axis=0, keepdims=True)
            peak = jnp.where(e < lens_ref[b], jnp.maximum(peak, other), peak)
        for kb in range(blocks):
            out_ref[kb, 0, h] = (out_ref[kb, 0, h] - peak) * LOG2E


def shifted_bias(halves, key_blocks, list_len, place, rows, far):
    _, row_count, heads, query_tile, key_tile = halves[0].shape
    inner = len(halves)
    blocks = key_blocks.shape[0]
    size = inner * far.count * query_tile // blocks
    subs = size // query_tile

    def part(sub):
        return pl.BlockSpec(
            (1, row_count, heads, query_tile, key_tile),
            lambda b, tables, lens, at: (
                far.came_at(at[2], (b * subs + sub) // inner), 0, 0, 0, 0
            ),
        )

    return pl.pallas_call(
        functools.partial(bias_kernel, inner, rows.came_at),
        grid_spec=pltpu.PrefetchScalarGridSpec(
            num_scalar_prefetch=3,
            grid=(blocks,),
            in_specs=[part(sub) for _ in halves for sub in range(subs)],
            out_specs=pl.BlockSpec((blocks, 1, heads, size, size), lambda b, *_: (0, b, 0, 0, 0)),
        ),
        out_shape=jax.ShapeDtypeStruct((blocks, blocks, heads, size, size), F32),
        compiler_params=pltpu.CompilerParams(vmem_limit_bytes=SMALL_LIMIT),
    )(key_blocks, list_len, place, *[x for x in halves for _ in range(subs)])


def attention_kernel(dims, first, last, owner_of, tables_ref, lens_ref, place_ref, *refs):
    pieces, heads, head_dim, blocks, size, slots, together, inner = dims
    refs = list(refs)
    take = lambda n: [refs.pop(0) for _ in range(n)]
    inputs = take(pieces)
    bias_ref, *w_refs, w_out_ref = take(6)
    carried = [] if first else take(4)
    d_pair_out = take(pieces)
    if last:
        keep_out, message_out, d_w_out = take(3)
    d_bias_s, dw_qg_s, dw_kv_s, dwo_s = sums = take(4)
    (w_all_ref, w_all_t_ref, act_s, grad_s, d_pair_s, act_t_s, kv_s, kv_t_s, w_score_s, w_probs_s, d_att_s, query_s, gate_t_s, d_gated_t_s,
     score_s, d_probs_s, probs_s, ds_s, d_kv_s, att_t_s, d_query_t_s) = refs
    proj = heads * head_dim
    scale = head_dim ** (-0.5)
    tile_rows, chan = inputs[0].shape[2:]
    tokens = blocks * size
    step = pl.program_id(0)
    span = [slice(b * size, (b + 1) * size) for b in range(blocks)]
    own = [slice(h * head_dim, (h + 1) * head_dim) for h in range(heads)]
    pair = math.gcd(2, heads)
    head_lanes = [slice(h * size, (h + 1) * size) for h in range(heads)]

    @pl.when(step == 0)
    def _():
        for n, ref in enumerate(w_refs):
            w_all_ref[:, n * proj : (n + 1) * proj] = ref[...]
            w_all_t_ref[n * proj : (n + 1) * proj, :] = ref[...].T
        w_score_s[...] = jnp.zeros_like(w_score_s)
        w_probs_s[...] = jnp.zeros_like(w_probs_s)
        for n, ref in enumerate(sums):
            ref[...] = jnp.zeros_like(ref) if first else carried[n][...]

    lane_head = lax.broadcasted_iota(jnp.int32, (size, proj), 1) // head_dim
    bound = jnp.float32(0.0)
    for c in range(together):
        for s in range(pieces):
            rows = aligned(owner_of(place_ref[0], s), tile_rows)
            act_s[c, rows, :] = inputs[s][0, c]
            grad_s[c, rows, :] = inputs[s][1, c]
        acts = act_s[c]
        grads = grad_s[c]
        acts_t = acts.T
        act_t_s[c] = acts_t
        natural = dot(acts, w_all_ref[:, : 3 * proj])
        across = dot(w_all_t_ref[...], acts_t)
        queries_t = (across[:proj] * scale).astype(BF16)
        kv_t = across[proj : 3 * proj].astype(BF16)
        gate_t = 1.0 / (1.0 + jnp.exp(-across[3 * proj :]))
        d_gated_t = dot(w_out_ref[...], grads.T)
        d_att_t = (d_gated_t * gate_t).astype(BF16)
        gate_t_s[c] = gate_t
        d_gated_t_s[c] = d_gated_t
        squares = lambda x: jnp.max(
            jnp.sum(jnp.square(x.astype(F32)).reshape(heads, head_dim, -1), axis=1)
        )
        bound = jnp.maximum(bound, squares(queries_t) * squares(kv_t[:proj]))
        queries = (natural[:, :proj] * scale).astype(BF16)
        kv = natural[:, proj:].astype(BF16)
        zero = jnp.zeros((size, proj), BF16)
        for b in range(blocks):
            kv_s[c, b] = kv[span[b]]
            kv_t_s[c, b] = kv_t[:, span[b]]
            d_att = d_att_t[:, span[b]].T
            for h in range(heads):
                w_score_s[c, b, own[h], head_lanes[h]] = queries_t[own[h], span[b]]
                w_probs_s[c, b, own[h], head_lanes[h]] = d_att_t[own[h], span[b]]
                here = lane_head == h
                query_s[c, b, h * size : (h + 1) * size, :] = jnp.where(here, queries[span[b]], zero)
                d_att_s[c, b, h * size : (h + 1) * size, :] = jnp.where(here, d_att, zero)
    d_kv_s[...] = jnp.zeros_like(d_kv_s)

    def query_block(b, live, shift):
        chosen = [tables_ref[b, e] for e in range(live)]
        strips = [
            (e, e * size + at, at) for e in range(live) for at in range(0, size, STRIP)
        ]
        rows_of = lambda x: jnp.sum(x.reshape(-1, 8, size), axis=0)
        for c in range(together):
            kv = jnp.concatenate([kv_s[c, k] for k in chosen], axis=0)
            score_s[c, : live * size, :] = dot(kv[:, :proj], w_score_s[c, b])
            d_probs_s[c, : live * size, :] = dot(kv[:, proj:], w_probs_s[c, b])
        for h in range(heads):
            lanes = head_lanes[h]
            stats = []
            for c in range(together):

                def scores(e, row, at):
                    return (
                        score_s[c, row : row + STRIP, lanes] * LOG2E
                        + bias_ref[chosen[e], b, h, at : at + STRIP, :]
                    )

                if shift:
                    peak = jnp.full((8, size), -jnp.inf, F32)
                    for strip in strips:
                        peak = jnp.maximum(
                            peak, jnp.max(scores(*strip).reshape(-1, 8, size), axis=0)
                        )
                    peak = jnp.max(peak, axis=0, keepdims=True)
                total = jnp.zeros((8, size), F32)
                mixed = jnp.zeros((8, size), F32)
                for e, row, at in strips:
                    value = scores(e, row, at)
                    weight = jnp.exp2(value - peak if shift else value)
                    total += rows_of(weight)
                    mixed += rows_of(weight * d_probs_s[c, row : row + STRIP, lanes])
                    score_s[c, row : row + STRIP, lanes] = weight
                norm = 1.0 / jnp.sum(total, axis=0, keepdims=True)
                stats.append((norm, jnp.sum(mixed, axis=0, keepdims=True) * norm))
            for e, row, at in strips:
                part = slice(row, row + STRIP)
                gathered = d_bias_s[b, e, h, at : at + STRIP, :]
                for c, (norm, delta) in enumerate(stats):
                    probs = score_s[c, part, lanes] * norm
                    d_scores = probs * (d_probs_s[c, part, lanes] - delta)
                    probs_s[c, part, lanes] = probs.astype(BF16)
                    ds_s[c, part, lanes] = d_scores.astype(BF16)
                    gathered += d_scores
                d_bias_s[b, e, h, at : at + STRIP, :] = gathered
        for c in range(together):
            kv_t = jnp.concatenate([kv_t_s[c, k] for k in chosen], axis=1)
            for h in range(0, heads, pair):
                lanes = slice(h * size, (h + pair) * size)
                both = slice(h * head_dim, (h + pair) * head_dim)
                low = slice(proj + both.start, proj + both.stop)
                att_t = dot(kv_t[low], probs_s[c, : live * size, lanes])
                d_query_t = dot(kv_t[both], ds_s[c, : live * size, lanes])
                for n in range(pair):
                    att_t_s[c, b, own[h + n], :] = att_t[own[n], head_lanes[n]]
                    d_query_t_s[c, b, own[h + n], :] = d_query_t[own[n], head_lanes[n]]
            d_values = dot(probs_s[c, : live * size, :], d_att_s[c, b])
            d_keys = dot(ds_s[c, : live * size, :], query_s[c, b])
            for e in range(live):
                part = slice(e * size, (e + 1) * size)
                d_kv_s[c, chosen[e], :, :proj] += d_keys[part]
                d_kv_s[c, chosen[e], :, proj:] += d_values[part]

    def all_blocks(shift):
        @pl.loop(0, blocks)
        def _(b):
            for live in range(1, slots + 1):

                @pl.when(lens_ref[b] == live)
                def _():
                    query_block(b, live, shift)

    small = bound <= SAFE_SCORE * SAFE_SCORE

    @pl.when(small)
    def _():
        all_blocks(False)

    @pl.when(jnp.logical_not(small))
    def _():
        all_blocks(True)

    w_qg = jnp.concatenate([w_all_ref[:, :proj], w_all_ref[:, 3 * proj :]], axis=1)
    for c in range(together):
        att_t = jnp.concatenate([att_t_s[c, b] for b in range(blocks)], axis=1)
        d_query_t = jnp.concatenate([d_query_t_s[c, b] for b in range(blocks)], axis=1)
        gate_t = gate_t_s[c]
        gated_t = (gate_t * att_t).astype(BF16)
        d_gpre_t = (d_gated_t_s[c] * att_t * gate_t * (1.0 - gate_t)).astype(BF16)
        d_qg_t = jnp.concatenate([(d_query_t * scale).astype(BF16), d_gpre_t], axis=0)
        d_kv = d_kv_s[c].reshape(tokens, 2 * proj).astype(BF16)
        d_pair = dot(d_kv, w_all_t_ref[proj : 3 * proj, :]) + dot(w_qg, d_qg_t).T
        d_pair_s[c] = d_pair
        for s in range(pieces):
            d_pair_out[s][c] = d_pair_s[c, aligned(owner_of(place_ref[0], s), tile_rows), :].astype(BF16)
        dw_qg_s[...] += dot(d_qg_t, act_s[c])
        dw_kv_s[...] += dot(act_t_s[c], d_kv)
        dwo_s[...] += dot(gated_t, grad_s[c])

    if not last:
        return

    @pl.when(step == pl.num_programs(0) - 1)
    def _():
        weights = [dw_qg_s[:proj, :].T, dw_kv_s[:, :proj], dw_kv_s[:, proj:], dw_qg_s[proj:, :].T]
        weights.append(dwo_s[...])
        far, each = keep_out.shape[0], keep_out.shape[1]
        tile = each // (slots * heads)
        for n, w in enumerate(weights):
            d_w_out[n * chan : (n + 1) * chan, :] = w
            message_out[far * each + n * chan : far * each + (n + 1) * chan, :] = w.astype(BF16)
        for mine in range(inner):

            @pl.when(place_ref[1] == mine)
            def _():
                for b in range(blocks):
                    for e in range(slots):
                        for h in range(heads):
                            turned = d_bias_s[b, e, h].astype(BF16).T
                            at = (e * heads + h) * tile
                            for sub in range(size // tile):
                                col = b * (size // tile) + sub
                                piece = turned[sub * tile : (sub + 1) * tile]
                                if col % inner == mine:
                                    keep_out[col // inner, at : at + tile, :] = piece
                                else:
                                    start = (col // inner) * each + at
                                    message_out[start : start + tile, :] = piece


def attention(
    pieces, bias, weights, tables, lens, place, rows, carried, last, query_tile, inner
):
    count = len(pieces)
    _, columns, tile_rows, chan = pieces[0].shape
    blocks, slots = tables.shape
    heads = bias.shape[2]
    proj = weights[-1].shape[0]
    tokens = tile_rows * count
    size = tokens // blocks
    together = math.gcd(TOGETHER, columns)
    dims = (count, heads, proj // heads, blocks, size, slots, together, inner)
    first = carried is None
    far = tokens // query_tile // inner

    whole = pl.BlockSpec(memory_space=pltpu.VMEM)
    sums = [
        ((blocks, slots, heads, size, size), F32),
        ((2 * proj, chan), F32),
        ((chan, 2 * proj), F32),
        ((proj, chan), F32),
    ]
    if last:
        each = slots * heads * query_tile
        results = [
            ((far, each, size), BF16),
            ((far * each + 5 * chan, size), BF16),
            ((5 * chan, proj), F32),
        ]
    else:
        results = sums
    results = [((columns, tile_rows, chan), BF16)] * count + results
    results = [jax.ShapeDtypeStruct(*x) for x in results]
    scratch = [
        ((chan, 4 * proj), BF16),
        ((4 * proj, chan), BF16),
        ((together, tokens, chan), BF16),
        ((together, tokens, chan), BF16),
        ((together, tokens, chan), F32),
        ((together, chan, tokens), BF16),
        ((together, blocks, size, 2 * proj), BF16),
        ((together, blocks, 2 * proj, size), BF16),
        ((together, blocks, proj, heads * size), BF16),
        ((together, blocks, proj, heads * size), BF16),
        ((together, blocks, heads * size, proj), BF16),
        ((together, blocks, heads * size, proj), BF16),
        ((together, proj, tokens), F32),
        ((together, proj, tokens), F32),
        ((together, slots * size, heads * size), F32),
        ((together, slots * size, heads * size), F32),
        ((together, slots * size, heads * size), BF16),
        ((together, slots * size, heads * size), BF16),
        ((together, blocks, size, 2 * proj), F32),
        ((together, blocks, proj, size), F32),
        ((together, blocks, proj, size), F32),
    ]
    scratch = [pltpu.VMEM(*x) for x in (sums if last else []) + scratch]
    fixed = [bias, *weights] + ([] if first else list(carried))
    scalars = [tables, lens, place]
    pairs = tokens * size * slots * heads
    outs = pl.pallas_call(
        functools.partial(attention_kernel, dims, first, last, rows.source_of),
        grid_spec=pltpu.PrefetchScalarGridSpec(
            num_scalar_prefetch=len(scalars),
            grid=(columns // together,),
            in_specs=[
                pl.BlockSpec((2, together, tile_rows, chan), lambda j, *_: (0, j, 0, 0))
            ] * count
            + [whole] * len(fixed),
            out_specs=[pl.BlockSpec((together, tile_rows, chan), lambda j, *_: (j, 0, 0))] * count
            + [whole] * len(results[count:]),
            scratch_shapes=scratch,
        ),
        out_shape=results,
        compiler_params=pltpu.CompilerParams(vmem_limit_bytes=VMEM_LIMIT),
        cost_estimate=pl.CostEstimate(
            flops=columns * pairs * 7000,
            bytes_accessed=columns * tokens * chan * 6 + 10 * 2**20,
            transcendentals=columns * pairs,
        ),
    )(*scalars, *pieces, *fixed)
    return outs[:count], outs[count:]


def small_call(body, scalars, arrays, results, scratch=()):
    return pl.pallas_call(
        body,
        in_specs=[pl.BlockSpec(memory_space=pltpu.SMEM)] * len(scalars)
        + [pl.BlockSpec(memory_space=pltpu.VMEM)] * len(arrays),
        out_specs=[pl.BlockSpec(memory_space=pltpu.VMEM)] * len(results),
        out_shape=[jax.ShapeDtypeStruct(*x) for x in results],
        scratch_shapes=list(scratch),
        compiler_params=pltpu.CompilerParams(vmem_limit_bytes=SMALL_LIMIT),
    )(*scalars, *arrays)


def aligned(index, count):
    return pl.ds(pl.multiple_of(index * count, count), count)


def split_by_far(place, peers, keep, came, weights):
    far, each, lanes = keep.shape
    share = weights.shape[0] // far

    def body(place_ref, keep_ref, came_ref, weights_ref, own_ref, *message_refs):
        for s in range(far):
            t = peers.step(place_ref[2], s)
            out = message_refs[s - 1] if s else own_ref
            bias = keep_ref[t].astype(F32)
            weight = weights_ref[aligned(t, share), :].astype(BF16).astype(F32)
            if came_ref is not None:
                bias += came_ref[aligned(t, each), :].astype(F32)
                rest = came_ref[far * each :, :].astype(F32)
                half = jnp.zeros_like(weight)
                for u in range(far):
                    half = jnp.where(t == u, rest[u * share : (u + 1) * share], half)
                weight += half
            out[:each, :] = bias.astype(out.dtype)
            out[each:, :] = weight.astype(out.dtype)

    results = [((each + share, lanes), F32 if s == 0 else BF16) for s in range(far)]
    return small_call(body, [place], [keep, came, weights], results)


def split_by_row(place, tables, lens, peers, own, came, dims):
    slots, per_block, each, block_of = dims
    rows = peers.count
    lanes = own.shape[1]
    part = each // slots
    share = own.shape[0] - each

    def body(place_ref, tables_ref, lens_ref, own_ref, *refs):
        block = block_of(place_ref)
        came_refs, outs = refs[: len(came)], refs[len(came) :]
        weight = own_ref[each:, :]
        for ref in came_refs:
            weight += ref[each:, :].astype(F32)
        for s in range(rows):
            outs[s][part:, :] = weight.astype(BF16).astype(outs[s].dtype)
            outs[s][:part, :] = jnp.zeros((part, lanes), outs[s].dtype)
        for e in range(slots):
            at = slice(e * part, (e + 1) * part)
            bias = own_ref[at, :]
            for ref in came_refs:
                bias += ref[at, :].astype(F32)
            for s in range(rows):
                owner = peers.step(place_ref[0], s)
                hit = (tables_ref[block, e] == owner // per_block) & (e < lens_ref[block])

                @pl.when(hit)
                def _():
                    outs[s][:part, :] = bias.astype(outs[s].dtype)

    results = [((part + share, lanes), F32 if s == 0 else BF16) for s in range(rows)]
    return small_call(body, [place, tables, lens], [own, *came], results)


def add_rows(own, came, part):
    share, lanes = own.shape[0] - part, own.shape[1]

    def body(own_ref, *refs):
        came_refs, (bias_ref, weight_ref) = refs[: len(came)], refs[len(came) :]
        terms = [own_ref[...]] + [ref[...].astype(F32) for ref in came_refs]
        while len(terms) > 1:
            terms = [sum(terms[n : n + 2]) for n in range(0, len(terms), 2)]
        total = terms[0]
        bias_ref[...] = total[:part]
        weight_ref[...] = total[part:].astype(BF16)

    results = [((part, lanes), F32), ((share, lanes), BF16)]
    return small_call(body, [], [own, *came], results)


def place_weights(place, peers, parts, count):
    share, lanes = parts[0].shape

    def body(place_ref, *refs):
        part_refs, out_refs, scratch = refs[: len(parts)], refs[len(parts) : -1], refs[-1]
        for s, ref in enumerate(part_refs):
            scratch[aligned(peers.source_of(place_ref[2], s), share), :] = ref[...].astype(F32)
        for n, ref in enumerate(out_refs):
            ref[...] = scratch[n * lanes : (n + 1) * lanes, :]

    rows = share * len(parts)
    results = [((rows // count, lanes), F32)] * count
    return small_call(body, [place], parts, results, [pltpu.VMEM((rows, lanes), F32)])


class Peers:
    def __init__(self, axis, stride, count):
        self.axis, self.count = axis, count
        self.paired = count & (count - 1) == 0
        place = lax.axis_index(axis)
        self.digit = place // stride % count
        everyone = range(lax.axis_size(axis))
        self.routes = []
        for s in range(count):
            route = []
            for p in everyone:
                d = p // stride % count
                route.append((p, p + (self.step(d, s) - d) * stride))
            self.routes.append(route)

    def step(self, digit, s):
        return digit ^ s if self.paired else (digit + s) % self.count

    def target(self, s):
        return self.step(self.digit, s)

    def source_of(self, digit, s):
        return self.step(digit, s) if self.paired else (digit + self.count - s) % self.count

    def came_at(self, digit, source):
        return digit ^ source if self.paired else (digit + self.count - source) % self.count

    def send(self, x, s, home=False):
        route = self.routes[s]
        if home:
            route = [(t, f) for f, t in route]
        return x if s == 0 else lax.ppermute(x, self.axis, route)

    def gather(self, x):
        return jnp.stack([self.send(x, s) for s in range(self.count)])

    def swap(self, messages):
        return [self.send(x, s + 1) for s, x in enumerate(messages)]


def on_device(
    pair_act, out_grad, tri_bias, w_query, w_key, w_value, w_gate, w_out, key_blocks, list_len
):
    row_count = lax.axis_size("row")
    col_count = lax.axis_size("col")
    tile_rows, tile_cols, chan = pair_act.shape
    heads = tri_bias.shape[0]
    query_tile = tri_bias.shape[2]
    proj = w_query.shape[1]
    blocks, slots = key_blocks.shape
    tokens = tile_rows * row_count
    size = tokens // blocks
    col_width = tile_cols // row_count
    chunks = math.gcd(CHUNKS, col_width)
    width = col_width // chunks
    inner = math.gcd(2, col_count)
    rows = Peers("row", 1, row_count)
    near = Peers("col", 1, inner)
    far = Peers("col", inner, col_count // inner)

    gathered = rows.gather(jnp.transpose(tri_bias, (0, 2, 1)))
    both = jnp.stack([pair_act, out_grad]).reshape(2, tile_rows, row_count, chunks, width, chan)
    both = jnp.transpose(both, (2, 3, 0, 4, 1, 5))
    outgoing = [
        [
            lax.dynamic_index_in_dim(both[:, c], rows.target(s), 0, keepdims=False)
            for s in range(row_count)
        ]
        for c in range(chunks)
    ]
    gathered, outgoing = lax.optimization_barrier((gathered, outgoing))
    arrived = [[rows.send(x, s) for s, x in enumerate(outgoing[0])]]
    gathered, arrived[0], outgoing[1:] = lax.optimization_barrier(
        (far.gather(gathered), arrived[0], outgoing[1:])
    )
    place = jnp.stack([rows.digit, near.digit, far.digit]).astype(jnp.int32)
    halves = [near.send(gathered, s) for s in range(inner)]
    bias = shifted_bias(halves, key_blocks, list_len, place, rows, far)
    projections = [w_query, w_key, w_value, w_gate, w_out]
    arrived += [[rows.send(x, s) for s, x in enumerate(part)] for part in outgoing[1:]]
    carried = None
    returned = []
    for c in range(chunks):
        d_pieces, carried = attention(
            arrived[c], bias, projections, key_blocks, list_len, place, rows, carried,
            c == chunks - 1, query_tile, inner,
        )
        if c < chunks - 1:
            d_pieces = [rows.send(x, s, home=True) for s, x in enumerate(d_pieces)]
        returned.append(d_pieces)
    keep, message, w_part = carried
    message, returned[:-1] = lax.optimization_barrier((message, returned[:-1]))

    each = keep.shape[1]
    own, *messages = split_by_far(place, far, keep, near.send(message, inner - 1), w_part)
    messages, returned[-1] = lax.optimization_barrier((messages, returned[-1]))
    came = far.swap(messages)
    returned[-1] = [rows.send(x, s, home=True) for s, x in enumerate(returned[-1])]
    per_block = size // tile_rows
    block_of = lambda at: (at[2] * inner + at[1]) * query_tile // size
    own, *messages = split_by_row(
        place, key_blocks, list_len, rows, own, came, (slots, per_block, each, block_of)
    )
    d_bias, w_part = add_rows(own, rows.swap(messages), each // slots)
    weights = place_weights(place, far, [far.send(w_part, s) for s in range(far.count)], 5)
    d_bias = d_bias.reshape(heads, query_tile, per_block, tile_rows)
    d_bias = lax.dynamic_index_in_dim(d_bias, rows.digit % per_block, 2, keepdims=False)


    d_pair = jnp.zeros((tile_rows, tile_cols, chan), BF16)
    for c, part in enumerate(returned):
        for s, x in enumerate(part):
            at = rows.target(s) * col_width + c * width
            d_pair = lax.dynamic_update_slice(d_pair, jnp.transpose(x, (1, 0, 2)), (0, at, 0))
    return (d_pair, jnp.transpose(d_bias, (0, 2, 1)), *weights)


def solution(mesh):
    in_specs = (
        P("row", "col", None),
        P("row", "col", None),
        P(None, "row", "col"),
        P(),
        P(),
        P(),
        P(),
        P(),
        P(),
        P(),
    )
    out_specs = (P("row", "col", None), P(None, "row", "col"), P(), P(), P(), P(), P())
    return jax.shard_map(
        on_device, mesh=mesh, in_specs=in_specs, out_specs=out_specs, check_vma=False
    )
```

```python
import functools
import math

import jax
import jax.numpy as jnp
from jax import lax
from jax.experimental import pallas as pl
from jax.experimental.pallas import tpu as pltpu
from jax.sharding import PartitionSpec as P

F32 = jnp.float32
BF16 = jnp.bfloat16
CHUNKS = 2
TOGETHER = 2
STRIP = 32
LOG2E = math.log2(math.e)
SAFE_SCORE = 30.0
VMEM_LIMIT = 32 * 1024 * 1024
SMALL_LIMIT = 16 * 1024 * 1024


def dot(a, b):
    return jnp.dot(a, b, preferred_element_type=F32)


def bias_kernel(inner, came_at, tables_ref, lens_ref, place_ref, *refs):
    *parts, out_ref = refs
    b = pl.program_id(0)
    blocks, _, heads, size, _ = out_ref.shape
    slots = tables_ref.shape[1]
    _, rows, _, query_tile, tile = parts[0].shape
    per_block = size // tile
    subs = size // query_tile
    for h in range(heads):
        for r in range(rows):
            at = came_at(place_ref[0], r)
            pieces = [p[0, at, h] for p in parts]
            if inner > 1:
                own, other = pieces[:subs], pieces[subs:]
                near = [(b * subs + n) % inner == place_ref[1] for n in range(subs)]
                pieces = [jnp.where(*x) for x in zip(near, own, other)]
            start = (r % per_block) * tile
            out_ref[r // per_block, 0, h, start : start + tile, :] = (
                jnp.concatenate(pieces, axis=0).T.astype(F32)
            )
    for h in range(heads):
        peak = jnp.max(out_ref[tables_ref[b, 0], 0, h], axis=0, keepdims=True)
        for e in range(1, slots):
            other = jnp.max(out_ref[tables_ref[b, e], 0, h], axis=0, keepdims=True)
            peak = jnp.where(e < lens_ref[b], jnp.maximum(peak, other), peak)
        for kb in range(blocks):
            out_ref[kb, 0, h] = (out_ref[kb, 0, h] - peak) * LOG2E


def shifted_bias(halves, key_blocks, list_len, place, rows, far):
    _, row_count, heads, query_tile, key_tile = halves[0].shape
    inner = len(halves)
    blocks = key_blocks.shape[0]
    size = inner * far.count * query_tile // blocks
    subs = size // query_tile

    def part(sub):
        return pl.BlockSpec(
            (1, row_count, heads, query_tile, key_tile),
            lambda b, tables, lens, at: (
                far.came_at(at[2], (b * subs + sub) // inner), 0, 0, 0, 0
            ),
        )

    return pl.pallas_call(
        functools.partial(bias_kernel, inner, rows.came_at),
        grid_spec=pltpu.PrefetchScalarGridSpec(
            num_scalar_prefetch=3,
            grid=(blocks,),
            in_specs=[part(sub) for _ in halves for sub in range(subs)],
            out_specs=pl.BlockSpec((blocks, 1, heads, size, size), lambda b, *_: (0, b, 0, 0, 0)),
        ),
        out_shape=jax.ShapeDtypeStruct((blocks, blocks, heads, size, size), F32),
        compiler_params=pltpu.CompilerParams(vmem_limit_bytes=SMALL_LIMIT),
    )(key_blocks, list_len, place, *[x for x in halves for _ in range(subs)])


def attention_kernel(dims, first, last, owner_of, tables_ref, lens_ref, place_ref, *refs):
    pieces, heads, head_dim, blocks, size, slots, together, inner = dims
    refs = list(refs)
    take = lambda n: [refs.pop(0) for _ in range(n)]
    inputs = take(pieces)
    bias_ref, w_ref = take(2)
    carried = [] if first else take(4)
    d_pair_out = take(pieces)
    if last:
        keep_out, message_out, d_w_out = take(3)
    d_bias_s, dw_qg_s, dw_kv_s, dwo_s = sums = take(4)
    (w_all_ref, w_all_t_ref, act_s, grad_s, d_pair_s, act_t_s, kv_s, kv_t_s, w_score_s, w_probs_s, d_att_s, query_s, gate_t_s, d_gated_t_s,
     score_s, d_probs_s, probs_s, ds_s, d_kv_s, att_t_s, d_query_t_s) = refs
    proj = heads * head_dim
    scale = head_dim ** (-0.5)
    tile_rows, chan = inputs[0].shape[2:]
    tokens = blocks * size
    step = pl.program_id(0)
    span = [slice(b * size, (b + 1) * size) for b in range(blocks)]
    own = [slice(h * head_dim, (h + 1) * head_dim) for h in range(heads)]
    pair = math.gcd(2, heads)
    head_lanes = [slice(h * size, (h + 1) * size) for h in range(heads)]

    @pl.when(step == 0)
    def _():
        for n in range(4):
            w_all_ref[:, n * proj : (n + 1) * proj] = w_ref[n]
            w_all_t_ref[n * proj : (n + 1) * proj, :] = w_ref[n].T
        w_score_s[...] = jnp.zeros_like(w_score_s)
        w_probs_s[...] = jnp.zeros_like(w_probs_s)
        for n, ref in enumerate(sums):
            ref[...] = jnp.zeros_like(ref) if first else carried[n][...]

    lane_head = lax.broadcasted_iota(jnp.int32, (size, proj), 1) // head_dim
    bound = jnp.float32(0.0)
    for c in range(together):
        for s in range(pieces):
            rows = aligned(owner_of(place_ref[0], s), tile_rows)
            act_s[c, rows, :] = inputs[s][0, c]
            grad_s[c, rows, :] = inputs[s][1, c]
        acts = act_s[c]
        grads = grad_s[c]
        acts_t = acts.T
        act_t_s[c] = acts_t
        natural = dot(acts, w_all_ref[:, : 3 * proj])
        across = dot(w_all_t_ref[...], acts_t)
        queries_t = (across[:proj] * scale).astype(BF16)
        kv_t = across[proj : 3 * proj].astype(BF16)
        gate_t = 1.0 / (1.0 + jnp.exp(-across[3 * proj :]))
        d_gated_t = dot(w_ref[4], grads.T)
        d_att_t = (d_gated_t * gate_t).astype(BF16)
        gate_t_s[c] = gate_t
        d_gated_t_s[c] = d_gated_t
        squares = lambda x: jnp.max(
            jnp.sum(jnp.square(x.astype(F32)).reshape(heads, head_dim, -1), axis=1)
        )
        bound = jnp.maximum(bound, squares(queries_t) * squares(kv_t[:proj]))
        queries = (natural[:, :proj] * scale).astype(BF16)
        kv = natural[:, proj:].astype(BF16)
        zero = jnp.zeros((size, proj), BF16)
        for b in range(blocks):
            kv_s[c, b] = kv[span[b]]
            kv_t_s[c, b] = kv_t[:, span[b]]
            d_att = d_att_t[:, span[b]].T
            for h in range(heads):
                w_score_s[c, b, own[h], head_lanes[h]] = queries_t[own[h], span[b]]
                w_probs_s[c, b, own[h], head_lanes[h]] = d_att_t[own[h], span[b]]
                here = lane_head == h
                query_s[c, b, h * size : (h + 1) * size, :] = jnp.where(here, queries[span[b]], zero)
                d_att_s[c, b, h * size : (h + 1) * size, :] = jnp.where(here, d_att, zero)
    d_kv_s[...] = jnp.zeros_like(d_kv_s)

    def query_block(b, live, shift):
        chosen = [tables_ref[b, e] for e in range(live)]
        strips = [
            (e, e * size + at, at) for e in range(live) for at in range(0, size, STRIP)
        ]
        rows_of = lambda x: jnp.sum(x.reshape(-1, 8, size), axis=0)
        for c in range(together):
            kv = jnp.concatenate([kv_s[c, k] for k in chosen], axis=0)
            score_s[c, : live * size, :] = dot(kv[:, :proj], w_score_s[c, b])
            d_probs_s[c, : live * size, :] = dot(kv[:, proj:], w_probs_s[c, b])
        for h in range(heads):
            lanes = head_lanes[h]
            stats = []
            for c in range(together):

                def scores(e, row, at):
                    return (
                        score_s[c, row : row + STRIP, lanes] * LOG2E
                        + bias_ref[chosen[e], b, h, at : at + STRIP, :]
                    )

                if shift:
                    peak = jnp.full((8, size), -jnp.inf, F32)
                    for strip in strips:
                        peak = jnp.maximum(
                            peak, jnp.max(scores(*strip).reshape(-1, 8, size), axis=0)
                        )
                    peak = jnp.max(peak, axis=0, keepdims=True)
                total = jnp.zeros((8, size), F32)
                mixed = jnp.zeros((8, size), F32)
                for e, row, at in strips:
                    value = scores(e, row, at)
                    weight = jnp.exp2(value - peak if shift else value)
                    total += rows_of(weight)
                    mixed += rows_of(weight * d_probs_s[c, row : row + STRIP, lanes])
                    score_s[c, row : row + STRIP, lanes] = weight
                norm = 1.0 / jnp.sum(total, axis=0, keepdims=True)
                stats.append((norm, jnp.sum(mixed, axis=0, keepdims=True) * norm))
            for e, row, at in strips:
                part = slice(row, row + STRIP)
                gathered = d_bias_s[b, e, h, at : at + STRIP, :]
                for c, (norm, delta) in enumerate(stats):
                    probs = score_s[c, part, lanes] * norm
                    d_scores = probs * (d_probs_s[c, part, lanes] - delta)
                    probs_s[c, part, lanes] = probs.astype(BF16)
                    ds_s[c, part, lanes] = d_scores.astype(BF16)
                    gathered += d_scores
                d_bias_s[b, e, h, at : at + STRIP, :] = gathered
        for c in range(together):
            kv_t = jnp.concatenate([kv_t_s[c, k] for k in chosen], axis=1)
            for h in range(0, heads, pair):
                lanes = slice(h * size, (h + pair) * size)
                both = slice(h * head_dim, (h + pair) * head_dim)
                low = slice(proj + both.start, proj + both.stop)
                att_t = dot(kv_t[low], probs_s[c, : live * size, lanes])
                d_query_t = dot(kv_t[both], ds_s[c, : live * size, lanes])
                for n in range(pair):
                    att_t_s[c, b, own[h + n], :] = att_t[own[n], head_lanes[n]]
                    d_query_t_s[c, b, own[h + n], :] = d_query_t[own[n], head_lanes[n]]
            d_values = dot(probs_s[c, : live * size, :], d_att_s[c, b])
            d_keys = dot(ds_s[c, : live * size, :], query_s[c, b])
            for e in range(live):
                part = slice(e * size, (e + 1) * size)
                d_kv_s[c, chosen[e], :, :proj] += d_keys[part]
                d_kv_s[c, chosen[e], :, proj:] += d_values[part]

    def all_blocks(shift):
        @pl.loop(0, blocks)
        def _(b):
            for live in range(1, slots + 1):

                @pl.when(lens_ref[b] == live)
                def _():
                    query_block(b, live, shift)

    small = bound <= SAFE_SCORE * SAFE_SCORE

    @pl.when(small)
    def _():
        all_blocks(False)

    @pl.when(jnp.logical_not(small))
    def _():
        all_blocks(True)

    w_qg = jnp.concatenate([w_all_ref[:, :proj], w_all_ref[:, 3 * proj :]], axis=1)
    for c in range(together):
        att_t = jnp.concatenate([att_t_s[c, b] for b in range(blocks)], axis=1)
        d_query_t = jnp.concatenate([d_query_t_s[c, b] for b in range(blocks)], axis=1)
        gate_t = gate_t_s[c]
        gated_t = (gate_t * att_t).astype(BF16)
        d_gpre_t = (d_gated_t_s[c] * att_t * gate_t * (1.0 - gate_t)).astype(BF16)
        d_qg_t = jnp.concatenate([(d_query_t * scale).astype(BF16), d_gpre_t], axis=0)
        d_kv = d_kv_s[c].reshape(tokens, 2 * proj).astype(BF16)
        d_pair = dot(d_kv, w_all_t_ref[proj : 3 * proj, :]) + dot(w_qg, d_qg_t).T
        d_pair_s[c] = d_pair
        for s in range(pieces):
            d_pair_out[s][c] = d_pair_s[c, aligned(owner_of(place_ref[0], s), tile_rows), :].astype(BF16)
        dw_qg_s[...] += dot(d_qg_t, act_s[c])
        dw_kv_s[...] += dot(act_t_s[c], d_kv)
        dwo_s[...] += dot(gated_t, grad_s[c])

    if not last:
        return

    @pl.when(step == pl.num_programs(0) - 1)
    def _():
        weights = [dw_qg_s[:proj, :].T, dw_kv_s[:, :proj], dw_kv_s[:, proj:], dw_qg_s[proj:, :].T]
        weights.append(dwo_s[...])
        far, each = keep_out.shape[0], keep_out.shape[1]
        tile = each // (slots * heads)
        for n, w in enumerate(weights):
            d_w_out[n * chan : (n + 1) * chan, :] = w
            message_out[far * each + n * chan : far * each + (n + 1) * chan, :] = w.astype(BF16)
        for mine in range(inner):

            @pl.when(place_ref[1] == mine)
            def _():
                for b in range(blocks):
                    for e in range(slots):
                        for h in range(heads):
                            turned = d_bias_s[b, e, h].astype(BF16).T
                            at = (e * heads + h) * tile
                            for sub in range(size // tile):
                                col = b * (size // tile) + sub
                                piece = turned[sub * tile : (sub + 1) * tile]
                                if col % inner == mine:
                                    keep_out[col // inner, at : at + tile, :] = piece
                                else:
                                    start = (col // inner) * each + at
                                    message_out[start : start + tile, :] = piece


def attention(
    pieces, bias, weights, tables, lens, place, rows, carried, last, query_tile, inner
):
    count = len(pieces)
    _, columns, tile_rows, chan = pieces[0].shape
    blocks, slots = tables.shape
    heads = bias.shape[2]
    proj = weights.shape[2]
    tokens = tile_rows * count
    size = tokens // blocks
    together = math.gcd(TOGETHER, columns)
    dims = (count, heads, proj // heads, blocks, size, slots, together, inner)
    first = carried is None
    far = tokens // query_tile // inner

    def whole(x):
        return pl.BlockSpec(
            x.shape, lambda j, *_: (0,) * len(x.shape), pipeline_mode=pl.Buffered(1)
        )

    sums = [
        ((blocks, slots, heads, size, size), F32),
        ((2 * proj, chan), F32),
        ((chan, 2 * proj), F32),
        ((proj, chan), F32),
    ]
    if last:
        each = slots * heads * query_tile
        results = [
            ((far, each, size), BF16),
            ((far * each + 5 * chan, size), BF16),
            ((5 * chan, proj), F32),
        ]
    else:
        results = sums
    results = [((columns, tile_rows, chan), BF16)] * count + results
    results = [jax.ShapeDtypeStruct(*x) for x in results]
    scratch = [
        ((chan, 4 * proj), BF16),
        ((4 * proj, chan), BF16),
        ((together, tokens, chan), BF16),
        ((together, tokens, chan), BF16),
        ((together, tokens, chan), F32),
        ((together, chan, tokens), BF16),
        ((together, blocks, size, 2 * proj), BF16),
        ((together, blocks, 2 * proj, size), BF16),
        ((together, blocks, proj, heads * size), BF16),
        ((together, blocks, proj, heads * size), BF16),
        ((together, blocks, heads * size, proj), BF16),
        ((together, blocks, heads * size, proj), BF16),
        ((together, proj, tokens), F32),
        ((together, proj, tokens), F32),
        ((together, slots * size, heads * size), F32),
        ((together, slots * size, heads * size), F32),
        ((together, slots * size, heads * size), BF16),
        ((together, slots * size, heads * size), BF16),
        ((together, blocks, size, 2 * proj), F32),
        ((together, blocks, proj, size), F32),
        ((together, blocks, proj, size), F32),
    ]
    scratch = [pltpu.VMEM(*x) for x in (sums if last else []) + scratch]
    fixed = [bias, weights] + ([] if first else list(carried))
    scalars = [tables, lens, place]
    pairs = tokens * size * slots * heads
    outs = pl.pallas_call(
        functools.partial(attention_kernel, dims, first, last, rows.source_of),
        grid_spec=pltpu.PrefetchScalarGridSpec(
            num_scalar_prefetch=len(scalars),
            grid=(columns // together,),
            in_specs=[
                pl.BlockSpec((2, together, tile_rows, chan), lambda j, *_: (0, j, 0, 0))
            ] * count
            + [whole(x) for x in fixed],
            out_specs=[pl.BlockSpec((together, tile_rows, chan), lambda j, *_: (j, 0, 0))] * count
            + [whole(x) for x in results[count:]],
            scratch_shapes=scratch,
        ),
        out_shape=results,
        compiler_params=pltpu.CompilerParams(vmem_limit_bytes=VMEM_LIMIT),
        cost_estimate=pl.CostEstimate(
            flops=columns * pairs * 7000,
            bytes_accessed=columns * tokens * chan * 6 + 10 * 2**20,
            transcendentals=columns * pairs,
        ),
    )(*scalars, *pieces, *fixed)
    return outs[:count], outs[count:]


def small_call(body, scalars, arrays, results, scratch=()):
    return pl.pallas_call(
        body,
        in_specs=[pl.BlockSpec(memory_space=pltpu.SMEM)] * len(scalars)
        + [pl.BlockSpec(memory_space=pltpu.VMEM)] * len(arrays),
        out_specs=[pl.BlockSpec(memory_space=pltpu.VMEM)] * len(results),
        out_shape=[jax.ShapeDtypeStruct(*x) for x in results],
        scratch_shapes=list(scratch),
        compiler_params=pltpu.CompilerParams(vmem_limit_bytes=SMALL_LIMIT),
    )(*scalars, *arrays)


def aligned(index, count):
    return pl.ds(pl.multiple_of(index * count, count), count)


def split_by_far(place, peers, keep, came, weights):
    far, each, lanes = keep.shape
    share = weights.shape[0] // far

    def body(place_ref, keep_ref, came_ref, weights_ref, own_ref, *message_refs):
        for s in range(far):
            t = peers.step(place_ref[2], s)
            out = message_refs[s - 1] if s else own_ref
            bias = keep_ref[t].astype(F32)
            weight = weights_ref[aligned(t, share), :].astype(BF16).astype(F32)
            if came_ref is not None:
                bias += came_ref[aligned(t, each), :].astype(F32)
                rest = came_ref[far * each :, :].astype(F32)
                half = jnp.zeros_like(weight)
                for u in range(far):
                    half = jnp.where(t == u, rest[u * share : (u + 1) * share], half)
                weight += half
            out[:each, :] = bias.astype(out.dtype)
            out[each:, :] = weight.astype(out.dtype)

    results = [((each + share, lanes), F32 if s == 0 else BF16) for s in range(far)]
    return small_call(body, [place], [keep, came, weights], results)


def split_by_row(place, tables, lens, peers, own, came, dims):
    slots, per_block, each, block_of = dims
    rows = peers.count
    lanes = own.shape[1]
    part = each // slots
    share = own.shape[0] - each

    def body(place_ref, tables_ref, lens_ref, own_ref, *refs):
        block = block_of(place_ref)
        came_refs, outs = refs[: len(came)], refs[len(came) :]
        weight = own_ref[each:, :]
        for ref in came_refs:
            weight += ref[each:, :].astype(F32)
        for s in range(rows):
            outs[s][part:, :] = weight.astype(BF16).astype(outs[s].dtype)
            outs[s][:part, :] = jnp.zeros((part, lanes), outs[s].dtype)
        for e in range(slots):
            at = slice(e * part, (e + 1) * part)
            bias = own_ref[at, :]
            for ref in came_refs:
                bias += ref[at, :].astype(F32)
            for s in range(rows):
                owner = peers.step(place_ref[0], s)
                hit = (tables_ref[block, e] == owner // per_block) & (e < lens_ref[block])

                @pl.when(hit)
                def _():
                    outs[s][:part, :] = bias.astype(outs[s].dtype)

    results = [((part + share, lanes), F32 if s == 0 else BF16) for s in range(rows)]
    return small_call(body, [place, tables, lens], [own, *came], results)


def add_rows(own, came, part):
    share, lanes = own.shape[0] - part, own.shape[1]

    def body(own_ref, *refs):
        came_refs, (bias_ref, weight_ref) = refs[: len(came)], refs[len(came) :]
        terms = [own_ref[...]] + [ref[...].astype(F32) for ref in came_refs]
        while len(terms) > 1:
            terms = [sum(terms[n : n + 2]) for n in range(0, len(terms), 2)]
        total = terms[0]
        bias_ref[...] = total[:part]
        weight_ref[...] = total[part:].astype(BF16)

    results = [((part, lanes), F32), ((share, lanes), BF16)]
    return small_call(body, [], [own, *came], results)


def place_weights(place, peers, parts, count):
    share, lanes = parts[0].shape

    def body(place_ref, *refs):
        part_refs, out_refs, scratch = refs[: len(parts)], refs[len(parts) : -1], refs[-1]
        for s, ref in enumerate(part_refs):
            scratch[aligned(peers.source_of(place_ref[2], s), share), :] = ref[...].astype(F32)
        for n, ref in enumerate(out_refs):
            ref[...] = scratch[n * lanes : (n + 1) * lanes, :]

    rows = share * len(parts)
    results = [((rows // count, lanes), F32)] * count
    return small_call(body, [place], parts, results, [pltpu.VMEM((rows, lanes), F32)])


class Peers:
    def __init__(self, axis, stride, count):
        self.axis, self.count = axis, count
        self.paired = count & (count - 1) == 0
        place = lax.axis_index(axis)
        self.digit = place // stride % count
        everyone = range(lax.axis_size(axis))
        self.routes = []
        for s in range(count):
            route = []
            for p in everyone:
                d = p // stride % count
                route.append((p, p + (self.step(d, s) - d) * stride))
            self.routes.append(route)

    def step(self, digit, s):
        return digit ^ s if self.paired else (digit + s) % self.count

    def target(self, s):
        return self.step(self.digit, s)

    def source_of(self, digit, s):
        return self.step(digit, s) if self.paired else (digit + self.count - s) % self.count

    def came_at(self, digit, source):
        return digit ^ source if self.paired else (digit + self.count - source) % self.count

    def send(self, x, s, home=False):
        route = self.routes[s]
        if home:
            route = [(t, f) for f, t in route]
        return x if s == 0 else lax.ppermute(x, self.axis, route)

    def gather(self, x):
        return jnp.stack([self.send(x, s) for s in range(self.count)])

    def swap(self, messages):
        return [self.send(x, s + 1) for s, x in enumerate(messages)]


def on_device(
    pair_act, out_grad, tri_bias, w_query, w_key, w_value, w_gate, w_out, key_blocks, list_len
):
    row_count = lax.axis_size("row")
    col_count = lax.axis_size("col")
    tile_rows, tile_cols, chan = pair_act.shape
    heads = tri_bias.shape[0]
    query_tile = tri_bias.shape[2]
    proj = w_query.shape[1]
    blocks, slots = key_blocks.shape
    tokens = tile_rows * row_count
    size = tokens // blocks
    col_width = tile_cols // row_count
    chunks = math.gcd(CHUNKS, col_width)
    width = col_width // chunks
    inner = math.gcd(2, col_count)
    rows = Peers("row", 1, row_count)
    near = Peers("col", 1, inner)
    far = Peers("col", inner, col_count // inner)

    gathered = rows.gather(jnp.transpose(tri_bias, (0, 2, 1)))
    both = jnp.stack([pair_act, out_grad]).reshape(2, tile_rows, row_count, chunks, width, chan)
    both = jnp.transpose(both, (2, 3, 0, 4, 1, 5))
    outgoing = [
        [
            lax.dynamic_index_in_dim(both[:, c], rows.target(s), 0, keepdims=False)
            for s in range(row_count)
        ]
        for c in range(chunks)
    ]
    gathered, outgoing[0] = lax.optimization_barrier((gathered, outgoing[0]))
    arrived = [[rows.send(x, s) for s, x in enumerate(outgoing[0])]]
    projections = jnp.stack([w_query, w_key, w_value, w_gate, w_out])
    gathered, arrived[0], outgoing[1:], projections = lax.optimization_barrier(
        (far.gather(gathered), arrived[0], outgoing[1:], projections)
    )
    place = jnp.stack([rows.digit, near.digit, far.digit]).astype(jnp.int32)
    halves = [near.send(gathered, s) for s in range(inner)]
    bias = shifted_bias(halves, key_blocks, list_len, place, rows, far)
    arrived += [[rows.send(x, s) for s, x in enumerate(part)] for part in outgoing[1:]]
    carried = None
    returned = []
    for c in range(chunks):
        d_pieces, carried = attention(
            arrived[c], bias, projections, key_blocks, list_len, place, rows, carried,
            c == chunks - 1, query_tile, inner,
        )
        if c < chunks - 1:
            d_pieces = [rows.send(x, s, home=True) for s, x in enumerate(d_pieces)]
        returned.append(d_pieces)
    keep, message, w_part = carried
    message, returned[:-1] = lax.optimization_barrier((message, returned[:-1]))

    each = keep.shape[1]
    own, *messages = split_by_far(place, far, keep, near.send(message, inner - 1), w_part)
    messages, returned[-1] = lax.optimization_barrier((messages, returned[-1]))
    came = far.swap(messages)
    returned[-1] = [rows.send(x, s, home=True) for s, x in enumerate(returned[-1])]
    per_block = size // tile_rows
    block_of = lambda at: (at[2] * inner + at[1]) * query_tile // size
    own, *messages = split_by_row(
        place, key_blocks, list_len, rows, own, came, (slots, per_block, each, block_of)
    )
    d_bias, w_part = add_rows(own, rows.swap(messages), each // slots)
    weights = place_weights(place, far, [far.send(w_part, s) for s in range(far.count)], 5)
    d_bias = d_bias.reshape(heads, query_tile, per_block, tile_rows)
    d_bias = lax.dynamic_index_in_dim(d_bias, rows.digit % per_block, 2, keepdims=False)


    d_pair = jnp.zeros((tile_rows, tile_cols, chan), BF16)
    for c, part in enumerate(returned):
        for s, x in enumerate(part):
            at = rows.target(s) * col_width + c * width
            d_pair = lax.dynamic_update_slice(d_pair, jnp.transpose(x, (1, 0, 2)), (0, at, 0))
    return (d_pair, jnp.transpose(d_bias, (0, 2, 1)), *weights)


def solution(mesh):
    in_specs = (
        P("row", "col", None),
        P("row", "col", None),
        P(None, "row", "col"),
        P(),
        P(),
        P(),
        P(),
        P(),
        P(),
        P(),
    )
    out_specs = (P("row", "col", None), P(None, "row", "col"), P(), P(), P(), P(), P())
    return jax.shard_map(
        on_device, mesh=mesh, in_specs=in_specs, out_specs=out_specs, check_vma=False
    )
```
